512 devices in a mesh: row: 16 (over z, core), col: 32 (over x, y).
Axes of the slice: x: 4, y: 8, z: 8, core: 2. Of those that a mesh axis runs over, the one named last changes fastest.
Arguments:
- noise: bfloat16 [4096, 8192], P('row', 'col'), as said below
- data: bfloat16 [8192, 8192], P('col'), as said below
Outputs:
- noise_potential: float32 [4096], P('row')
- data_potential: float32 [8192], P('col')
- targets: bfloat16 [4096, 8192], P('row', 'col')
Inputs may be any that keep to these rules, and one draw needn't show every extreme that they name: noise latents, rows of different scales. data latents, rows of different scales.
All inputs are finite; a program needn't handle non-finite values.
Results may differ from the reference program's by a relative error of at most 0.02.
Values may be sent and summed in bfloat16 or wider, within the bound.
No kernel may reach another device: no remote copies, remote signals or barrier semaphores. Data moves between devices by JAX's collectives and lax.ppermute only.
A program may use at most 64 MiB of HBM per device.

```python
import jax
import jax.numpy as jnp
from jax import lax

F = 8192
COLS_DEV = 256
ITERS = 4
N = 4096
M = 8192
N_COL = 32


def data_rows(key, low, high):
    key = jax.random.fold_in(key, 11)
    first, second = jax.random.split(key)
    scales = jnp.exp(jax.random.uniform(first, (M, 1), jnp.float32, jnp.log(low), jnp.log(high)))
    return scales * jax.random.normal(second, (M, F), jnp.float32)


def draw_data(key, part):
    return data_rows(key, 0.5, 2.0).astype(jnp.bfloat16)


def draw_noise(key, part):
    key = jax.random.fold_in(key, 5)
    first, second = jax.random.split(key)
    scales = jnp.exp(jax.random.uniform(first, (N, 1), jnp.float32, jnp.log(0.5), jnp.log(2.0)))
    return (scales * jax.random.normal(second, (N, F), jnp.float32)).astype(jnp.bfloat16)


def setup_inputs(seed: int = 0) -> dict:
    key_of = jax.random.split(jax.random.key(seed), 3)
    noise = draw_noise(jax.random.fold_in(key_of[2], 71), 0)
    data = draw_data(jax.random.fold_in(key_of[2], 71), 0)
    return dict(noise=noise, data=data)


EPSILON = 0.01


def log_totals(scores, axis_dim):
    top = jnp.max(scores, axis=axis_dim)
    total = jnp.sum(jnp.exp(scores - jnp.expand_dims(top, axis_dim)), axis=axis_dim)
    return top, total


def reference(noise, data):
    inner = jnp.dot(noise, data.T, preferred_element_type=jnp.float32)
    noise_sq = jnp.sum(jnp.square(noise.astype(jnp.float32)), axis=1)
    data_sq = jnp.sum(jnp.square(data.astype(jnp.float32)), axis=1)
    cost = (noise_sq[:, None] + data_sq[None, :] - 2.0 * inner) / F
    log_rows = jnp.log(jnp.float32(N))
    log_cols = jnp.log(jnp.float32(M))
    data_potential = jnp.zeros((M,), jnp.float32)
    for step in range(ITERS):
        top, total = log_totals((data_potential[None, :] - cost) / EPSILON, 1)
        noise_potential = -EPSILON * (log_rows + top + jnp.log(total))
        top, total = log_totals((noise_potential[:, None] - cost) / EPSILON, 0)
        data_potential = -EPSILON * (log_cols + top + jnp.log(total))
    scores = (data_potential[None, :] - cost) / EPSILON
    top, total = log_totals(scores, 1)
    noise_potential = -EPSILON * (log_rows + top + jnp.log(total))
    weights = (jnp.exp(scores - top[:, None]) / total[:, None]).astype(jnp.bfloat16)
    weight_blocks = weights.reshape(N, N_COL, COLS_DEV).transpose(1, 0, 2)
    data_blocks = data.reshape(N_COL, COLS_DEV, F)

    def add_block(carry, pair):
        part = jnp.dot(pair[0], pair[1], preferred_element_type=jnp.float32).astype(jnp.bfloat16)
        part = lax.optimization_barrier(part)
        return carry + part.astype(jnp.float32), None

    summed, unused = lax.scan(add_block, jnp.zeros((N, F), jnp.float32), (weight_blocks, data_blocks))
    return noise_potential, data_potential, summed.astype(jnp.bfloat16)
```

```python
import jax
import jax.numpy as jnp
from jax import lax
from jax.sharding import Mesh, PartitionSpec as P

ITERS = 4
EPSILON = 0.01
ROW = ("z", "core")
COL = ("x", "y")


def spread(values, axes):
    members = lax.axis_size(axes)
    sent = jnp.broadcast_to(values.reshape(1, -1, 128), (members, values.size // 128, 128))
    return lax.all_to_all(sent, axes, 0, 0).reshape(members, values.size)


def lse(scores, axis):
    top = jnp.max(scores, axis=axis, keepdims=True)
    total = jnp.sum(jnp.exp(scores - top), axis=axis, keepdims=True)
    return jnp.squeeze(top + jnp.log(total), axis)


def shards(noise, data):
    rows, width = noise.shape
    cols, features = data.shape
    nx, ny = lax.axis_size("x"), lax.axis_size("y")
    log_rows = jnp.log(jnp.float32(rows * lax.axis_size(ROW)))
    log_cols = jnp.log(jnp.float32(cols * lax.axis_size(COL)))

    part = lax.all_gather(noise, "x", axis=1, tiled=True)
    gathered = lax.all_gather(part, "y", axis=1, tiled=True)
    by_y = data.reshape(cols, nx, ny, width).transpose(0, 2, 1, 3).reshape(cols, features)

    noise_sq = jnp.sum(jnp.square(noise.astype(jnp.float32)), axis=1)
    data_sq = jnp.sum(jnp.square(data.astype(jnp.float32)), axis=1)
    noise_sq = jnp.sum(spread(noise_sq, COL), axis=0)

    inner = lax.dot_general(
        gathered, by_y, (((1,), (1,)), ((), ())), preferred_element_type=jnp.float32
    )
    scaled = inner * (2.0 / (features * EPSILON))
    col_pot = data_sq * (-1.0 / (features * EPSILON))
    for step in range(ITERS):
        row_lse = lse(spread(lse(col_pot[None, :] + scaled, 1), COL), 0)
        row_pot = -(log_rows + row_lse)
        col_lse = lse(spread(lse(row_pot[:, None] + scaled, 0), ROW), 0)
        col_pot = -(log_cols + col_lse)
    scores = col_pot[None, :] + scaled
    row_lse = lse(spread(lse(scores, 1), COL), 0)
    noise_potential = noise_sq / features - EPSILON * (log_rows + row_lse)
    data_potential = data_sq / features + EPSILON * col_pot
    weights = jnp.exp(scores - row_lse[:, None]).astype(jnp.bfloat16)
    term = jnp.dot(weights, data, preferred_element_type=jnp.float32).astype(jnp.bfloat16)
    part = lax.psum_scatter(term, "x", scatter_dimension=1, tiled=True)
    targets = lax.psum_scatter(part, "y", scatter_dimension=1, tiled=True)
    return (noise_potential, data_potential, targets)


def solution(mesh):
    devices = mesh.devices.reshape(8, 2, 4, 8)
    return jax.shard_map(
        shards,
        mesh=Mesh(devices, ("z", "core", "x", "y")),
        in_specs=(P(ROW, COL), P(COL, None)),
        out_specs=(P(ROW), P(COL), P(ROW, COL)),
        check_vma=False,
    )
```

```python
import jax
import jax.numpy as jnp
from jax import lax
from jax.sharding import Mesh, PartitionSpec as P

ITERS = 4
EPSILON = 0.01
ROW = ("z", "core")
COL = ("x", "y")


def spread(values, axes):
    members = lax.axis_size(axes)
    sent = jnp.broadcast_to(values.reshape(1, -1, 128), (members, values.size // 128, 128))
    return lax.all_to_all(sent, axes, 0, 0).reshape(members, *values.shape)


def lse(scores, axis):
    top = jnp.max(scores, axis=axis, keepdims=True)
    total = jnp.sum(jnp.exp(scores - top), axis=axis, keepdims=True)
    return jnp.squeeze(top + jnp.log(total), axis)


def parts_of(values):
    first = lax.reduce_precision(values, 8, 7)
    second = lax.reduce_precision(values - first, 8, 7)
    third = values - first - second
    return jnp.stack([first, second, third]).astype(jnp.bfloat16)


def shards(noise, data):
    rows, width = noise.shape
    cols, features = data.shape
    nx, ny, nrow = lax.axis_size("x"), lax.axis_size("y"), lax.axis_size(ROW)
    log_rows = jnp.log(jnp.float32(rows * nrow))
    log_cols = jnp.log(jnp.float32(cols * nx * ny))

    part = lax.all_gather(noise, "x", axis=1, tiled=True)
    gathered = lax.all_gather(part, "y", axis=1, tiled=True)
    by_y = data.reshape(cols, nx, ny, width).transpose(0, 2, 1, 3).reshape(cols, features)

    share = cols // nrow
    piece = lax.dynamic_slice_in_dim(by_y, lax.axis_index(ROW) * share, share, 0)
    piece = piece.reshape(share, ny, nx * width).transpose(1, 0, 2)
    piece = lax.all_to_all(piece, "y", 0, 0)
    mine = lax.all_gather(piece, ROW, axis=1, tiled=True).reshape(ny * cols, nx * width)

    noise_sq = jnp.sum(jnp.square(noise.astype(jnp.float32)), axis=1)
    data_sq = jnp.sum(jnp.square(data.astype(jnp.float32)), axis=1)

    inner = lax.dot_general(
        gathered, by_y, (((1,), (1,)), ((), ())), preferred_element_type=jnp.float32
    )
    scaled = inner * (2.0 / (features * EPSILON))
    wide = lax.all_gather(scaled, "y", axis=1, tiled=True)

    col_pot = data_sq * (-1.0 / (features * EPSILON))
    for step in range(ITERS):
        local = lse(col_pot[None, :] + scaled, 1)
        if step == 0:
            got = spread(jnp.stack([local, noise_sq]), COL)
            noise_sq = jnp.sum(got[:, 1], axis=0)
            row_lse = lse(got[:, 0], 0)
        else:
            row_lse = lse(spread(local, COL), 0)
        row_pot = -(log_rows + row_lse)
        block = wide if step == ITERS - 1 else scaled
        col_pot = -(log_cols + lse(spread(lse(row_pot[:, None] + block, 0), ROW), 0))
    own = lax.dynamic_slice_in_dim(col_pot, lax.axis_index("y") * cols, cols, 0)
    data_potential = data_sq / features + EPSILON * own

    scores = col_pot[None, :] + wide
    top = jnp.max(scores, axis=1, keepdims=True)
    weights = jnp.exp(scores - top)
    total = jnp.sum(weights, axis=1, keepdims=True)
    term = jnp.dot(weights.astype(jnp.bfloat16), mine, preferred_element_type=jnp.float32)
    term = (term / total).astype(jnp.bfloat16).reshape(rows, nx, width).transpose(1, 0, 2)
    local = (top + jnp.log(total))[:, 0]
    extra = jnp.pad(parts_of(local), ((0, 13), (0, 0)))
    extra = jnp.broadcast_to(extra[None], (nx, 16, rows))
    got = lax.all_to_all(jnp.concatenate([term, extra], axis=1), "x", 0, 0)
    locals_ = jnp.sum(got[:, rows : rows + 3].astype(jnp.float32), axis=1)
    row_lse = lse(locals_, 0)
    scale = jnp.exp(locals_ - row_lse[None])
    targets = jnp.sum(scale[:, :, None] * got[:, :rows].astype(jnp.float32), axis=0)
    noise_potential = noise_sq / features - EPSILON * (log_rows + row_lse)
    return (noise_potential, data_potential, targets.astype(jnp.bfloat16))


def solution(mesh):
    devices = mesh.devices.reshape(8, 2, 4, 8)
    return jax.shard_map(
        shards,
        mesh=Mesh(devices, ("z", "core", "x", "y")),
        in_specs=(P(ROW, COL), P(COL, None)),
        out_specs=(P(ROW), P(COL), P(ROW, COL)),
        check_vma=False,
    )
```

```python
import functools

import jax
import jax.numpy as jnp
import numpy as np
from jax import lax
from jax.experimental import pallas as pl
from jax.experimental.pallas import tpu as pltpu
from jax.sharding import Mesh, PartitionSpec as P

ITERS = 4
EPSILON = 0.01
ROW = ("z", "core")
COL = ("x", "y")
LANES = 128
FIRST_ROWS = 160
VMEM = pl.BlockSpec(memory_space=pltpu.VMEM)
ANY = pl.BlockSpec(memory_space=pl.ANY)
PARAMS = pltpu.CompilerParams(vmem_limit_bytes=40 * 2**20)


def spread(values, axes):
    members = lax.axis_size(axes)
    sent = jnp.broadcast_to(values.reshape(1, -1, LANES), (members, values.size // LANES, LANES))
    return lax.all_to_all(sent, axes, 0, 0).reshape(members, *values.shape)


def lse(scores, axis):
    top = jnp.max(scores, axis=axis, keepdims=True)
    total = jnp.sum(jnp.exp(scores - top), axis=axis, keepdims=True)
    return jnp.squeeze(top + jnp.log(total), axis)


def as_column(values):
    return jnp.broadcast_to(values, (LANES, values.shape[1])).T


def as_rows(column):
    return jnp.broadcast_to(column, (column.shape[0], LANES)).T


def joined(got_ref):
    got = got_ref[...]
    top = jnp.max(got, axis=0)
    return top + jnp.log(jnp.sum(jnp.exp(got - top[None]), axis=0))


def inner_kernel(scale, nx, steps, first_ref, second_ref, *rest):
    data_refs, (out_ref, total) = rest[:nx], rest[nx:]
    step = pl.program_id(0)
    width = data_refs[0].shape[1]
    split = first_ref.shape[0]
    dims = (((1,), (1,)), ((), ()))
    upper, lower = None, None
    for x in range(nx):
        block = data_refs[x][...]
        one = lax.dot_general(
            first_ref[:, x * width : (x + 1) * width], block, dims, preferred_element_type=jnp.float32
        )
        two = lax.dot_general(second_ref[x, 0], block, dims, preferred_element_type=jnp.float32)
        upper = one if upper is None else upper + one
        lower = two if lower is None else lower + two

    @pl.when(step == 0)
    def _():
        total[:split] = upper
        total[split:] = lower

    @pl.when(step > 0)
    def _():
        total[:split] += upper
        total[split:] += lower

    @pl.when(step == steps - 1)
    def _():
        out_ref[...] = total[...] * scale


def inner_product(first, second, data, scale):
    nx, ny, low, width = second.shape
    high, cols = first.shape[0], data.shape[0]
    at = lambda x: pl.BlockSpec((cols, width), lambda y: (0, x * ny + y))
    return pl.pallas_call(
        functools.partial(inner_kernel, scale, nx, ny),
        grid=(ny,),
        out_shape=jax.ShapeDtypeStruct((high + low, cols), jnp.float32),
        in_specs=[
            pl.BlockSpec((high, nx * width), lambda y: (0, y)),
            pl.BlockSpec((nx, 1, low, width), lambda y: (0, y, 0, 0)),
        ]
        + [at(x) for x in range(nx)],
        out_specs=pl.BlockSpec((high + low, cols), lambda y: (0, 0)),
        scratch_shapes=[pltpu.VMEM((high + low, cols), jnp.float32)],
        compiler_params=PARAMS,
        name="inner_product",
    )(first, second, *([data] * nx))


def wide_cols_kernel(pot_ref, wide_ref, out_ref):
    pot = as_column(pot_ref[...])
    members = out_ref.shape[0]
    for k in range(wide_ref.shape[1] // LANES):
        scores = wide_ref[:, k * LANES : (k + 1) * LANES] + pot
        top = jnp.max(scores, axis=0, keepdims=True)
        local = top + jnp.log(jnp.sum(jnp.exp(scores - top), axis=0, keepdims=True))
        out_ref[:, k, :] = jnp.broadcast_to(local, (members, LANES))


def wide_cols(pot, wide, members):
    return pl.pallas_call(
        wide_cols_kernel,
        out_shape=jax.ShapeDtypeStruct((members, wide.shape[1] // LANES, LANES), jnp.float32),
        in_specs=[VMEM, VMEM],
        out_specs=VMEM,
        compiler_params=PARAMS,
        name="wide_cols",
    )(pot.reshape(1, -1), wide)


def row_top(wide_ref, pot):
    top = None
    for k in range(pot.shape[0]):
        scores = wide_ref[:, k * LANES : (k + 1) * LANES] + pot[k : k + 1]
        top = scores if top is None else jnp.maximum(top, scores)
    return jnp.max(top, axis=1, keepdims=True)


def wide_rows_kernel(log_cols, got_ref, wide_ref, out_ref):
    pot = -(log_cols + joined(got_ref))
    top = row_top(wide_ref, pot)
    total = None
    for k in range(pot.shape[0]):
        part = jnp.exp(wide_ref[:, k * LANES : (k + 1) * LANES] + pot[k : k + 1] - top)
        total = part if total is None else total + part
    local = as_rows(top + jnp.log(jnp.sum(total, axis=1, keepdims=True)))[:1]
    for k in range(out_ref.shape[1]):
        out_ref[:, k, :] = jnp.broadcast_to(local[:, k * LANES : (k + 1) * LANES], (out_ref.shape[0], LANES))


def wide_rows(got, wide, members, log_cols):
    return pl.pallas_call(
        functools.partial(wide_rows_kernel, log_cols),
        out_shape=jax.ShapeDtypeStruct((members, wide.shape[0] // LANES, LANES), jnp.float32),
        in_specs=[VMEM, VMEM],
        out_specs=VMEM,
        compiler_params=PARAMS,
        name="wide_rows",
    )(got, wide)


def rounded(values):
    return values.astype(jnp.bfloat16).astype(jnp.float32)


def final_kernel(log_cols, got_ref, wide_ref, data_ref, out_ref, pot_ref, weights):
    pot = -(log_cols + joined(got_ref))
    pot_ref[...] = pot
    ny, nx, cols, width = data_ref.shape
    rows = wide_ref.shape[0]
    top = row_top(wide_ref, pot)
    total = None
    for k in range(pot.shape[0]):
        lanes = slice(k * LANES, (k + 1) * LANES)
        part = jnp.exp(wide_ref[:, lanes] + pot[k : k + 1] - top)
        weights[:, lanes] = part.astype(jnp.bfloat16)
        total = part if total is None else total + part
    total = jnp.sum(total, axis=1, keepdims=True)
    inverse = 1.0 / total
    for x in range(nx):
        term = None
        for y in range(ny):
            one = jnp.dot(
                weights[:, y * cols : (y + 1) * cols], data_ref[y, x], preferred_element_type=jnp.float32
            )
            term = one if term is None else term + one
        out_ref[x, :rows, :] = (term * inverse).astype(jnp.bfloat16)
    local = as_rows(top + jnp.log(total))[:16]
    first = rounded(local)
    second = rounded(local - first)
    third = local - first - second
    place = lax.broadcasted_iota(jnp.int32, local.shape, 0)
    extra = jnp.where(place == 0, first, jnp.where(place == 1, second, third))
    extra = jnp.where(place < 3, extra, 0.0).astype(jnp.bfloat16)
    for x in range(nx):
        out_ref[x, rows:, :] = extra


def final_terms(got, wide, data, log_cols):
    ny, nx, cols, width = data.shape
    rows = wide.shape[0]
    return pl.pallas_call(
        functools.partial(final_kernel, log_cols),
        out_shape=(
            jax.ShapeDtypeStruct((nx, rows + 16, width), jnp.bfloat16),
            jax.ShapeDtypeStruct(got.shape[1:], jnp.float32),
        ),
        in_specs=[VMEM] * 3,
        out_specs=(VMEM, VMEM),
        scratch_shapes=[pltpu.VMEM(wide.shape, jnp.bfloat16)],
        compiler_params=PARAMS,
        name="final_terms",
    )(got, wide, data)


def combine_kernel(log_rows, features, got_ref, sq_ref, out_ref, pot_ref):
    nx, rows = got_ref.shape[0], out_ref.shape[0]
    locals_ = [
        jnp.sum(got_ref[x, rows:, :].astype(jnp.float32), axis=0, keepdims=True) for x in range(nx)
    ]
    top = functools.reduce(jnp.maximum, locals_)
    whole = top + jnp.log(functools.reduce(jnp.add, [jnp.exp(v - top) for v in locals_]))
    pot_ref[...] = sq_ref[...] * (1.0 / features) - EPSILON * (log_rows + whole)
    scales = [as_column(jnp.exp(v - whole)) for v in locals_]
    for k in range(out_ref.shape[1] // LANES):
        lanes = slice(k * LANES, (k + 1) * LANES)
        parts = [scales[x] * got_ref[x, :rows, lanes].astype(jnp.float32) for x in range(nx)]
        out_ref[:, lanes] = functools.reduce(jnp.add, parts).astype(jnp.bfloat16)


def combine(got, noise_sq, features, log_rows):
    nx, held, width = got.shape
    rows = held - 16
    return pl.pallas_call(
        functools.partial(combine_kernel, log_rows, features),
        out_shape=(
            jax.ShapeDtypeStruct((rows, width), jnp.bfloat16),
            jax.ShapeDtypeStruct((1, rows), jnp.float32),
        ),
        in_specs=[VMEM, VMEM],
        out_specs=(VMEM, VMEM),
        compiler_params=PARAMS,
        name="combine",
    )(got, noise_sq.reshape(1, -1))


def shards(noise, data):
    rows, width = noise.shape
    cols, features = data.shape
    nx, ny, nrow = lax.axis_size("x"), lax.axis_size("y"), lax.axis_size(ROW)
    log_rows = _log(rows * nrow)
    log_cols = _log(cols * nx * ny)

    part = lax.all_gather(noise[:FIRST_ROWS], "x", axis=1, tiled=True)
    first = lax.all_gather(part, "y", axis=1, tiled=True)
    low = rows - FIRST_ROWS
    share = cols // nrow
    piece = lax.dynamic_slice_in_dim(data, lax.axis_index(ROW) * share, share, 0)
    piece = piece.reshape(share, nx, ny, width).transpose(2, 1, 0, 3).reshape(ny, nx * share, width)
    sent = jnp.broadcast_to(noise[None, FIRST_ROWS:], (ny, low, width))
    sent = jnp.concatenate([sent, piece], axis=1)
    part, sent = lax.optimization_barrier((part, sent))
    got = lax.all_to_all(sent, "y", 0, 0)
    second = jnp.broadcast_to(got[None, :, :low], (nx, ny, low, width))
    second = lax.all_to_all(second, "x", 0, 0)
    piece = got[:, low:].reshape(ny, nx, share, width)

    noise_sq = jnp.sum(jnp.square(noise.astype(jnp.float32)), axis=1)
    data_sq = jnp.sum(jnp.square(data.astype(jnp.float32)), axis=1)

    scaled = inner_product(first, second, data, 2.0 / (features * EPSILON))
    wide = lax.all_gather(scaled, "y", axis=1, tiled=True)

    col_pot = data_sq * (-1.0 / (features * EPSILON))
    for step in range(ITERS - 1):
        local = lse(col_pot[None, :] + scaled, 1)
        if step == 0:
            got = spread(jnp.stack([local, noise_sq]), COL)
            noise_sq = jnp.sum(got[:, 1], axis=0)
            row_lse = lse(got[:, 0], 0)
            row_lse, piece = lax.optimization_barrier((row_lse, piece))
            mine = lax.all_gather(piece, ROW, axis=2, tiled=True)
        else:
            row_lse = lse(spread(local, COL), 0)
        row_pot = -(log_rows + row_lse)
        if step < ITERS - 2:
            local = lse(row_pot[:, None] + scaled, 0)
            col_pot = -(log_cols + lse(spread(local, ROW), 0))
    got = lax.all_to_all(wide_cols(row_pot, wide, nrow), ROW, 0, 0)
    got = lax.all_to_all(wide_rows(got, wide, nx, log_cols), "x", 0, 0)
    row_pot = -(log_rows + lse(got.reshape(nx, rows), 0))
    got = lax.all_to_all(wide_cols(row_pot, wide, nrow), ROW, 0, 0)
    terms, col_pot = final_terms(got, wide, mine, log_cols)
    own = lax.dynamic_slice_in_dim(col_pot, lax.axis_index("y") * (cols // LANES), cols // LANES, 0)
    data_potential = data_sq / features + EPSILON * own.reshape(cols)
    got = lax.all_to_all(terms, "x", 0, 0)
    targets, noise_potential = combine(got, noise_sq, features, log_rows)
    return (noise_potential.reshape(rows), data_potential, targets)


def _log(count):
    return float(np.log(np.float32(count)))


def solution(mesh):
    devices = mesh.devices.reshape(8, 2, 4, 8)
    return jax.shard_map(
        shards,
        mesh=Mesh(devices, ("z", "core", "x", "y")),
        in_specs=(P(ROW, COL), P(COL, None)),
        out_specs=(P(ROW), P(COL), P(ROW, COL)),
        check_vma=False,
    )
```

```python
import functools

import jax
import jax.numpy as jnp
import numpy as np
from jax import lax
from jax.experimental import pallas as pl
from jax.experimental.pallas import tpu as pltpu
from jax.sharding import Mesh, PartitionSpec as P

ITERS = 4
EPSILON = 0.01
ROW = ("z", "core")
COL = ("x", "y")
LANES = 128
FIRST_ROWS = 160
WIDE_FROM = 1
VMEM = pl.BlockSpec(memory_space=pltpu.VMEM)
HBM = pl.BlockSpec(memory_space=pltpu.HBM)
MIB = 2**20
F32, BF16 = jnp.float32, jnp.bfloat16


def call(kernel, name, out_shape, in_specs, out_specs, *args, scratch_shapes=(), vmem=40):
    return pl.pallas_call(
        kernel,
        out_shape=out_shape,
        in_specs=in_specs,
        out_specs=out_specs,
        scratch_shapes=scratch_shapes,
        compiler_params=pltpu.CompilerParams(vmem_limit_bytes=vmem * MIB),
        name=name,
    )(*args)


def shape(dims, dtype=F32):
    return jax.ShapeDtypeStruct(dims, dtype)


def lanes(k):
    return slice(k * LANES, (k + 1) * LANES)


def as_column(values):
    return jnp.broadcast_to(values, (LANES, values.shape[1])).T


def as_rows(column):
    return jnp.broadcast_to(column, (column.shape[0], LANES)).T


def joined(got):
    top = jnp.max(got, axis=0)
    return top + jnp.log(jnp.sum(jnp.exp(got - top[None]), axis=0))


def products(read, data_ref, nx, ny, width):
    total = None
    for y in range(ny):
        left = jnp.concatenate([read(y, x) for x in range(nx)], axis=1)
        right = jnp.concatenate(
            [data_ref[:, (x * ny + y) * width : (x * ny + y + 1) * width] for x in range(nx)], axis=1
        )
        one = lax.dot_general(left, right, (((1,), (1,)), ((), ())), preferred_element_type=F32)
        total = one if total is None else total + one
    return total


def second_kernel(scale, second_ref, data_ref, out_ref):
    nx, ny, _, width = second_ref.shape
    out_ref[...] = products(lambda y, x: second_ref[x, y], data_ref, nx, ny, width) * scale


def first_kernel(scale, first_ref, data_ref, low_ref, pot_ref, sq_ref, out_ref, copy_ref, send_ref, held, sems):
    ny, nx, high, width = first_ref.shape
    copies = [pltpu.make_async_copy(first_ref.at[y], held.at[y], sems.at[y]) for y in range(ny)]
    for copy in copies:
        copy.start()

    def read(y, x):
        if x == 0:
            copies[y].wait()
        return held[y, x]

    out_ref[:high] = products(read, data_ref, nx, ny, width) * scale
    out_ref[high:] = low_ref[...]
    out = pltpu.make_async_copy(out_ref, copy_ref, sems.at[ny])
    out.start()
    local = local_rows(out_ref, pot_ref[...])
    chunks = local.shape[1] // LANES
    members = send_ref.shape[0]
    for k in range(chunks):
        send_ref[:, k, :] = jnp.broadcast_to(local[:, lanes(k)], (members, LANES))
        send_ref[:, chunks + k, :] = jnp.broadcast_to(sq_ref[k : k + 1], (members, LANES))
    out.wait()


def row_top(block_ref, pot):
    top = None
    for k in range(pot.shape[0]):
        scores = block_ref[:, lanes(k)] + pot[k : k + 1]
        top = scores if top is None else jnp.maximum(top, scores)
    return jnp.max(top, axis=1, keepdims=True)


def local_rows(block_ref, pot):
    top = row_top(block_ref, pot)
    total = None
    for k in range(pot.shape[0]):
        part = jnp.exp(block_ref[:, lanes(k)] + pot[k : k + 1] - top)
        total = part if total is None else total + part
    return as_rows(top + jnp.log(jnp.sum(total, axis=1, keepdims=True)))[:1]


def rows_kernel(log_cols, got_ref, block_ref, out_ref):
    local = local_rows(block_ref, -(log_cols + joined(got_ref[...])))
    for k in range(out_ref.shape[1]):
        out_ref[:, k, :] = jnp.broadcast_to(local[:, lanes(k)], (out_ref.shape[0], LANES))


def half_rows(got, block, members, log_cols):
    out = shape((members, block.shape[0] // LANES, LANES))
    return call(functools.partial(rows_kernel, log_cols), "half_rows", out, [VMEM, VMEM], VMEM, got, block)


def cols_kernel(log_rows, got_ref, block_ref, out_ref):
    chunks = block_ref.shape[0] // LANES
    pot = -(log_rows + joined(got_ref[:, :chunks, :]))
    pot = jnp.concatenate([as_column(pot[k : k + 1]) for k in range(chunks)], axis=0)
    members = out_ref.shape[0]
    for k in range(out_ref.shape[1]):
        scores = block_ref[:, lanes(k)] + pot
        top = jnp.max(scores, axis=0, keepdims=True)
        local = top + jnp.log(jnp.sum(jnp.exp(scores - top), axis=0, keepdims=True))
        out_ref[:, k, :] = jnp.broadcast_to(local, (members, LANES))


def half_cols(got, block, members, log_rows):
    out = shape((members, block.shape[1] // LANES, LANES))
    return call(functools.partial(cols_kernel, log_rows), "half_cols", out, [VMEM, VMEM], VMEM, got, block)


def rounded(values):
    return values.astype(BF16).astype(F32)


def final_kernel(log_cols, got_ref, wide_ref, data_ref, out_ref, pot_ref, weights, held, sems):
    ny, nx, cols, width = data_ref.shape
    rows = wide_ref.shape[0]
    copies = [pltpu.make_async_copy(data_ref.at[y], held.at[y], sems.at[y]) for y in range(ny)]
    for copy in copies:
        copy.start()
    pot = -(log_cols + joined(got_ref[...]))
    pot_ref[...] = pot
    top = row_top(wide_ref, pot)
    total = None
    for k in range(pot.shape[0]):
        part = jnp.exp(wide_ref[:, lanes(k)] + pot[k : k + 1] - top)
        weights[:, lanes(k)] = part.astype(BF16)
        total = part if total is None else total + part
    total = jnp.sum(total, axis=1, keepdims=True)
    inverse = 1.0 / total
    local = as_rows(top + jnp.log(total))[:16]
    first = rounded(local)
    second = rounded(local - first)
    third = local - first - second
    place = lax.broadcasted_iota(jnp.int32, local.shape, 0)
    extra = jnp.where(place == 0, first, jnp.where(place == 1, second, third))
    extra = jnp.where(place < 3, extra, 0.0).astype(BF16)
    for copy in copies:
        copy.wait()
    for x in range(nx):
        right = jnp.concatenate([held[y, x] for y in range(ny)], axis=0)
        term = jnp.dot(weights[...], right, preferred_element_type=F32)
        out_ref[x, :rows, :] = (term * inverse).astype(BF16)
        out_ref[x, rows:, :] = extra


def final_terms(got, wide, data, log_cols):
    ny, nx, cols, width = data.shape
    rows = wide.shape[0]
    return call(
        functools.partial(final_kernel, log_cols),
        "final_terms",
        (shape((nx, rows + 16, width), BF16), shape(got.shape[1:])),
        [VMEM, VMEM, HBM],
        (VMEM, VMEM),
        got,
        wide,
        data,
        scratch_shapes=[
            pltpu.VMEM(wide.shape, BF16),
            pltpu.VMEM(data.shape, BF16),
            pltpu.SemaphoreType.DMA((ny,)),
        ],
        vmem=52,
    )


def combine_kernel(log_rows, features, got_ref, began_ref, out_ref, pot_ref):
    nx, rows = got_ref.shape[0], out_ref.shape[0]
    chunks = rows // LANES
    locals_ = [jnp.sum(got_ref[x, rows:, :].astype(F32), axis=0, keepdims=True) for x in range(nx)]
    top = functools.reduce(jnp.maximum, locals_)
    whole = top + jnp.log(functools.reduce(jnp.add, [jnp.exp(v - top) for v in locals_]))
    noise_sq = jnp.sum(began_ref[:, chunks:, :], axis=0)
    for k in range(chunks):
        pot_ref[k : k + 1, :] = noise_sq[k : k + 1] * (1.0 / features) - EPSILON * (log_rows + whole[:, lanes(k)])
    scales = [as_column(jnp.exp(v - whole)) for v in locals_]
    for k in range(out_ref.shape[1] // LANES):
        parts = [scales[x] * got_ref[x, :rows, lanes(k)].astype(F32) for x in range(nx)]
        out_ref[:, lanes(k)] = functools.reduce(jnp.add, parts).astype(BF16)


def shards(noise, data):
    rows, width = noise.shape
    cols, features = data.shape
    nx, ny, nrow, ncol = (lax.axis_size(axes) for axes in ("x", "y", ROW, COL))
    log_rows, log_cols = _log(rows * nrow), _log(cols * ncol)
    chunks = rows // LANES

    sent = jnp.broadcast_to(noise[None, :FIRST_ROWS], (nx, FIRST_ROWS, width))
    part = lax.all_to_all(sent, "x", 0, 0)
    first = lax.all_gather(part, "y")
    low = rows - FIRST_ROWS
    share = cols // nrow
    piece = lax.dynamic_slice_in_dim(data, lax.axis_index(ROW) * share, share, 0)
    piece = piece.reshape(share, nx, ny, width).transpose(2, 1, 0, 3).reshape(ny, nx * share, width)
    sent = jnp.broadcast_to(noise[None, FIRST_ROWS:], (ny, low, width))
    sent = jnp.concatenate([sent, piece], axis=1)
    part, sent = lax.optimization_barrier((part, sent))
    got = lax.all_to_all(sent, "y", 0, 0)
    second = jnp.broadcast_to(got[None, :, :low], (nx, ny, low, width))
    second = lax.all_to_all(second, "x", 0, 0)
    piece = got[:, low:].reshape(ny, nx, share, width)

    noise_sq = jnp.sum(jnp.square(noise.astype(F32)), axis=1)
    data_sq = jnp.sum(jnp.square(data.astype(F32)), axis=1)
    col_pot = (data_sq * (-1.0 / (features * EPSILON))).reshape(-1, LANES)
    scale = 2.0 / (features * EPSILON)
    lower = call(
        functools.partial(second_kernel, scale), "second_rows", shape((low, cols)), [VMEM, VMEM], VMEM, second, data
    )
    scaled, copied, sent = call(
        functools.partial(first_kernel, scale),
        "first_rows",
        (shape((rows, cols)), shape((rows, cols)), shape((ncol, 2 * chunks, LANES))),
        [HBM, VMEM, VMEM, VMEM, VMEM],
        (VMEM, HBM, VMEM),
        first,
        data,
        lower,
        col_pot,
        noise_sq.reshape(-1, LANES),
        scratch_shapes=[
            pltpu.VMEM((ny, nx, FIRST_ROWS, width), BF16),
            pltpu.SemaphoreType.DMA((ny + 1,)),
        ],
        vmem=52,
    )
    wide = lax.all_gather(copied, "y", axis=1, tiled=True)

    began = None
    for step in range(ITERS):
        got = lax.all_to_all(sent, "x" if step > WIDE_FROM else COL, 0, 0)
        if step == 0:
            began, piece = lax.optimization_barrier((got, piece))
            mine = lax.all_gather(piece, ROW, axis=2, tiled=True)
        sent = half_cols(got, wide if step >= WIDE_FROM else scaled, nrow, log_rows)
        got = lax.all_to_all(sent, ROW, 0, 0)
        if step < WIDE_FROM:
            sent = half_rows(got, scaled, ncol, log_cols)
        elif step < ITERS - 1:
            sent = half_rows(got, wide, nx, log_cols)
    terms, col_pot = final_terms(got, wide, mine, log_cols)
    own = lax.dynamic_slice_in_dim(col_pot, lax.axis_index("y") * (cols // LANES), cols // LANES, 0)
    data_potential = data_sq / features + EPSILON * own.reshape(cols)
    got = lax.all_to_all(terms, "x", 0, 0)
    targets, noise_potential = call(
        functools.partial(combine_kernel, log_rows, features),
        "combine",
        (shape((rows, width), BF16), shape((chunks, LANES))),
        [VMEM, VMEM],
        (VMEM, VMEM),
        got,
        began,
    )
    return (noise_potential.reshape(rows), data_potential, targets)


def _log(count):
    return float(np.log(np.float32(count)))


def solution(mesh):
    devices = mesh.devices.reshape(8, 2, 4, 8)
    return jax.shard_map(
        shards,
        mesh=Mesh(devices, ("z", "core", "x", "y")),
        in_specs=(P(ROW, COL), P(COL, None)),
        out_specs=(P(ROW), P(COL), P(ROW, COL)),
        check_vma=False,
    )
```

```python
import functools

import jax
import jax.numpy as jnp
import numpy as np
from jax import lax
from jax.experimental import pallas as pl
from jax.experimental.pallas import tpu as pltpu
from jax.sharding import Mesh, PartitionSpec as P

ITERS = 4
EPSILON = 0.01
ROW = ("z", "core")
COL = ("x", "y")
LANES = 128
FIRST_ROWS = 160
WIDE_FROM = 1
VMEM = pl.BlockSpec(memory_space=pltpu.VMEM)
HBM = pl.BlockSpec(memory_space=pltpu.HBM)
MIB = 2**20
F32, BF16 = jnp.float32, jnp.bfloat16


def call(kernel, name, out_shape, in_specs, out_specs, *args, scratch_shapes=(), vmem=40):
    return pl.pallas_call(
        kernel,
        out_shape=out_shape,
        in_specs=in_specs,
        out_specs=out_specs,
        scratch_shapes=scratch_shapes,
        compiler_params=pltpu.CompilerParams(vmem_limit_bytes=vmem * MIB),
        name=name,
    )(*args)


def shape(dims, dtype=F32):
    return jax.ShapeDtypeStruct(dims, dtype)


def lanes(k):
    return slice(k * LANES, (k + 1) * LANES)


def as_column(values):
    return jnp.broadcast_to(values, (LANES, values.shape[1])).T


def as_rows(column):
    return jnp.broadcast_to(column, (column.shape[0], LANES)).T


def joined(got):
    top = jnp.max(got, axis=0)
    return top + jnp.log(jnp.sum(jnp.exp(got - top[None]), axis=0))


def prepare_kernel(high, noise_ref, data_ref, by_x_ref, by_y_ref, sq_ref, held, sem):
    nx = by_x_ref.shape[0]
    ny, sent, width = by_y_ref.shape
    rows = noise_ref.shape[0]
    low = rows - high
    share = (sent - low) // nx
    at = (lax.axis_index(ROW[0]) * lax.axis_size(ROW[1]) + lax.axis_index(ROW[1])) * share
    copy = pltpu.make_async_copy(data_ref.at[pl.ds(pl.multiple_of(at, share), share), :], held, sem)
    copy.start()
    for x in range(nx):
        by_x_ref[x] = noise_ref[:high]
    for y in range(ny):
        by_y_ref[y, :low] = noise_ref[high:]
    squares = jnp.square(noise_ref[...].astype(F32))
    squares = as_rows(jnp.sum(squares, axis=1, keepdims=True))[:1]
    for k in range(rows // LANES):
        sq_ref[k : k + 1, :] = squares[:, lanes(k)]
    copy.wait()
    for y in range(ny):
        for x in range(nx):
            block = held[:, (x * ny + y) * width : (x * ny + y + 1) * width]
            by_y_ref[y, low + x * share : low + (x + 1) * share] = block


def data_copies(data_ref, held, sems):
    ny, nx, _, width = held.shape
    return [
        [
            pltpu.make_async_copy(
                data_ref.at[:, (x * ny + y) * width : (x * ny + y + 1) * width], held.at[y, x], sems.at[y, x]
            )
            for x in range(nx)
        ]
        for y in range(ny)
    ]


def products(read, held):
    ny, nx, _, _ = held.shape
    total = None
    for y in range(ny):
        left = [read(y, x) for x in range(nx)]
        left = jnp.concatenate(left, axis=1)
        right = jnp.concatenate([held[y, x] for x in range(nx)], axis=1)
        one = lax.dot_general(left, right, (((1,), (1,)), ((), ())), preferred_element_type=F32)
        total = one if total is None else total + one
    return total


def second_kernel(scale, second_ref, data_ref, out_ref, held, sems):
    copies = data_copies(data_ref, held, sems)
    for group in copies:
        for copy in group:
            copy.start()

    def read(y, x):
        copies[y][x].wait()
        return second_ref[x, y]

    out_ref[...] = products(read, held) * scale


def first_kernel(
    scale, first_ref, data_ref, low_ref, pot_ref, sq_ref, out_ref, copy_ref, send_ref, rows_held, held, sems, row_sems
):
    ny, _, high, _ = first_ref.shape
    copies = data_copies(data_ref, held, sems)
    row_copies = [pltpu.make_async_copy(first_ref.at[y], rows_held.at[y], row_sems.at[y]) for y in range(ny)]
    for y in range(ny):
        row_copies[y].start()
        for copy in copies[y]:
            copy.start()

    def read(y, x):
        if x == 0:
            row_copies[y].wait()
        copies[y][x].wait()
        return rows_held[y, x]

    out_ref[:high] = products(read, held) * scale
    out_ref[high:] = low_ref[...]
    out = pltpu.make_async_copy(out_ref, copy_ref, row_sems.at[ny])
    out.start()
    local = local_rows(out_ref, pot_ref[...])
    chunks = local.shape[1] // LANES
    members = send_ref.shape[0]
    for k in range(chunks):
        send_ref[:, k, :] = jnp.broadcast_to(local[:, lanes(k)], (members, LANES))
        send_ref[:, chunks + k, :] = jnp.broadcast_to(sq_ref[k : k + 1], (members, LANES))
    out.wait()


def row_top(block_ref, pot):
    top = None
    for k in range(pot.shape[0]):
        scores = block_ref[:, lanes(k)] + pot[k : k + 1]
        top = scores if top is None else jnp.maximum(top, scores)
    return jnp.max(top, axis=1, keepdims=True)


def local_rows(block_ref, pot):
    top = row_top(block_ref, pot)
    total = None
    for k in range(pot.shape[0]):
        part = jnp.exp(block_ref[:, lanes(k)] + pot[k : k + 1] - top)
        total = part if total is None else total + part
    return as_rows(top + jnp.log(jnp.sum(total, axis=1, keepdims=True)))[:1]


def rows_kernel(log_cols, got_ref, block_ref, out_ref):
    local = local_rows(block_ref, -(log_cols + joined(got_ref[...])))
    for k in range(out_ref.shape[1]):
        out_ref[:, k, :] = jnp.broadcast_to(local[:, lanes(k)], (out_ref.shape[0], LANES))


def half_rows(got, block, members, log_cols):
    out = shape((members, block.shape[0] // LANES, LANES))
    return call(functools.partial(rows_kernel, log_cols), "half_rows", out, [VMEM, VMEM], VMEM, got, block)


def cols_kernel(log_rows, got_ref, block_ref, out_ref):
    chunks = block_ref.shape[0] // LANES
    pot = -(log_rows + joined(got_ref[:, :chunks, :]))
    pot = jnp.concatenate([as_column(pot[k : k + 1]) for k in range(chunks)], axis=0)
    members = out_ref.shape[0]
    for k in range(out_ref.shape[1]):
        scores = block_ref[:, lanes(k)] + pot
        top = jnp.max(scores, axis=0, keepdims=True)
        local = top + jnp.log(jnp.sum(jnp.exp(scores - top), axis=0, keepdims=True))
        out_ref[:, k, :] = jnp.broadcast_to(local, (members, LANES))


def half_cols(got, block, members, log_rows):
    out = shape((members, block.shape[1] // LANES, LANES))
    return call(functools.partial(cols_kernel, log_rows), "half_cols", out, [VMEM, VMEM], VMEM, got, block)


def rounded(values):
    return values.astype(BF16).astype(F32)


def final_kernel(log_cols, got_ref, wide_ref, data_ref, out_ref, pot_ref, weights, held, sems):
    ny, nx, cols, width = data_ref.shape
    rows = wide_ref.shape[0]
    copies = [pltpu.make_async_copy(data_ref.at[:, x], held.at[x], sems.at[x]) for x in range(nx)]
    for copy in copies:
        copy.start()
    pot = -(log_cols + joined(got_ref[...]))
    pot_ref[...] = pot
    top = row_top(wide_ref, pot)
    total = None
    for k in range(pot.shape[0]):
        part = jnp.exp(wide_ref[:, lanes(k)] + pot[k : k + 1] - top)
        weights[:, lanes(k)] = part.astype(BF16)
        total = part if total is None else total + part
    total = jnp.sum(total, axis=1, keepdims=True)
    inverse = 1.0 / total
    local = as_rows(top + jnp.log(total))[:16]
    first = rounded(local)
    second = rounded(local - first)
    third = local - first - second
    place = lax.broadcasted_iota(jnp.int32, local.shape, 0)
    extra = jnp.where(place == 0, first, jnp.where(place == 1, second, third))
    extra = jnp.where(place < 3, extra, 0.0).astype(BF16)
    for x in range(nx):
        copies[x].wait()
        right = jnp.concatenate([held[x, y] for y in range(ny)], axis=0)
        term = jnp.dot(weights[...], right, preferred_element_type=F32)
        out_ref[x, :rows, :] = (term * inverse).astype(BF16)
        out_ref[x, rows:, :] = extra


def final_terms(got, wide, data, log_cols):
    ny, nx, cols, width = data.shape
    rows = wide.shape[0]
    return call(
        functools.partial(final_kernel, log_cols),
        "final_terms",
        (shape((nx, rows + 16, width), BF16), shape(got.shape[1:])),
        [VMEM, VMEM, HBM],
        (VMEM, VMEM),
        got,
        wide,
        data,
        scratch_shapes=[
            pltpu.VMEM(wide.shape, BF16),
            pltpu.VMEM((nx, ny, cols, width), BF16),
            pltpu.SemaphoreType.DMA((nx,)),
        ],
        vmem=50,
    )


def combine_kernel(log_rows, features, got_ref, began_ref, out_ref, pot_ref):
    nx, rows = got_ref.shape[0], out_ref.shape[0]
    chunks = rows // LANES
    locals_ = [jnp.sum(got_ref[x, rows:, :].astype(F32), axis=0, keepdims=True) for x in range(nx)]
    top = functools.reduce(jnp.maximum, locals_)
    whole = top + jnp.log(functools.reduce(jnp.add, [jnp.exp(v - top) for v in locals_]))
    noise_sq = jnp.sum(began_ref[:, chunks:, :], axis=0)
    for k in range(chunks):
        pot_ref[k : k + 1, :] = noise_sq[k : k + 1] * (1.0 / features) - EPSILON * (log_rows + whole[:, lanes(k)])
    scales = [as_column(jnp.exp(v - whole)) for v in locals_]
    for k in range(out_ref.shape[1] // LANES):
        parts = [scales[x] * got_ref[x, :rows, lanes(k)].astype(F32) for x in range(nx)]
        out_ref[:, lanes(k)] = functools.reduce(jnp.add, parts).astype(BF16)


def shards(noise, data):
    rows, width = noise.shape
    cols, features = data.shape
    nx, ny, nrow, ncol = (lax.axis_size(axes) for axes in ("x", "y", ROW, COL))
    log_rows, log_cols = _log(rows * nrow), _log(cols * ncol)
    chunks = rows // LANES

    low = rows - FIRST_ROWS
    share = cols // nrow
    by_x, by_y, noise_sq = call(
        functools.partial(prepare_kernel, FIRST_ROWS),
        "prepare",
        (
            shape((nx, FIRST_ROWS, width), BF16),
            shape((ny, low + nx * share, width), BF16),
            shape((chunks, LANES)),
        ),
        [VMEM, HBM],
        (VMEM, VMEM, VMEM),
        noise,
        data,
        scratch_shapes=[pltpu.VMEM((share, features), BF16), pltpu.SemaphoreType.DMA],
        vmem=52,
    )
    part = lax.all_to_all(by_x, "x", 0, 0)
    first = lax.all_gather(part, "y")
    part, by_y = lax.optimization_barrier((part, by_y))
    got = lax.all_to_all(by_y, "y", 0, 0)
    second = jnp.broadcast_to(got[None, :, :low], (nx, ny, low, width))
    second = lax.all_to_all(second, "x", 0, 0)
    piece = got[:, low:].reshape(ny, nx, share, width)

    data_sq = jnp.sum(jnp.square(data.astype(F32)), axis=1)
    col_pot = (data_sq * (-1.0 / (features * EPSILON))).reshape(-1, LANES)
    scale = 2.0 / (features * EPSILON)
    lower = call(
        functools.partial(second_kernel, scale),
        "second_rows",
        shape((low, cols)),
        [VMEM, HBM],
        VMEM,
        second,
        data,
        scratch_shapes=[pltpu.VMEM((ny, nx, cols, width), BF16), pltpu.SemaphoreType.DMA((ny, nx))],
        vmem=50,
    )
    scaled, copied, sent = call(
        functools.partial(first_kernel, scale),
        "first_rows",
        (shape((rows, cols)), shape((rows, cols)), shape((ncol, 2 * chunks, LANES))),
        [HBM, HBM, VMEM, VMEM, VMEM],
        (VMEM, HBM, VMEM),
        first,
        data,
        lower,
        col_pot,
        noise_sq,
        scratch_shapes=[
            pltpu.VMEM((ny, nx, FIRST_ROWS, width), BF16),
            pltpu.VMEM((ny, nx, cols, width), BF16),
            pltpu.SemaphoreType.DMA((ny, nx)),
            pltpu.SemaphoreType.DMA((ny + 1,)),
        ],
        vmem=52,
    )
    wide = lax.all_gather(copied, "y", axis=1, tiled=True)

    began = None
    for step in range(ITERS):
        got = lax.all_to_all(sent, "x" if step > WIDE_FROM else COL, 0, 0)
        if step == 0:
            began, piece = lax.optimization_barrier((got, piece))
            mine = lax.all_gather(piece, ROW, axis=2, tiled=True)
        sent = half_cols(got, wide if step >= WIDE_FROM else scaled, nrow, log_rows)
        got = lax.all_to_all(sent, ROW, 0, 0)
        if step < WIDE_FROM:
            sent = half_rows(got, scaled, ncol, log_cols)
        elif step < ITERS - 1:
            sent = half_rows(got, wide, nx, log_cols)
    terms, col_pot = final_terms(got, wide, mine, log_cols)
    own = lax.dynamic_slice_in_dim(col_pot, lax.axis_index("y") * (cols // LANES), cols // LANES, 0)
    data_potential = data_sq / features + EPSILON * own.reshape(cols)
    got = lax.all_to_all(terms, "x", 0, 0)
    targets, noise_potential = call(
        functools.partial(combine_kernel, log_rows, features),
        "combine",
        (shape((rows, width), BF16), shape((chunks, LANES))),
        [VMEM, VMEM],
        (VMEM, VMEM),
        got,
        began,
    )
    return (noise_potential.reshape(rows), data_potential, targets)


def _log(count):
    return float(np.log(np.float32(count)))


def solution(mesh):
    devices = mesh.devices.reshape(8, 2, 4, 8)
    return jax.shard_map(
        shards,
        mesh=Mesh(devices, ("z", "core", "x", "y")),
        in_specs=(P(ROW, COL), P(COL, None)),
        out_specs=(P(ROW), P(COL), P(ROW, COL)),
        check_vma=False,
    )
```

```python
import functools

import jax
import jax.numpy as jnp
import numpy as np
from jax import lax
from jax.experimental import pallas as pl
from jax.experimental.pallas import tpu as pltpu
from jax.sharding import Mesh, PartitionSpec as P

ITERS = 4
EPSILON = 0.01
ROW = ("z", "core")
COL = ("x", "y")
LANES = 128
FIRST_ROWS = 160
WIDE_FROM = 1
VMEM = pl.BlockSpec(memory_space=pltpu.VMEM)
HBM = pl.BlockSpec(memory_space=pltpu.HBM)
MIB = 2**20
F32, BF16 = jnp.float32, jnp.bfloat16


def call(kernel, name, out_shape, in_specs, out_specs, *args, scratch_shapes=(), vmem=40):
    return pl.pallas_call(
        kernel,
        out_shape=out_shape,
        in_specs=in_specs,
        out_specs=out_specs,
        scratch_shapes=scratch_shapes,
        compiler_params=pltpu.CompilerParams(vmem_limit_bytes=vmem * MIB),
        name=name,
    )(*args)


def shape(dims, dtype=F32):
    return jax.ShapeDtypeStruct(dims, dtype)


def lanes(k):
    return slice(k * LANES, (k + 1) * LANES)


def as_column(values):
    return jnp.broadcast_to(values, (LANES, values.shape[1])).T


def as_rows(column):
    return jnp.broadcast_to(column, (column.shape[0], LANES)).T


def joined(got):
    top = jnp.max(got, axis=0)
    return top + jnp.log(jnp.sum(jnp.exp(got - top[None]), axis=0))


def prepare_kernel(high, noise_ref, data_ref, by_x_ref, by_y_ref, sq_ref, held, sem):
    nx = by_x_ref.shape[0]
    ny, sent, width = by_y_ref.shape
    rows = noise_ref.shape[0]
    low = rows - high
    share = (sent - low) // nx
    at = (lax.axis_index(ROW[0]) * lax.axis_size(ROW[1]) + lax.axis_index(ROW[1])) * share
    copy = pltpu.make_async_copy(data_ref.at[pl.ds(pl.multiple_of(at, share), share), :], held, sem)
    copy.start()
    for x in range(nx):
        by_x_ref[x] = noise_ref[:high]
    for y in range(ny):
        by_y_ref[y, :low] = noise_ref[high:]
    squares = jnp.square(noise_ref[...].astype(F32))
    squares = as_rows(jnp.sum(squares, axis=1, keepdims=True))[:1]
    for k in range(rows // LANES):
        sq_ref[k : k + 1, :] = squares[:, lanes(k)]
    copy.wait()
    for y in range(ny):
        for x in range(nx):
            block = held[:, (x * ny + y) * width : (x * ny + y + 1) * width]
            by_y_ref[y, low + x * share : low + (x + 1) * share] = block


def products(read, data_ref, nx, ny, width):
    total = None
    for y in range(ny):
        for x in range(nx):
            at = (x * ny + y) * width
            one = lax.dot_general(
                read(y, x), data_ref[:, at : at + width], (((1,), (1,)), ((), ())), preferred_element_type=F32
            )
            total = one if total is None else total + one
    return total


def second_kernel(scale, second_ref, data_ref, out_ref):
    nx, ny, _, width = second_ref.shape
    out_ref[...] = products(lambda y, x: second_ref[x, y], data_ref, nx, ny, width) * scale


def first_kernel(scale, first_ref, data_ref, low_ref, pot_ref, sq_ref, out_ref, copy_ref, send_ref, sem):
    ny, nx, high, width = first_ref.shape
    out_ref[:high] = products(lambda y, x: first_ref[y, x], data_ref, nx, ny, width) * scale
    out_ref[high:] = low_ref[...]
    out = pltpu.make_async_copy(out_ref, copy_ref, sem)
    out.start()
    local = local_rows(out_ref, pot_ref[...])
    chunks = local.shape[1] // LANES
    members = send_ref.shape[0]
    for k in range(chunks):
        send_ref[:, k, :] = jnp.broadcast_to(local[:, lanes(k)], (members, LANES))
        send_ref[:, chunks + k, :] = jnp.broadcast_to(sq_ref[k : k + 1], (members, LANES))
    out.wait()


def row_top(block_ref, pot):
    top = None
    for k in range(pot.shape[0]):
        scores = block_ref[:, lanes(k)] + pot[k : k + 1]
        top = scores if top is None else jnp.maximum(top, scores)
    return jnp.max(top, axis=1, keepdims=True)


def local_rows(block_ref, pot):
    top = row_top(block_ref, pot)
    total = None
    for k in range(pot.shape[0]):
        part = jnp.exp(block_ref[:, lanes(k)] + pot[k : k + 1] - top)
        total = part if total is None else total + part
    return as_rows(top + jnp.log(jnp.sum(total, axis=1, keepdims=True)))[:1]


def rows_kernel(log_cols, got_ref, block_ref, out_ref):
    local = local_rows(block_ref, -(log_cols + joined(got_ref[...])))
    for k in range(out_ref.shape[1]):
        out_ref[:, k, :] = jnp.broadcast_to(local[:, lanes(k)], (out_ref.shape[0], LANES))


def half_rows(got, block, members, log_cols):
    out = shape((members, block.shape[0] // LANES, LANES))
    return call(functools.partial(rows_kernel, log_cols), "half_rows", out, [VMEM, VMEM], VMEM, got, block)


def cols_kernel(log_rows, got_ref, block_ref, out_ref, *kept_ref):
    chunks = block_ref.shape[0] // LANES
    pot = -(log_rows + joined(got_ref[:, :chunks, :]))
    pot = jnp.concatenate([as_column(pot[k : k + 1]) for k in range(chunks)], axis=0)
    members = out_ref.shape[0]
    for k in range(out_ref.shape[1]):
        block = block_ref[:, lanes(k)]
        for kept in kept_ref:
            kept[:, lanes(k)] = block
        scores = block + pot
        top = jnp.max(scores, axis=0, keepdims=True)
        local = top + jnp.log(jnp.sum(jnp.exp(scores - top), axis=0, keepdims=True))
        out_ref[:, k, :] = jnp.broadcast_to(local, (members, LANES))


def half_cols(got, block, members, log_rows, keep=False):
    out = [shape((members, block.shape[1] // LANES, LANES))] + [shape(block.shape)] * keep
    return call(
        functools.partial(cols_kernel, log_rows), "half_cols", out, [VMEM, VMEM], [VMEM] * len(out), got, block
    )


def rounded(values):
    return values.astype(BF16).astype(F32)


def final_kernel(log_cols, got_ref, wide_ref, data_ref, out_ref, pot_ref, weights, held, terms, sems):
    ny, nx, cols, width = data_ref.shape
    rows = wide_ref.shape[0]
    copies = [pltpu.make_async_copy(data_ref.at[y], held.at[y], sems.at[y]) for y in range(ny)]
    for copy in copies:
        copy.start()
    pot = -(log_cols + joined(got_ref[...]))
    pot_ref[...] = pot
    top = row_top(wide_ref, pot)
    total = None
    for k in range(pot.shape[0]):
        part = jnp.exp(wide_ref[:, lanes(k)] + pot[k : k + 1] - top)
        weights[:, lanes(k)] = part.astype(BF16)
        total = part if total is None else total + part
    total = jnp.sum(total, axis=1, keepdims=True)
    inverse = 1.0 / total
    local = as_rows(top + jnp.log(total))[:16]
    first = rounded(local)
    second = rounded(local - first)
    third = local - first - second
    place = lax.broadcasted_iota(jnp.int32, local.shape, 0)
    extra = jnp.where(place == 0, first, jnp.where(place == 1, second, third))
    extra = jnp.where(place < 3, extra, 0.0).astype(BF16)
    half = ny // 2
    for copy in copies[:half]:
        copy.wait()
    for x in range(nx):
        right = jnp.concatenate([held[y, x] for y in range(half)], axis=0)
        terms[x] = jnp.dot(weights[:, : half * cols], right, preferred_element_type=F32)
    for copy in copies[half:]:
        copy.wait()
    for x in range(nx):
        right = jnp.concatenate([held[y, x] for y in range(half, ny)], axis=0)
        term = terms[x] + jnp.dot(weights[:, half * cols :], right, preferred_element_type=F32)
        out_ref[x, :rows, :] = (term * inverse).astype(BF16)
        out_ref[x, rows:, :] = extra


def final_terms(got, wide, data, log_cols):
    ny, nx, cols, width = data.shape
    rows = wide.shape[0]
    return call(
        functools.partial(final_kernel, log_cols),
        "final_terms",
        (shape((nx, rows + 16, width), BF16), shape(got.shape[1:])),
        [VMEM, VMEM, HBM],
        (VMEM, VMEM),
        got,
        wide,
        data,
        scratch_shapes=[
            pltpu.VMEM(wide.shape, BF16),
            pltpu.VMEM(data.shape, BF16),
            pltpu.VMEM((nx, rows, width), F32),
            pltpu.SemaphoreType.DMA((ny,)),
        ],
        vmem=50,
    )


def combine_kernel(log_rows, features, got_ref, began_ref, out_ref, pot_ref):
    nx, rows = got_ref.shape[0], out_ref.shape[0]
    chunks = rows // LANES
    locals_ = [jnp.sum(got_ref[x, rows:, :].astype(F32), axis=0, keepdims=True) for x in range(nx)]
    top = functools.reduce(jnp.maximum, locals_)
    whole = top + jnp.log(functools.reduce(jnp.add, [jnp.exp(v - top) for v in locals_]))
    noise_sq = jnp.sum(began_ref[:, chunks:, :], axis=0)
    for k in range(chunks):
        pot_ref[k : k + 1, :] = noise_sq[k : k + 1] * (1.0 / features) - EPSILON * (log_rows + whole[:, lanes(k)])
    scales = [as_column(jnp.exp(v - whole)) for v in locals_]
    for k in range(out_ref.shape[1] // LANES):
        parts = [scales[x] * got_ref[x, :rows, lanes(k)].astype(F32) for x in range(nx)]
        out_ref[:, lanes(k)] = functools.reduce(jnp.add, parts).astype(BF16)


def shards(noise, data):
    rows, width = noise.shape
    cols, features = data.shape
    nx, ny, nrow, ncol = (lax.axis_size(axes) for axes in ("x", "y", ROW, COL))
    log_rows, log_cols = _log(rows * nrow), _log(cols * ncol)
    chunks = rows // LANES

    low = rows - FIRST_ROWS
    share = cols // nrow
    by_x, by_y, noise_sq = call(
        functools.partial(prepare_kernel, FIRST_ROWS),
        "prepare",
        (
            shape((nx, FIRST_ROWS, width), BF16),
            shape((ny, low + nx * share, width), BF16),
            shape((chunks, LANES)),
        ),
        [VMEM, HBM],
        (VMEM, VMEM, VMEM),
        noise,
        data,
        scratch_shapes=[pltpu.VMEM((share, features), BF16), pltpu.SemaphoreType.DMA],
        vmem=52,
    )
    part = lax.all_to_all(by_x, "x", 0, 0)
    first = lax.all_gather(part, "y")
    part, by_y = lax.optimization_barrier((part, by_y))
    got = lax.all_to_all(by_y, "y", 0, 0)
    second = jnp.broadcast_to(got[None, :, :low], (nx, ny, low, width))
    second = lax.all_to_all(second, "x", 0, 0)
    piece = got[:, low:].reshape(ny, nx, share, width)

    scale = 2.0 / (features * EPSILON)
    data_sq = jnp.sum(jnp.square(data.astype(F32)), axis=1)
    col_pot = (data_sq * (-1.0 / (features * EPSILON))).reshape(-1, LANES)
    lower = call(
        functools.partial(second_kernel, scale), "second_rows", shape((low, cols)), [VMEM, VMEM], VMEM, second, data
    )
    scaled, copied, sent = call(
        functools.partial(first_kernel, scale),
        "first_rows",
        (shape((rows, cols)), shape((rows, cols)), shape((ncol, 2 * chunks, LANES))),
        [VMEM] * 5,
        (VMEM, HBM, VMEM),
        first,
        data,
        lower,
        col_pot,
        noise_sq,
        scratch_shapes=[pltpu.SemaphoreType.DMA],
    )
    wide = lax.all_gather(copied, "y", axis=1, tiled=True)

    began = None
    for step in range(ITERS):
        got = lax.all_to_all(sent, "x" if step > WIDE_FROM else COL, 0, 0)
        if step == 0:
            began, piece = lax.optimization_barrier((got, piece))
            mine = lax.all_gather(piece, ROW, axis=2, tiled=True)
        if step == WIDE_FROM:
            sent, wide = half_cols(got, wide, nrow, log_rows, keep=True)
        else:
            (sent,) = half_cols(got, wide if step > WIDE_FROM else scaled, nrow, log_rows)
        got = lax.all_to_all(sent, ROW, 0, 0)
        if step < WIDE_FROM:
            sent = half_rows(got, scaled, ncol, log_cols)
        elif step < ITERS - 1:
            sent = half_rows(got, wide, nx, log_cols)
    terms, col_pot = final_terms(got, wide, mine, log_cols)
    own = lax.dynamic_slice_in_dim(col_pot, lax.axis_index("y") * (cols // LANES), cols // LANES, 0)
    data_potential = data_sq / features + EPSILON * own.reshape(cols)
    got = lax.all_to_all(terms, "x", 0, 0)
    targets, noise_potential = call(
        functools.partial(combine_kernel, log_rows, features),
        "combine",
        (shape((rows, width), BF16), shape((chunks, LANES))),
        [VMEM, VMEM],
        (VMEM, VMEM),
        got,
        began,
    )
    return (noise_potential.reshape(rows), data_potential, targets)


def _log(count):
    return float(np.log(np.float32(count)))


def solution(mesh):
    devices = mesh.devices.reshape(8, 2, 4, 8)
    return jax.shard_map(
        shards,
        mesh=Mesh(devices, ("z", "core", "x", "y")),
        in_specs=(P(ROW, COL), P(COL, None)),
        out_specs=(P(ROW), P(COL), P(ROW, COL)),
        check_vma=False,
    )
```

```python
import functools

import jax
import jax.numpy as jnp
import numpy as np
from jax import lax
from jax.experimental import pallas as pl
from jax.experimental.pallas import tpu as pltpu
from jax.sharding import Mesh, PartitionSpec as P

ITERS = 4
EPSILON = 0.01
ROW = ("z", "core")
COL = ("x", "y")
LANES = 128
FIRST_ROWS = 160
WIDE_FROM = 1
VMEM = pl.BlockSpec(memory_space=pltpu.VMEM)
HBM = pl.BlockSpec(memory_space=pltpu.HBM)
MIB = 2**20
F32, BF16 = jnp.float32, jnp.bfloat16


def call(kernel, name, out_shape, in_specs, out_specs, *args, scratch_shapes=(), vmem=40, cost=None):
    return pl.pallas_call(
        kernel,
        out_shape=out_shape,
        in_specs=in_specs,
        out_specs=out_specs,
        scratch_shapes=scratch_shapes,
        compiler_params=pltpu.CompilerParams(vmem_limit_bytes=vmem * MIB),
        cost_estimate=cost,
        name=name,
    )(*args)


def shape(dims, dtype=F32):
    return jax.ShapeDtypeStruct(dims, dtype)


def lanes(k):
    return slice(k * LANES, (k + 1) * LANES)


def as_column(values):
    return jnp.broadcast_to(values, (LANES, values.shape[1])).T


def as_rows(column):
    return jnp.broadcast_to(column, (column.shape[0], LANES)).T


def joined(got):
    top = jnp.max(got, axis=0)
    return top + jnp.log(jnp.sum(jnp.exp(got - top[None]), axis=0))


def prepare_kernel(high, noise_ref, data_ref, by_x_ref, by_y_ref, sq_ref, held, sem):
    nx = by_x_ref.shape[0]
    ny, sent, width = by_y_ref.shape
    rows = noise_ref.shape[0]
    low = rows - high
    share = (sent - low) // nx
    at = (lax.axis_index(ROW[0]) * lax.axis_size(ROW[1]) + lax.axis_index(ROW[1])) * share
    copy = pltpu.make_async_copy(data_ref.at[pl.ds(pl.multiple_of(at, share), share), :], held, sem)
    copy.start()
    for x in range(nx):
        by_x_ref[x] = noise_ref[:high]
    for y in range(ny):
        by_y_ref[y, :low] = noise_ref[high:]
    squares = jnp.square(noise_ref[...].astype(F32))
    squares = as_rows(jnp.sum(squares, axis=1, keepdims=True))[:1]
    for k in range(rows // LANES):
        sq_ref[k : k + 1, :] = squares[:, lanes(k)]
    copy.wait()
    for y in range(ny):
        for x in range(nx):
            block = held[:, (x * ny + y) * width : (x * ny + y + 1) * width]
            by_y_ref[y, low + x * share : low + (x + 1) * share] = block


def fan_kernel(got_ref, second_ref, piece_ref):
    nx, ny, low, _ = second_ref.shape
    share = piece_ref.shape[2]
    for y in range(ny):
        block = got_ref[y, :low]
        for x in range(nx):
            second_ref[x, y] = block
            piece_ref[y, x] = got_ref[y, low + x * share : low + (x + 1) * share]


def load_kernel(scale, after_ref, data_ref, out_ref, pot_ref, sems):
    parts = pot_ref.shape[0]
    copies = [pltpu.make_async_copy(data_ref.at[lanes(k)], out_ref.at[lanes(k)], sems.at[k]) for k in range(parts)]
    for copy in copies:
        copy.start()
    for k in range(parts):
        copies[k].wait()
        total = None
        for f in range(out_ref.shape[1] // LANES):
            block = out_ref[lanes(k), lanes(f)].astype(F32)
            total = block * block if total is None else total + block * block
        pot_ref[k : k + 1, :] = as_rows(jnp.sum(total, axis=1, keepdims=True))[:1] * scale


def products(read, data_ref, nx, ny, width):
    total = None
    for y in range(ny):
        for x in range(nx):
            at = (x * ny + y) * width
            one = lax.dot_general(
                read(y, x), data_ref[:, at : at + width], (((1,), (1,)), ((), ())), preferred_element_type=F32
            )
            total = one if total is None else total + one
    return total


def second_kernel(scale, second_ref, data_ref, out_ref):
    nx, ny, _, width = second_ref.shape
    out_ref[...] = products(lambda y, x: second_ref[x, y], data_ref, nx, ny, width) * scale


def first_kernel(scale, first_ref, data_ref, low_ref, pot_ref, sq_ref, out_ref, copy_ref, send_ref, sem):
    ny, nx, high, width = first_ref.shape
    out_ref[:high] = products(lambda y, x: first_ref[y, x], data_ref, nx, ny, width) * scale
    out_ref[high:] = low_ref[...]
    out = pltpu.make_async_copy(out_ref, copy_ref, sem)
    out.start()
    local = local_rows(out_ref, pot_ref[...])
    chunks = local.shape[1] // LANES
    members = send_ref.shape[0]
    for k in range(chunks):
        send_ref[:, k, :] = jnp.broadcast_to(local[:, lanes(k)], (members, LANES))
        send_ref[:, chunks + k, :] = jnp.broadcast_to(sq_ref[k : k + 1], (members, LANES))
    out.wait()


def row_top(block_ref, pot):
    top = None
    for k in range(pot.shape[0]):
        scores = block_ref[:, lanes(k)] + pot[k : k + 1]
        top = scores if top is None else jnp.maximum(top, scores)
    return jnp.max(top, axis=1, keepdims=True)


def local_rows(block_ref, pot):
    top = row_top(block_ref, pot)
    total = None
    for k in range(pot.shape[0]):
        part = jnp.exp(block_ref[:, lanes(k)] + pot[k : k + 1] - top)
        total = part if total is None else total + part
    return as_rows(top + jnp.log(jnp.sum(total, axis=1, keepdims=True)))[:1]


def rows_kernel(log_cols, got_ref, block_ref, out_ref):
    local = local_rows(block_ref, -(log_cols + joined(got_ref[...])))
    for k in range(out_ref.shape[1]):
        out_ref[:, k, :] = jnp.broadcast_to(local[:, lanes(k)], (out_ref.shape[0], LANES))


def half_rows(got, block, members, log_cols):
    out = shape((members, block.shape[0] // LANES, LANES))
    return call(functools.partial(rows_kernel, log_cols), "half_rows", out, [VMEM, VMEM], VMEM, got, block)


def column_pot(got_ref, chunks, log_rows):
    pot = -(log_rows + joined(got_ref[:, :chunks, :]))
    return jnp.concatenate([as_column(pot[k : k + 1]) for k in range(chunks)], axis=0)


def send_cols(block_ref, pot, out_ref, places):
    for k in places:
        scores = block_ref[:, lanes(k)] + pot
        top = jnp.max(scores, axis=0, keepdims=True)
        local = top + jnp.log(jnp.sum(jnp.exp(scores - top), axis=0, keepdims=True))
        out_ref[:, k, :] = jnp.broadcast_to(local, (out_ref.shape[0], LANES))


def cols_kernel(log_rows, got_ref, block_ref, out_ref):
    pot = column_pot(got_ref, block_ref.shape[0] // LANES, log_rows)
    send_cols(block_ref, pot, out_ref, range(out_ref.shape[1]))


def half_cols(got, block, members, log_rows):
    out = shape((members, block.shape[1] // LANES, LANES))
    return call(functools.partial(cols_kernel, log_rows), "half_cols", out, [VMEM, VMEM], VMEM, got, block)


def first_wide_kernel(log_rows, got_ref, block_ref, out_ref, held_ref, sems):
    parts = sems.shape[0]
    places = out_ref.shape[1] // parts
    width = places * LANES
    copies = [
        pltpu.make_async_copy(
            block_ref.at[:, k * width : (k + 1) * width], held_ref.at[:, k * width : (k + 1) * width], sems.at[k]
        )
        for k in range(parts)
    ]
    for copy in copies:
        copy.start()
    pot = column_pot(got_ref, block_ref.shape[0] // LANES, log_rows)
    for k in range(parts):
        copies[k].wait()
        send_cols(held_ref, pot, out_ref, range(k * places, (k + 1) * places))


def first_wide(got, block, members, log_rows):
    return call(
        functools.partial(first_wide_kernel, log_rows),
        "first_wide",
        (shape((members, block.shape[1] // LANES, LANES)), shape(block.shape)),
        [VMEM, HBM],
        (VMEM, VMEM),
        got,
        block,
        scratch_shapes=[pltpu.SemaphoreType.DMA((4,))],
        vmem=51,
    )


def rounded(values):
    return values.astype(BF16).astype(F32)


def final_kernel(log_cols, got_ref, wide_ref, data_ref, out_ref, pot_ref, weights, held, terms, sems):
    ny, nx, cols, width = data_ref.shape
    rows = wide_ref.shape[0]
    copies = [pltpu.make_async_copy(data_ref.at[y], held.at[y], sems.at[y]) for y in range(ny)]
    for copy in copies:
        copy.start()
    pot = -(log_cols + joined(got_ref[...]))
    pot_ref[...] = pot
    top = row_top(wide_ref, pot)
    total = None
    for k in range(pot.shape[0]):
        part = jnp.exp(wide_ref[:, lanes(k)] + pot[k : k + 1] - top)
        weights[:, lanes(k)] = part.astype(BF16)
        total = part if total is None else total + part
    total = jnp.sum(total, axis=1, keepdims=True)
    inverse = 1.0 / total
    local = as_rows(top + jnp.log(total))[:16]
    first = rounded(local)
    second = rounded(local - first)
    third = local - first - second
    place = lax.broadcasted_iota(jnp.int32, local.shape, 0)
    extra = jnp.where(place == 0, first, jnp.where(place == 1, second, third))
    extra = jnp.where(place < 3, extra, 0.0).astype(BF16)
    half = ny // 2
    for copy in copies[:half]:
        copy.wait()
    for x in range(nx):
        right = jnp.concatenate([held[y, x] for y in range(half)], axis=0)
        terms[x] = jnp.dot(weights[:, : half * cols], right, preferred_element_type=F32)
    for copy in copies[half:]:
        copy.wait()
    for x in range(nx):
        right = jnp.concatenate([held[y, x] for y in range(half, ny)], axis=0)
        term = terms[x] + jnp.dot(weights[:, half * cols :], right, preferred_element_type=F32)
        out_ref[x, :rows, :] = (term * inverse).astype(BF16)
        out_ref[x, rows:, :] = extra


def final_terms(got, wide, data, log_cols):
    ny, nx, cols, width = data.shape
    rows = wide.shape[0]
    return call(
        functools.partial(final_kernel, log_cols),
        "final_terms",
        (shape((nx, rows + 16, width), BF16), shape(got.shape[1:])),
        [VMEM, VMEM, HBM],
        (VMEM, VMEM),
        got,
        wide,
        data,
        scratch_shapes=[
            pltpu.VMEM(wide.shape, BF16),
            pltpu.VMEM(data.shape, BF16),
            pltpu.VMEM((nx, rows, width), F32),
            pltpu.SemaphoreType.DMA((ny,)),
        ],
        vmem=50,
    )


def combine_kernel(log_rows, features, got_ref, began_ref, out_ref, pot_ref):
    nx, rows = got_ref.shape[0], out_ref.shape[0]
    chunks = rows // LANES
    locals_ = [jnp.sum(got_ref[x, rows:, :].astype(F32), axis=0, keepdims=True) for x in range(nx)]
    top = functools.reduce(jnp.maximum, locals_)
    whole = top + jnp.log(functools.reduce(jnp.add, [jnp.exp(v - top) for v in locals_]))
    noise_sq = jnp.sum(began_ref[:, chunks:, :], axis=0)
    for k in range(chunks):
        pot_ref[k : k + 1, :] = noise_sq[k : k + 1] * (1.0 / features) - EPSILON * (log_rows + whole[:, lanes(k)])
    scales = [as_column(jnp.exp(v - whole)) for v in locals_]
    for k in range(out_ref.shape[1] // LANES):
        parts = [scales[x] * got_ref[x, :rows, lanes(k)].astype(F32) for x in range(nx)]
        out_ref[:, lanes(k)] = functools.reduce(jnp.add, parts).astype(BF16)


def shards(noise, data):
    rows, width = noise.shape
    cols, features = data.shape
    nx, ny, nrow, ncol = (lax.axis_size(axes) for axes in ("x", "y", ROW, COL))
    log_rows, log_cols = _log(rows * nrow), _log(cols * ncol)
    chunks = rows // LANES

    low = rows - FIRST_ROWS
    share = cols // nrow
    by_x, by_y, noise_sq = call(
        functools.partial(prepare_kernel, FIRST_ROWS),
        "prepare",
        (
            shape((nx, FIRST_ROWS, width), BF16),
            shape((ny, low + nx * share, width), BF16),
            shape((chunks, LANES)),
        ),
        [VMEM, HBM],
        (VMEM, VMEM, VMEM),
        noise,
        data,
        scratch_shapes=[pltpu.VMEM((share, features), BF16), pltpu.SemaphoreType.DMA],
        vmem=52,
    )
    part = lax.all_to_all(by_x, "x", 0, 0)
    first = lax.all_gather(part, "y")
    part, by_y = lax.optimization_barrier((part, by_y))
    got = lax.all_to_all(by_y, "y", 0, 0)
    second, piece = call(
        fan_kernel,
        "fan",
        (shape((nx, ny, low, width), BF16), shape((ny, nx, share, width), BF16)),
        [VMEM],
        (VMEM, VMEM),
        got,
    )
    second = lax.all_to_all(second, "x", 0, 0)

    scale = 2.0 / (features * EPSILON)
    held, col_pot = call(
        functools.partial(load_kernel, -1.0 / (features * EPSILON)),
        "load",
        (shape(data.shape, BF16), shape((cols // LANES, LANES))),
        [HBM, HBM],
        (VMEM, VMEM),
        got,
        data,
        scratch_shapes=[pltpu.SemaphoreType.DMA((cols // LANES,))],
        vmem=48,
        cost=pl.CostEstimate(flops=4 * data.size, bytes_accessed=4 * data.size, transcendentals=0),
    )
    data_sq = col_pot * -EPSILON
    lower = call(
        functools.partial(second_kernel, scale), "second_rows", shape((low, cols)), [VMEM, VMEM], VMEM, second, held
    )
    scaled, copied, sent = call(
        functools.partial(first_kernel, scale),
        "first_rows",
        (shape((rows, cols)), shape((rows, cols)), shape((ncol, 2 * chunks, LANES))),
        [VMEM] * 5,
        (VMEM, HBM, VMEM),
        first,
        held,
        lower,
        col_pot,
        noise_sq,
        scratch_shapes=[pltpu.SemaphoreType.DMA],
    )
    wide = lax.all_gather(copied, "y", axis=1, tiled=True)

    began = None
    for step in range(ITERS):
        got = lax.all_to_all(sent, "x" if step > WIDE_FROM else COL, 0, 0)
        if step == 0:
            began, piece = lax.optimization_barrier((got, piece))
            mine = lax.all_gather(piece, ROW, axis=2, tiled=True)
        if step == WIDE_FROM:
            sent, wide = first_wide(got, wide, nrow, log_rows)
        else:
            sent = half_cols(got, wide if step > WIDE_FROM else scaled, nrow, log_rows)
        got = lax.all_to_all(sent, ROW, 0, 0)
        if step < WIDE_FROM:
            sent = half_rows(got, scaled, ncol, log_cols)
        elif step < ITERS - 1:
            sent = half_rows(got, wide, nx, log_cols)
    terms, col_pot = final_terms(got, wide, mine, log_cols)
    own = lax.dynamic_slice_in_dim(col_pot, lax.axis_index("y") * (cols // LANES), cols // LANES, 0)
    data_potential = (data_sq + EPSILON * own).reshape(cols)
    got = lax.all_to_all(terms, "x", 0, 0)
    targets, noise_potential = call(
        functools.partial(combine_kernel, log_rows, features),
        "combine",
        (shape((rows, width), BF16), shape((chunks, LANES))),
        [VMEM, VMEM],
        (VMEM, VMEM),
        got,
        began,
    )
    return (noise_potential.reshape(rows), data_potential, targets)


def _log(count):
    return float(np.log(np.float32(count)))


def solution(mesh):
    devices = mesh.devices.reshape(8, 2, 4, 8)
    return jax.shard_map(
        shards,
        mesh=Mesh(devices, ("z", "core", "x", "y")),
        in_specs=(P(ROW, COL), P(COL, None)),
        out_specs=(P(ROW), P(COL), P(ROW, COL)),
        check_vma=False,
    )
```

```python
import functools

import jax
import jax.numpy as jnp
import numpy as np
from jax import lax
from jax.experimental import pallas as pl
from jax.experimental.pallas import tpu as pltpu
from jax.sharding import Mesh, PartitionSpec as P

ITERS = 4
EPSILON = 0.01
ROW = ("z", "core")
COL = ("x", "y")
LANES = 128
FIRST_ROWS = 160
WIDE_FROM = 1
VMEM = pl.BlockSpec(memory_space=pltpu.VMEM)
HBM = pl.BlockSpec(memory_space=pltpu.HBM)
MIB = 2**20
F32, BF16 = jnp.float32, jnp.bfloat16


def call(kernel, name, out_shape, in_specs, out_specs, *args, scratch_shapes=(), vmem=40):
    return pl.pallas_call(
        kernel,
        out_shape=out_shape,
        in_specs=in_specs,
        out_specs=out_specs,
        scratch_shapes=scratch_shapes,
        compiler_params=pltpu.CompilerParams(vmem_limit_bytes=vmem * MIB),
        name=name,
    )(*args)


def shape(dims, dtype=F32):
    return jax.ShapeDtypeStruct(dims, dtype)


def lanes(k):
    return slice(k * LANES, (k + 1) * LANES)


def as_column(values):
    return jnp.broadcast_to(values, (LANES, values.shape[1])).T


def as_rows(column):
    return jnp.broadcast_to(column, (column.shape[0], LANES)).T


def joined(got):
    top = jnp.max(got, axis=0)
    return top + jnp.log(jnp.sum(jnp.exp(got - top[None]), axis=0))


def prepare_kernel(high, noise_ref, data_ref, by_x_ref, by_y_ref, sq_ref, held, sem):
    nx = by_x_ref.shape[0]
    ny, sent, width = by_y_ref.shape
    rows = noise_ref.shape[0]
    low = rows - high
    share = (sent - low) // nx
    at = (lax.axis_index(ROW[0]) * lax.axis_size(ROW[1]) + lax.axis_index(ROW[1])) * share
    copy = pltpu.make_async_copy(data_ref.at[pl.ds(pl.multiple_of(at, share), share), :], held, sem)
    copy.start()
    for x in range(nx):
        by_x_ref[x] = noise_ref[:high]
    for y in range(ny):
        by_y_ref[y, :low] = noise_ref[high:]
    squares = jnp.square(noise_ref[...].astype(F32))
    squares = as_rows(jnp.sum(squares, axis=1, keepdims=True))[:1]
    for k in range(rows // LANES):
        sq_ref[k : k + 1, :] = squares[:, lanes(k)]
    copy.wait()
    for y in range(ny):
        for x in range(nx):
            block = held[:, (x * ny + y) * width : (x * ny + y + 1) * width]
            by_y_ref[y, low + x * share : low + (x + 1) * share] = block


def inner_kernel(
    scale, first_ref, second_ref, data_ref, pot_ref, sq_ref, out_ref, copy_ref, send_ref, rows_held, held, row_sems, sems
):
    ny, nx, _, width = first_ref.shape
    wide = ny * width
    copies = [
        (
            pltpu.make_async_copy(
                data_ref.at[:, x * wide : (x + 1) * wide], held.at[:, x * wide : (x + 1) * wide], sems.at[x]
            ),
            pltpu.make_async_copy(first_ref.at[:, x], rows_held.at[:, x], row_sems.at[x]),
        )
        for x in range(nx)
    ]
    for pair in copies:
        for copy in pair:
            copy.start()
    total = None
    for x in range(nx):
        for copy in copies[x]:
            copy.wait()
        for y in range(ny):
            left = jnp.concatenate([rows_held[y, x], second_ref[x, y]], axis=0)
            at = x * wide + y * width
            one = lax.dot_general(
                left, held[:, at : at + width], (((1,), (1,)), ((), ())), preferred_element_type=F32
            )
            total = one if total is None else total + one
    out_ref[...] = total * scale
    out = pltpu.make_async_copy(out_ref, copy_ref, sems.at[nx])
    out.start()
    local = local_rows(out_ref, pot_ref[...])
    chunks = local.shape[1] // LANES
    members = send_ref.shape[0]
    for k in range(chunks):
        send_ref[:, k, :] = jnp.broadcast_to(local[:, lanes(k)], (members, LANES))
        send_ref[:, chunks + k, :] = jnp.broadcast_to(sq_ref[k : k + 1], (members, LANES))
    out.wait()


def row_top(block_ref, pot):
    top = None
    for k in range(pot.shape[0]):
        scores = block_ref[:, lanes(k)] + pot[k : k + 1]
        top = scores if top is None else jnp.maximum(top, scores)
    return jnp.max(top, axis=1, keepdims=True)


def local_rows(block_ref, pot):
    top = row_top(block_ref, pot)
    total = None
    for k in range(pot.shape[0]):
        part = jnp.exp(block_ref[:, lanes(k)] + pot[k : k + 1] - top)
        total = part if total is None else total + part
    return as_rows(top + jnp.log(jnp.sum(total, axis=1, keepdims=True)))[:1]


def rows_kernel(log_cols, got_ref, block_ref, out_ref):
    local = local_rows(block_ref, -(log_cols + joined(got_ref[...])))
    for k in range(out_ref.shape[1]):
        out_ref[:, k, :] = jnp.broadcast_to(local[:, lanes(k)], (out_ref.shape[0], LANES))


def half_rows(got, block, members, log_cols):
    out = shape((members, block.shape[0] // LANES, LANES))
    return call(functools.partial(rows_kernel, log_cols), "half_rows", out, [VMEM, VMEM], VMEM, got, block)


def column_pot(got_ref, chunks, log_rows):
    pot = -(log_rows + joined(got_ref[:, :chunks, :]))
    return jnp.concatenate([as_column(pot[k : k + 1]) for k in range(chunks)], axis=0)


def send_cols(block_ref, pot, out_ref, places):
    for k in places:
        scores = block_ref[:, lanes(k)] + pot
        top = jnp.max(scores, axis=0, keepdims=True)
        local = top + jnp.log(jnp.sum(jnp.exp(scores - top), axis=0, keepdims=True))
        out_ref[:, k, :] = jnp.broadcast_to(local, (out_ref.shape[0], LANES))


def cols_kernel(log_rows, got_ref, block_ref, out_ref):
    pot = column_pot(got_ref, block_ref.shape[0] // LANES, log_rows)
    send_cols(block_ref, pot, out_ref, range(out_ref.shape[1]))


def half_cols(got, block, members, log_rows):
    out = shape((members, block.shape[1] // LANES, LANES))
    return call(functools.partial(cols_kernel, log_rows), "half_cols", out, [VMEM, VMEM], VMEM, got, block)


def first_wide_kernel(log_rows, got_ref, block_ref, out_ref, held_ref, sems):
    parts = sems.shape[0]
    places = out_ref.shape[1] // parts
    width = places * LANES
    copies = [
        pltpu.make_async_copy(
            block_ref.at[:, k * width : (k + 1) * width], held_ref.at[:, k * width : (k + 1) * width], sems.at[k]
        )
        for k in range(parts)
    ]
    for copy in copies:
        copy.start()
    pot = column_pot(got_ref, block_ref.shape[0] // LANES, log_rows)
    for k in range(parts):
        copies[k].wait()
        send_cols(held_ref, pot, out_ref, range(k * places, (k + 1) * places))


def first_wide(got, block, members, log_rows):
    return call(
        functools.partial(first_wide_kernel, log_rows),
        "first_wide",
        (shape((members, block.shape[1] // LANES, LANES)), shape(block.shape)),
        [VMEM, HBM],
        (VMEM, VMEM),
        got,
        block,
        scratch_shapes=[pltpu.SemaphoreType.DMA((4,))],
        vmem=51,
    )


def rounded(values):
    return values.astype(BF16).astype(F32)


def final_kernel(log_cols, got_ref, wide_ref, data_ref, out_ref, pot_ref, weights, held, terms, sems):
    ny, nx, cols, width = data_ref.shape
    rows = wide_ref.shape[0]
    copies = [pltpu.make_async_copy(data_ref.at[y], held.at[y], sems.at[y]) for y in range(ny)]
    for copy in copies:
        copy.start()
    pot = -(log_cols + joined(got_ref[...]))
    pot_ref[...] = pot
    top = row_top(wide_ref, pot)
    total = None
    for k in range(pot.shape[0]):
        part = jnp.exp(wide_ref[:, lanes(k)] + pot[k : k + 1] - top)
        weights[:, lanes(k)] = part.astype(BF16)
        total = part if total is None else total + part
    total = jnp.sum(total, axis=1, keepdims=True)
    inverse = 1.0 / total
    local = as_rows(top + jnp.log(total))[:16]
    first = rounded(local)
    second = rounded(local - first)
    third = local - first - second
    place = lax.broadcasted_iota(jnp.int32, local.shape, 0)
    extra = jnp.where(place == 0, first, jnp.where(place == 1, second, third))
    extra = jnp.where(place < 3, extra, 0.0).astype(BF16)
    half = ny // 2
    for copy in copies[:half]:
        copy.wait()
    for x in range(nx):
        right = jnp.concatenate([held[y, x] for y in range(half)], axis=0)
        terms[x] = jnp.dot(weights[:, : half * cols], right, preferred_element_type=F32)
    for copy in copies[half:]:
        copy.wait()
    for x in range(nx):
        right = jnp.concatenate([held[y, x] for y in range(half, ny)], axis=0)
        term = terms[x] + jnp.dot(weights[:, half * cols :], right, preferred_element_type=F32)
        out_ref[x, :rows, :] = (term * inverse).astype(BF16)
        out_ref[x, rows:, :] = extra


def final_terms(got, wide, data, log_cols):
    ny, nx, cols, width = data.shape
    rows = wide.shape[0]
    return call(
        functools.partial(final_kernel, log_cols),
        "final_terms",
        (shape((nx, rows + 16, width), BF16), shape(got.shape[1:])),
        [VMEM, VMEM, HBM],
        (VMEM, VMEM),
        got,
        wide,
        data,
        scratch_shapes=[
            pltpu.VMEM(wide.shape, BF16),
            pltpu.VMEM(data.shape, BF16),
            pltpu.VMEM((nx, rows, width), F32),
            pltpu.SemaphoreType.DMA((ny,)),
        ],
        vmem=50,
    )


def combine_kernel(log_rows, features, got_ref, began_ref, out_ref, pot_ref):
    nx, rows = got_ref.shape[0], out_ref.shape[0]
    chunks = rows // LANES
    locals_ = [jnp.sum(got_ref[x, rows:, :].astype(F32), axis=0, keepdims=True) for x in range(nx)]
    top = functools.reduce(jnp.maximum, locals_)
    whole = top + jnp.log(functools.reduce(jnp.add, [jnp.exp(v - top) for v in locals_]))
    noise_sq = jnp.sum(began_ref[:, chunks:, :], axis=0)
    for k in range(chunks):
        pot_ref[k : k + 1, :] = noise_sq[k : k + 1] * (1.0 / features) - EPSILON * (log_rows + whole[:, lanes(k)])
    scales = [as_column(jnp.exp(v - whole)) for v in locals_]
    for k in range(out_ref.shape[1] // LANES):
        parts = [scales[x] * got_ref[x, :rows, lanes(k)].astype(F32) for x in range(nx)]
        out_ref[:, lanes(k)] = functools.reduce(jnp.add, parts).astype(BF16)


def shards(noise, data):
    rows, width = noise.shape
    cols, features = data.shape
    nx, ny, nrow, ncol = (lax.axis_size(axes) for axes in ("x", "y", ROW, COL))
    log_rows, log_cols = _log(rows * nrow), _log(cols * ncol)
    chunks = rows // LANES

    low = rows - FIRST_ROWS
    share = cols // nrow
    by_x, by_y, noise_sq = call(
        functools.partial(prepare_kernel, FIRST_ROWS),
        "prepare",
        (
            shape((nx, FIRST_ROWS, width), BF16),
            shape((ny, low + nx * share, width), BF16),
            shape((chunks, LANES)),
        ),
        [VMEM, HBM],
        (VMEM, VMEM, VMEM),
        noise,
        data,
        scratch_shapes=[pltpu.VMEM((share, features), BF16), pltpu.SemaphoreType.DMA],
        vmem=52,
    )
    part = lax.all_to_all(by_x, "x", 0, 0)
    first = lax.all_gather(part, "y")
    part, by_y = lax.optimization_barrier((part, by_y))
    got = lax.all_to_all(by_y, "y", 0, 0)
    second = jnp.broadcast_to(got[None, :, :low], (nx, ny, low, width))
    second = lax.all_to_all(second, "x", 0, 0)
    piece = got[:, low:].reshape(ny, nx, share, width)

    data_sq = jnp.sum(jnp.square(data.astype(F32)), axis=1)
    col_pot = (data_sq * (-1.0 / (features * EPSILON))).reshape(-1, LANES)
    scale = 2.0 / (features * EPSILON)
    scaled, copied, sent = call(
        functools.partial(inner_kernel, scale),
        "inner",
        (shape((rows, cols)), shape((rows, cols)), shape((ncol, 2 * chunks, LANES))),
        [HBM, VMEM, HBM, VMEM, VMEM],
        (VMEM, HBM, VMEM),
        first,
        second,
        data,
        col_pot,
        noise_sq,
        scratch_shapes=[
            pltpu.VMEM(first.shape, BF16),
            pltpu.VMEM(data.shape, BF16),
            pltpu.SemaphoreType.DMA((nx,)),
            pltpu.SemaphoreType.DMA((nx + 1,)),
        ],
        vmem=51,
    )
    wide = lax.all_gather(copied, "y", axis=1, tiled=True)

    began = None
    for step in range(ITERS):
        got = lax.all_to_all(sent, "x" if step > WIDE_FROM else COL, 0, 0)
        if step == 0:
            began, piece = lax.optimization_barrier((got, piece))
            mine = lax.all_gather(piece, ROW, axis=2, tiled=True)
        if step == WIDE_FROM:
            sent, wide = first_wide(got, wide, nrow, log_rows)
        else:
            sent = half_cols(got, wide if step > WIDE_FROM else scaled, nrow, log_rows)
        got = lax.all_to_all(sent, ROW, 0, 0)
        if step < WIDE_FROM:
            sent = half_rows(got, scaled, ncol, log_cols)
        elif step < ITERS - 1:
            sent = half_rows(got, wide, nx, log_cols)
    terms, col_pot = final_terms(got, wide, mine, log_cols)
    own = lax.dynamic_slice_in_dim(col_pot, lax.axis_index("y") * (cols // LANES), cols // LANES, 0)
    data_potential = data_sq / features + EPSILON * own.reshape(cols)
    got = lax.all_to_all(terms, "x", 0, 0)
    targets, noise_potential = call(
        functools.partial(combine_kernel, log_rows, features),
        "combine",
        (shape((rows, width), BF16), shape((chunks, LANES))),
        [VMEM, VMEM],
        (VMEM, VMEM),
        got,
        began,
    )
    return (noise_potential.reshape(rows), data_potential, targets)


def _log(count):
    return float(np.log(np.float32(count)))


def solution(mesh):
    devices = mesh.devices.reshape(8, 2, 4, 8)
    return jax.shard_map(
        shards,
        mesh=Mesh(devices, ("z", "core", "x", "y")),
        in_specs=(P(ROW, COL), P(COL, None)),
        out_specs=(P(ROW), P(COL), P(ROW, COL)),
        check_vma=False,
    )
```

```python
import functools

import jax
import jax.numpy as jnp
import numpy as np
from jax import lax
from jax.experimental import pallas as pl
from jax.experimental.pallas import tpu as pltpu
from jax.sharding import Mesh, PartitionSpec as P

ITERS = 4
EPSILON = 0.01
ROW = ("z", "core")
COL = ("x", "y")
LANES = 128
FIRST_ROWS = 160
WIDE_FROM = 1
VMEM = pl.BlockSpec(memory_space=pltpu.VMEM)
HBM = pl.BlockSpec(memory_space=pltpu.HBM)
MIB = 2**20
F32, BF16 = jnp.float32, jnp.bfloat16


def call(kernel, name, out_shape, in_specs, out_specs, *args, scratch_shapes=(), vmem=40):
    return pl.pallas_call(
        kernel,
        out_shape=out_shape,
        in_specs=in_specs,
        out_specs=out_specs,
        scratch_shapes=scratch_shapes,
        compiler_params=pltpu.CompilerParams(vmem_limit_bytes=vmem * MIB),
        name=name,
    )(*args)


def shape(dims, dtype=F32):
    return jax.ShapeDtypeStruct(dims, dtype)


def lanes(k):
    return slice(k * LANES, (k + 1) * LANES)


def as_column(values):
    return jnp.broadcast_to(values, (LANES, values.shape[1])).T


def as_rows(column):
    return jnp.broadcast_to(column, (column.shape[0], LANES)).T


def joined(got):
    top = jnp.max(got, axis=0)
    return top + jnp.log(jnp.sum(jnp.exp(got - top[None]), axis=0))


def prepare_kernel(high, noise_ref, data_ref, by_y_ref, sq_ref, held, sem):
    ny, sent, width = by_y_ref.shape
    rows = noise_ref.shape[0]
    low = rows - high
    nx = data_ref.shape[1] // (ny * width)
    share = (sent - low) // nx
    at = (lax.axis_index(ROW[0]) * lax.axis_size(ROW[1]) + lax.axis_index(ROW[1])) * share
    copy = pltpu.make_async_copy(data_ref.at[pl.ds(pl.multiple_of(at, share), share), :], held, sem)
    copy.start()
    for y in range(ny):
        by_y_ref[y, :low] = noise_ref[high:]
    squares = jnp.square(noise_ref[...].astype(F32))
    squares = as_rows(jnp.sum(squares, axis=1, keepdims=True))[:1]
    for k in range(rows // LANES):
        sq_ref[k : k + 1, :] = squares[:, lanes(k)]
    copy.wait()
    for y in range(ny):
        for x in range(nx):
            block = held[:, (x * ny + y) * width : (x * ny + y + 1) * width]
            by_y_ref[y, low + x * share : low + (x + 1) * share] = block


def inner_kernel(
    scale,
    first_ref,
    second_ref,
    data_ref,
    pot_ref,
    sq_ref,
    got_ref,
    out_ref,
    copy_ref,
    send_ref,
    piece_ref,
    rows_held,
    held,
    row_sems,
    sems,
):
    ny, nx, _, width = first_ref.shape
    apart = pltpu.make_async_copy(got_ref.at[:, second_ref.shape[2] :], piece_ref, row_sems.at[nx])
    apart.start()
    wide = ny * width
    copies = [
        (
            pltpu.make_async_copy(
                data_ref.at[:, x * wide : (x + 1) * wide], held.at[:, x * wide : (x + 1) * wide], sems.at[x]
            ),
            pltpu.make_async_copy(first_ref.at[:, x], rows_held.at[:, x], row_sems.at[x]),
        )
        for x in range(nx)
    ]
    for pair in copies:
        for copy in pair:
            copy.start()
    total = None
    for x in range(nx):
        for copy in copies[x]:
            copy.wait()
        for y in range(ny):
            left = jnp.concatenate([rows_held[y, x], second_ref[x, y]], axis=0)
            at = x * wide + y * width
            one = lax.dot_general(
                left, held[:, at : at + width], (((1,), (1,)), ((), ())), preferred_element_type=F32
            )
            total = one if total is None else total + one
    out_ref[...] = total * scale
    out = pltpu.make_async_copy(out_ref, copy_ref, sems.at[nx])
    out.start()
    local = local_rows(out_ref, pot_ref[...])
    chunks = local.shape[1] // LANES
    members = send_ref.shape[0]
    for k in range(chunks):
        send_ref[:, k, :] = jnp.broadcast_to(local[:, lanes(k)], (members, LANES))
        send_ref[:, chunks + k, :] = jnp.broadcast_to(sq_ref[k : k + 1], (members, LANES))
    out.wait()
    apart.wait()


def row_top(block_ref, pot):
    top = None
    for k in range(pot.shape[0]):
        scores = block_ref[:, lanes(k)] + pot[k : k + 1]
        top = scores if top is None else jnp.maximum(top, scores)
    return jnp.max(top, axis=1, keepdims=True)


def local_rows(block_ref, pot):
    top = row_top(block_ref, pot)
    total = None
    for k in range(pot.shape[0]):
        part = jnp.exp(block_ref[:, lanes(k)] + pot[k : k + 1] - top)
        total = part if total is None else total + part
    return as_rows(top + jnp.log(jnp.sum(total, axis=1, keepdims=True)))[:1]


def rows_kernel(log_cols, got_ref, block_ref, out_ref):
    local = local_rows(block_ref, -(log_cols + joined(got_ref[...])))
    for k in range(out_ref.shape[1]):
        out_ref[:, k, :] = jnp.broadcast_to(local[:, lanes(k)], (out_ref.shape[0], LANES))


def half_rows(got, block, members, log_cols):
    out = shape((members, block.shape[0] // LANES, LANES))
    return call(functools.partial(rows_kernel, log_cols), "half_rows", out, [VMEM, VMEM], VMEM, got, block)


def column_pot(got_ref, chunks, log_rows):
    pot = -(log_rows + joined(got_ref[:, :chunks, :]))
    return jnp.concatenate([as_column(pot[k : k + 1]) for k in range(chunks)], axis=0)


def send_cols(block_ref, pot, out_ref, places):
    for k in places:
        scores = block_ref[:, lanes(k)] + pot
        top = jnp.max(scores, axis=0, keepdims=True)
        local = top + jnp.log(jnp.sum(jnp.exp(scores - top), axis=0, keepdims=True))
        out_ref[:, k, :] = jnp.broadcast_to(local, (out_ref.shape[0], LANES))


def cols_kernel(log_rows, got_ref, block_ref, out_ref):
    pot = column_pot(got_ref, block_ref.shape[0] // LANES, log_rows)
    send_cols(block_ref, pot, out_ref, range(out_ref.shape[1]))


def half_cols(got, block, members, log_rows):
    out = shape((members, block.shape[1] // LANES, LANES))
    return call(functools.partial(cols_kernel, log_rows), "half_cols", out, [VMEM, VMEM], VMEM, got, block)


def first_wide_kernel(log_rows, got_ref, block_ref, out_ref, held_ref, sems):
    parts = sems.shape[0]
    places = out_ref.shape[1] // parts
    width = places * LANES
    copies = [
        pltpu.make_async_copy(
            block_ref.at[:, k * width : (k + 1) * width], held_ref.at[:, k * width : (k + 1) * width], sems.at[k]
        )
        for k in range(parts)
    ]
    for copy in copies:
        copy.start()
    pot = column_pot(got_ref, block_ref.shape[0] // LANES, log_rows)
    for k in range(parts):
        copies[k].wait()
        send_cols(held_ref, pot, out_ref, range(k * places, (k + 1) * places))


def first_wide(got, block, members, log_rows):
    return call(
        functools.partial(first_wide_kernel, log_rows),
        "first_wide",
        (shape((members, block.shape[1] // LANES, LANES)), shape(block.shape)),
        [VMEM, HBM],
        (VMEM, VMEM),
        got,
        block,
        scratch_shapes=[pltpu.SemaphoreType.DMA((4,))],
        vmem=51,
    )


def rounded(values):
    return values.astype(BF16).astype(F32)


def final_kernel(log_cols, got_ref, wide_ref, data_ref, out_ref, pot_ref, weights, held, terms, sems):
    ny, nx, cols, width = data_ref.shape
    rows = wide_ref.shape[0]
    copies = [pltpu.make_async_copy(data_ref.at[y], held.at[y], sems.at[y]) for y in range(ny)]
    for copy in copies:
        copy.start()
    pot = -(log_cols + joined(got_ref[...]))
    pot_ref[...] = pot
    top = row_top(wide_ref, pot)
    total = None
    for k in range(pot.shape[0]):
        part = jnp.exp(wide_ref[:, lanes(k)] + pot[k : k + 1] - top)
        weights[:, lanes(k)] = part.astype(BF16)
        total = part if total is None else total + part
    total = jnp.sum(total, axis=1, keepdims=True)
    inverse = 1.0 / total
    local = as_rows(top + jnp.log(total))[:16]
    first = rounded(local)
    second = rounded(local - first)
    third = local - first - second
    place = lax.broadcasted_iota(jnp.int32, local.shape, 0)
    extra = jnp.where(place == 0, first, jnp.where(place == 1, second, third))
    extra = jnp.where(place < 3, extra, 0.0).astype(BF16)
    half = ny // 2
    for copy in copies[:half]:
        copy.wait()
    for x in range(nx):
        right = jnp.concatenate([held[y, x] for y in range(half)], axis=0)
        terms[x] = jnp.dot(weights[:, : half * cols], right, preferred_element_type=F32)
    for copy in copies[half:]:
        copy.wait()
    for x in range(nx):
        right = jnp.concatenate([held[y, x] for y in range(half, ny)], axis=0)
        term = terms[x] + jnp.dot(weights[:, half * cols :], right, preferred_element_type=F32)
        out_ref[x, :rows, :] = (term * inverse).astype(BF16)
        out_ref[x, rows:, :] = extra


def final_terms(got, wide, data, log_cols):
    ny, nx, cols, width = data.shape
    rows = wide.shape[0]
    return call(
        functools.partial(final_kernel, log_cols),
        "final_terms",
        (shape((nx, rows + 16, width), BF16), shape(got.shape[1:])),
        [VMEM, VMEM, HBM],
        (VMEM, VMEM),
        got,
        wide,
        data,
        scratch_shapes=[
            pltpu.VMEM(wide.shape, BF16),
            pltpu.VMEM(data.shape, BF16),
            pltpu.VMEM((nx, rows, width), F32),
            pltpu.SemaphoreType.DMA((ny,)),
        ],
        vmem=50,
    )


def combine_kernel(log_rows, features, got_ref, began_ref, out_ref, pot_ref):
    nx, rows = got_ref.shape[0], out_ref.shape[0]
    chunks = rows // LANES
    locals_ = [jnp.sum(got_ref[x, rows:, :].astype(F32), axis=0, keepdims=True) for x in range(nx)]
    top = functools.reduce(jnp.maximum, locals_)
    whole = top + jnp.log(functools.reduce(jnp.add, [jnp.exp(v - top) for v in locals_]))
    noise_sq = jnp.sum(began_ref[:, chunks:, :], axis=0)
    for k in range(chunks):
        pot_ref[k : k + 1, :] = noise_sq[k : k + 1] * (1.0 / features) - EPSILON * (log_rows + whole[:, lanes(k)])
    scales = [as_column(jnp.exp(v - whole)) for v in locals_]
    for k in range(out_ref.shape[1] // LANES):
        parts = [scales[x] * got_ref[x, :rows, lanes(k)].astype(F32) for x in range(nx)]
        out_ref[:, lanes(k)] = functools.reduce(jnp.add, parts).astype(BF16)


def shards(noise, data):
    rows, width = noise.shape
    cols, features = data.shape
    nx, ny, nrow, ncol = (lax.axis_size(axes) for axes in ("x", "y", ROW, COL))
    log_rows, log_cols = _log(rows * nrow), _log(cols * ncol)
    chunks = rows // LANES

    low = rows - FIRST_ROWS
    share = cols // nrow
    part = lax.all_to_all(jnp.broadcast_to(noise[None, :FIRST_ROWS], (nx, FIRST_ROWS, width)), "x", 0, 0)
    first = lax.all_gather(part, "y")
    part, noise = lax.optimization_barrier((part, noise))
    by_y, noise_sq = call(
        functools.partial(prepare_kernel, FIRST_ROWS),
        "prepare",
        (shape((ny, low + nx * share, width), BF16), shape((chunks, LANES))),
        [VMEM, HBM],
        (VMEM, VMEM),
        noise,
        data,
        scratch_shapes=[pltpu.VMEM((share, features), BF16), pltpu.SemaphoreType.DMA],
        vmem=52,
    )
    got = lax.all_to_all(by_y, "y", 0, 0)
    second = jnp.broadcast_to(got[None, :, :low], (nx, ny, low, width))
    second = lax.all_to_all(second, "x", 0, 0)

    data_sq = jnp.sum(jnp.square(data.astype(F32)), axis=1)
    col_pot = (data_sq * (-1.0 / (features * EPSILON))).reshape(-1, LANES)
    scale = 2.0 / (features * EPSILON)
    scaled, copied, sent, piece = call(
        functools.partial(inner_kernel, scale),
        "inner",
        (
            shape((rows, cols)),
            shape((rows, cols)),
            shape((ncol, 2 * chunks, LANES)),
            shape((ny, nx * share, width), BF16),
        ),
        [HBM, VMEM, HBM, VMEM, VMEM, HBM],
        (VMEM, HBM, VMEM, HBM),
        first,
        second,
        data,
        col_pot,
        noise_sq,
        got,
        scratch_shapes=[
            pltpu.VMEM(first.shape, BF16),
            pltpu.VMEM(data.shape, BF16),
            pltpu.SemaphoreType.DMA((nx + 1,)),
            pltpu.SemaphoreType.DMA((nx + 1,)),
        ],
        vmem=50,
    )
    wide = lax.all_gather(copied, "y", axis=1, tiled=True)

    began = None
    for step in range(ITERS):
        got = lax.all_to_all(sent, "x" if step > WIDE_FROM else COL, 0, 0)
        if step == 0:
            began, piece = lax.optimization_barrier((got, piece))
            mine = lax.all_gather(piece.reshape(ny, nx, share, width), ROW, axis=2, tiled=True)
        if step == WIDE_FROM:
            sent, wide = first_wide(got, wide, nrow, log_rows)
        else:
            sent = half_cols(got, wide if step > WIDE_FROM else scaled, nrow, log_rows)
        got = lax.all_to_all(sent, ROW, 0, 0)
        if step < WIDE_FROM:
            sent = half_rows(got, scaled, ncol, log_cols)
        elif step < ITERS - 1:
            sent = half_rows(got, wide, nx, log_cols)
    terms, col_pot = final_terms(got, wide, mine, log_cols)
    own = lax.dynamic_slice_in_dim(col_pot, lax.axis_index("y") * (cols // LANES), cols // LANES, 0)
    data_potential = data_sq / features + EPSILON * own.reshape(cols)
    got = lax.all_to_all(terms, "x", 0, 0)
    targets, noise_potential = call(
        functools.partial(combine_kernel, log_rows, features),
        "combine",
        (shape((rows, width), BF16), shape((chunks, LANES))),
        [VMEM, VMEM],
        (VMEM, VMEM),
        got,
        began,
    )
    return (noise_potential.reshape(rows), data_potential, targets)


def _log(count):
    return float(np.log(np.float32(count)))


def solution(mesh):
    devices = mesh.devices.reshape(8, 2, 4, 8)
    return jax.shard_map(
        shards,
        mesh=Mesh(devices, ("z", "core", "x", "y")),
        in_specs=(P(ROW, COL), P(COL, None)),
        out_specs=(P(ROW), P(COL), P(ROW, COL)),
        check_vma=False,
    )
```

```python
import functools

import jax
import jax.numpy as jnp
import numpy as np
from jax import lax
from jax.experimental import pallas as pl
from jax.experimental.pallas import tpu as pltpu
from jax.sharding import Mesh, PartitionSpec as P

ITERS = 4
EPSILON = 0.01
ROW = ("z", "core")
COL = ("x", "y")
LANES = 128
FIRST_ROWS = 160
WIDE_FROM = 1
VMEM = pl.BlockSpec(memory_space=pltpu.VMEM)
HBM = pl.BlockSpec(memory_space=pltpu.HBM)
MIB = 2**20
F32, BF16 = jnp.float32, jnp.bfloat16


def call(kernel, name, out_shape, in_specs, out_specs, *args, scratch_shapes=(), vmem=40):
    return pl.pallas_call(
        kernel,
        out_shape=out_shape,
        in_specs=in_specs,
        out_specs=out_specs,
        scratch_shapes=scratch_shapes,
        compiler_params=pltpu.CompilerParams(vmem_limit_bytes=vmem * MIB),
        name=name,
    )(*args)


def shape(dims, dtype=F32):
    return jax.ShapeDtypeStruct(dims, dtype)


def lanes(k):
    return slice(k * LANES, (k + 1) * LANES)


def as_column(values):
    return jnp.broadcast_to(values, (LANES, values.shape[1])).T


def as_rows(column):
    return jnp.broadcast_to(column, (column.shape[0], LANES)).T


def joined(got):
    top = jnp.max(got, axis=0)
    return top + jnp.log(jnp.sum(jnp.exp(got - top[None]), axis=0))


def prepare_kernel(high, noise_ref, data_ref, by_y_ref, sq_ref, held, sem):
    ny, sent, width = by_y_ref.shape
    rows = noise_ref.shape[0]
    low = rows - high
    nx = data_ref.shape[1] // (ny * width)
    share = (sent - low) // nx
    at = (lax.axis_index(ROW[0]) * lax.axis_size(ROW[1]) + lax.axis_index(ROW[1])) * share
    copy = pltpu.make_async_copy(data_ref.at[pl.ds(pl.multiple_of(at, share), share), :], held, sem)
    copy.start()
    for y in range(ny):
        by_y_ref[y, :low] = noise_ref[high:]
    squares = jnp.square(noise_ref[...].astype(F32))
    squares = as_rows(jnp.sum(squares, axis=1, keepdims=True))[:1]
    for k in range(rows // LANES):
        sq_ref[k : k + 1, :] = squares[:, lanes(k)]
    copy.wait()
    for y in range(ny):
        for x in range(nx):
            block = held[:, (x * ny + y) * width : (x * ny + y + 1) * width]
            by_y_ref[y, low + x * share : low + (x + 1) * share] = block


def load_kernel(scale, after_ref, data_ref, out_ref, pot_ref, sems):
    parts = pot_ref.shape[0]
    copies = [pltpu.make_async_copy(data_ref.at[lanes(k)], out_ref.at[lanes(k)], sems.at[k]) for k in range(parts)]
    for copy in copies:
        copy.start()
    for k in range(parts):
        copies[k].wait()
        total = None
        for f in range(out_ref.shape[1] // LANES):
            block = out_ref[lanes(k), lanes(f)].astype(F32)
            total = block * block if total is None else total + block * block
        pot_ref[k : k + 1, :] = as_rows(jnp.sum(total, axis=1, keepdims=True))[:1] * scale


def inner_kernel(
    scale,
    first_ref,
    second_ref,
    data_ref,
    pot_ref,
    sq_ref,
    got_ref,
    out_ref,
    copy_ref,
    send_ref,
    piece_ref,
    sems,
):
    ny, nx, _, width = first_ref.shape
    apart = pltpu.make_async_copy(got_ref.at[:, second_ref.shape[2] :], piece_ref, sems.at[0])
    apart.start()
    wide = ny * width
    total = None
    for x in range(nx):
        for y in range(ny):
            left = jnp.concatenate([first_ref[y, x], second_ref[x, y]], axis=0)
            at = x * wide + y * width
            one = lax.dot_general(
                left, data_ref[:, at : at + width], (((1,), (1,)), ((), ())), preferred_element_type=F32
            )
            total = one if total is None else total + one
    out_ref[...] = total * scale
    out = pltpu.make_async_copy(out_ref, copy_ref, sems.at[1])
    out.start()
    local = local_rows(out_ref, pot_ref[...])
    chunks = local.shape[1] // LANES
    members = send_ref.shape[0]
    for k in range(chunks):
        send_ref[:, k, :] = jnp.broadcast_to(local[:, lanes(k)], (members, LANES))
        send_ref[:, chunks + k, :] = jnp.broadcast_to(sq_ref[k : k + 1], (members, LANES))
    out.wait()
    apart.wait()


def row_top(block_ref, pot):
    top = None
    for k in range(pot.shape[0]):
        scores = block_ref[:, lanes(k)] + pot[k : k + 1]
        top = scores if top is None else jnp.maximum(top, scores)
    return jnp.max(top, axis=1, keepdims=True)


def local_rows(block_ref, pot):
    top = row_top(block_ref, pot)
    total = None
    for k in range(pot.shape[0]):
        part = jnp.exp(block_ref[:, lanes(k)] + pot[k : k + 1] - top)
        total = part if total is None else total + part
    return as_rows(top + jnp.log(jnp.sum(total, axis=1, keepdims=True)))[:1]


def rows_kernel(log_cols, got_ref, block_ref, out_ref):
    local = local_rows(block_ref, -(log_cols + joined(got_ref[...])))
    for k in range(out_ref.shape[1]):
        out_ref[:, k, :] = jnp.broadcast_to(local[:, lanes(k)], (out_ref.shape[0], LANES))


def half_rows(got, block, members, log_cols):
    out = shape((members, block.shape[0] // LANES, LANES))
    return call(functools.partial(rows_kernel, log_cols), "half_rows", out, [VMEM, VMEM], VMEM, got, block)


def column_pot(got_ref, chunks, log_rows):
    pot = -(log_rows + joined(got_ref[:, :chunks, :]))
    return jnp.concatenate([as_column(pot[k : k + 1]) for k in range(chunks)], axis=0)


def send_cols(block_ref, pot, out_ref, places):
    for k in places:
        scores = block_ref[:, lanes(k)] + pot
        top = jnp.max(scores, axis=0, keepdims=True)
        local = top + jnp.log(jnp.sum(jnp.exp(scores - top), axis=0, keepdims=True))
        out_ref[:, k, :] = jnp.broadcast_to(local, (out_ref.shape[0], LANES))


def cols_kernel(log_rows, got_ref, block_ref, out_ref):
    pot = column_pot(got_ref, block_ref.shape[0] // LANES, log_rows)
    send_cols(block_ref, pot, out_ref, range(out_ref.shape[1]))


def half_cols(got, block, members, log_rows):
    out = shape((members, block.shape[1] // LANES, LANES))
    return call(functools.partial(cols_kernel, log_rows), "half_cols", out, [VMEM, VMEM], VMEM, got, block)


def first_wide_kernel(log_rows, got_ref, block_ref, out_ref, held_ref, sems):
    parts = sems.shape[0]
    places = out_ref.shape[1] // parts
    width = places * LANES
    copies = [
        pltpu.make_async_copy(
            block_ref.at[:, k * width : (k + 1) * width], held_ref.at[:, k * width : (k + 1) * width], sems.at[k]
        )
        for k in range(parts)
    ]
    for copy in copies:
        copy.start()
    pot = column_pot(got_ref, block_ref.shape[0] // LANES, log_rows)
    for k in range(parts):
        copies[k].wait()
        send_cols(held_ref, pot, out_ref, range(k * places, (k + 1) * places))


def first_wide(got, block, members, log_rows):
    return call(
        functools.partial(first_wide_kernel, log_rows),
        "first_wide",
        (shape((members, block.shape[1] // LANES, LANES)), shape(block.shape)),
        [VMEM, HBM],
        (VMEM, VMEM),
        got,
        block,
        scratch_shapes=[pltpu.SemaphoreType.DMA((4,))],
        vmem=51,
    )


def rounded(values):
    return values.astype(BF16).astype(F32)


def final_kernel(log_cols, got_ref, wide_ref, data_ref, out_ref, pot_ref, weights, held, terms, sems):
    ny, nx, cols, width = data_ref.shape
    rows = wide_ref.shape[0]
    copies = [pltpu.make_async_copy(data_ref.at[y], held.at[y], sems.at[y]) for y in range(ny)]
    for copy in copies:
        copy.start()
    pot = -(log_cols + joined(got_ref[...]))
    pot_ref[...] = pot
    top = row_top(wide_ref, pot)
    total = None
    for k in range(pot.shape[0]):
        part = jnp.exp(wide_ref[:, lanes(k)] + pot[k : k + 1] - top)
        weights[:, lanes(k)] = part.astype(BF16)
        total = part if total is None else total + part
    total = jnp.sum(total, axis=1, keepdims=True)
    inverse = 1.0 / total
    local = as_rows(top + jnp.log(total))[:16]
    first = rounded(local)
    second = rounded(local - first)
    third = local - first - second
    place = lax.broadcasted_iota(jnp.int32, local.shape, 0)
    extra = jnp.where(place == 0, first, jnp.where(place == 1, second, third))
    extra = jnp.where(place < 3, extra, 0.0).astype(BF16)
    half = ny // 2
    for copy in copies[:half]:
        copy.wait()
    for x in range(nx):
        right = jnp.concatenate([held[y, x] for y in range(half)], axis=0)
        terms[x] = jnp.dot(weights[:, : half * cols], right, preferred_element_type=F32)
    for copy in copies[half:]:
        copy.wait()
    for x in range(nx):
        right = jnp.concatenate([held[y, x] for y in range(half, ny)], axis=0)
        term = terms[x] + jnp.dot(weights[:, half * cols :], right, preferred_element_type=F32)
        out_ref[x, :rows, :] = (term * inverse).astype(BF16)
        out_ref[x, rows:, :] = extra


def final_terms(got, wide, data, log_cols):
    ny, nx, cols, width = data.shape
    rows = wide.shape[0]
    return call(
        functools.partial(final_kernel, log_cols),
        "final_terms",
        (shape((nx, rows + 16, width), BF16), shape(got.shape[1:])),
        [VMEM, VMEM, HBM],
        (VMEM, VMEM),
        got,
        wide,
        data,
        scratch_shapes=[
            pltpu.VMEM(wide.shape, BF16),
            pltpu.VMEM(data.shape, BF16),
            pltpu.VMEM((nx, rows, width), F32),
            pltpu.SemaphoreType.DMA((ny,)),
        ],
        vmem=50,
    )


def combine_kernel(log_rows, features, got_ref, began_ref, begin_ref, col_ref, out_ref, pot_ref, col_pot_ref):
    nx, rows = got_ref.shape[0], out_ref.shape[0]
    chunks = rows // LANES
    locals_ = [jnp.sum(got_ref[x, rows:, :].astype(F32), axis=0, keepdims=True) for x in range(nx)]
    top = functools.reduce(jnp.maximum, locals_)
    whole = top + jnp.log(functools.reduce(jnp.add, [jnp.exp(v - top) for v in locals_]))
    parts = col_pot_ref.shape[0]
    mine = lax.axis_index("y")
    own = jnp.zeros(col_pot_ref.shape, F32)
    for y in range(col_ref.shape[0] // parts):
        own = jnp.where(mine == y, col_ref[y * parts : (y + 1) * parts, :], own)
    col_pot_ref[...] = EPSILON * (own - begin_ref[...])
    noise_sq = jnp.sum(began_ref[:, chunks:, :], axis=0)
    for k in range(chunks):
        pot_ref[k : k + 1, :] = noise_sq[k : k + 1] * (1.0 / features) - EPSILON * (log_rows + whole[:, lanes(k)])
    scales = [as_column(jnp.exp(v - whole)) for v in locals_]
    for k in range(out_ref.shape[1] // LANES):
        parts = [scales[x] * got_ref[x, :rows, lanes(k)].astype(F32) for x in range(nx)]
        out_ref[:, lanes(k)] = functools.reduce(jnp.add, parts).astype(BF16)


def shards(noise, data):
    rows, width = noise.shape
    cols, features = data.shape
    nx, ny, nrow, ncol = (lax.axis_size(axes) for axes in ("x", "y", ROW, COL))
    log_rows, log_cols = _log(rows * nrow), _log(cols * ncol)
    chunks = rows // LANES

    low = rows - FIRST_ROWS
    share = cols // nrow
    part = lax.all_to_all(jnp.broadcast_to(noise[None, :FIRST_ROWS], (nx, FIRST_ROWS, width)), "x", 0, 0)
    first = lax.all_gather(part, "y")
    part, noise = lax.optimization_barrier((part, noise))
    by_y, noise_sq = call(
        functools.partial(prepare_kernel, FIRST_ROWS),
        "prepare",
        (shape((ny, low + nx * share, width), BF16), shape((chunks, LANES))),
        [VMEM, HBM],
        (VMEM, VMEM),
        noise,
        data,
        scratch_shapes=[pltpu.VMEM((share, features), BF16), pltpu.SemaphoreType.DMA],
        vmem=52,
    )
    got = lax.all_to_all(by_y, "y", 0, 0)
    second = jnp.broadcast_to(got[None, :, :low], (nx, ny, low, width))
    second = lax.all_to_all(second, "x", 0, 0)

    held, col_pot = call(
        functools.partial(load_kernel, -1.0 / (features * EPSILON)),
        "load",
        (shape(data.shape, BF16), shape((cols // LANES, LANES))),
        [HBM, HBM],
        (VMEM, VMEM),
        got,
        data,
        scratch_shapes=[pltpu.SemaphoreType.DMA((cols // LANES,))],
        vmem=46,
    )
    begin_pot = col_pot
    scale = 2.0 / (features * EPSILON)
    scaled, copied, sent, piece = call(
        functools.partial(inner_kernel, scale),
        "inner",
        (
            shape((rows, cols)),
            shape((rows, cols)),
            shape((ncol, 2 * chunks, LANES)),
            shape((ny, nx * share, width), BF16),
        ),
        [VMEM, VMEM, VMEM, VMEM, VMEM, HBM],
        (VMEM, HBM, VMEM, HBM),
        first,
        second,
        held,
        begin_pot,
        noise_sq,
        got,
        scratch_shapes=[pltpu.SemaphoreType.DMA((2,))],
    )
    wide = lax.all_gather(copied, "y", axis=1, tiled=True)

    began = None
    for step in range(ITERS):
        got = lax.all_to_all(sent, "x" if step > WIDE_FROM else COL, 0, 0)
        if step == 0:
            began, piece = lax.optimization_barrier((got, piece))
            mine = lax.all_gather(piece.reshape(ny, nx, share, width), ROW, axis=2, tiled=True)
        if step == WIDE_FROM:
            sent, wide = first_wide(got, wide, nrow, log_rows)
        else:
            sent = half_cols(got, wide if step > WIDE_FROM else scaled, nrow, log_rows)
        got = lax.all_to_all(sent, ROW, 0, 0)
        if step < WIDE_FROM:
            sent = half_rows(got, scaled, ncol, log_cols)
        elif step < ITERS - 1:
            sent = half_rows(got, wide, nx, log_cols)
    terms, col_pot = final_terms(got, wide, mine, log_cols)
    got = lax.all_to_all(terms, "x", 0, 0)
    targets, noise_potential, data_potential = call(
        functools.partial(combine_kernel, log_rows, features),
        "combine",
        (shape((rows, width), BF16), shape((chunks, LANES)), shape(begin_pot.shape)),
        [VMEM] * 4,
        (VMEM, VMEM, VMEM),
        got,
        began,
        begin_pot,
        col_pot,
    )
    return (noise_potential.reshape(rows), data_potential.reshape(cols), targets)


def _log(count):
    return float(np.log(np.float32(count)))


def solution(mesh):
    devices = mesh.devices.reshape(8, 2, 4, 8)
    return jax.shard_map(
        shards,
        mesh=Mesh(devices, ("z", "core", "x", "y")),
        in_specs=(P(ROW, COL), P(COL, None)),
        out_specs=(P(ROW), P(COL), P(ROW, COL)),
        check_vma=False,
    )
```

```python
import functools

import jax
import jax.numpy as jnp
import numpy as np
from jax import lax
from jax.experimental import pallas as pl
from jax.experimental.pallas import tpu as pltpu
from jax.sharding import Mesh, PartitionSpec as P

ITERS = 4
EPSILON = 0.01
ROW = ("z", "core")
COL = ("x", "y")
LANES = 128
FIRST_ROWS = 160
WIDE_FROM = 1
VMEM = pl.BlockSpec(memory_space=pltpu.VMEM)
HBM = pl.BlockSpec(memory_space=pltpu.HBM)
MIB = 2**20
F32, BF16 = jnp.float32, jnp.bfloat16


def call(kernel, name, out_shape, in_specs, out_specs, *args, scratch_shapes=(), vmem=40):
    return pl.pallas_call(
        kernel,
        out_shape=out_shape,
        in_specs=in_specs,
        out_specs=out_specs,
        scratch_shapes=scratch_shapes,
        compiler_params=pltpu.CompilerParams(vmem_limit_bytes=vmem * MIB),
        name=name,
    )(*args)


def shape(dims, dtype=F32):
    return jax.ShapeDtypeStruct(dims, dtype)


def lanes(k):
    return slice(k * LANES, (k + 1) * LANES)


def as_column(values):
    return jnp.broadcast_to(values, (LANES, values.shape[1])).T


def as_rows(column):
    return jnp.broadcast_to(column, (column.shape[0], LANES)).T


def joined(got):
    top = jnp.max(got, axis=0)
    return top + jnp.log(jnp.sum(jnp.exp(got - top[None]), axis=0))


def prepare_kernel(high, noise_ref, data_ref, by_x_ref, by_y_ref, sq_ref, held, sem):
    nx = by_x_ref.shape[0]
    ny, sent, width = by_y_ref.shape
    rows = noise_ref.shape[0]
    low = rows - high
    share = (sent - low) // nx
    at = (lax.axis_index(ROW[0]) * lax.axis_size(ROW[1]) + lax.axis_index(ROW[1])) * share
    copy = pltpu.make_async_copy(data_ref.at[pl.ds(pl.multiple_of(at, share), share), :], held, sem)
    copy.start()
    for x in range(nx):
        by_x_ref[x] = noise_ref[:high]
    for y in range(ny):
        by_y_ref[y, :low] = noise_ref[high:]
    squares = jnp.square(noise_ref[...].astype(F32))
    squares = as_rows(jnp.sum(squares, axis=1, keepdims=True))[:1]
    for k in range(rows // LANES):
        sq_ref[k : k + 1, :] = squares[:, lanes(k)]
    copy.wait()
    for y in range(ny):
        for x in range(nx):
            block = held[:, (x * ny + y) * width : (x * ny + y + 1) * width]
            by_y_ref[y, low + x * share : low + (x + 1) * share] = block


def inner_kernel(
    scale,
    first_ref,
    second_ref,
    data_ref,
    pot_ref,
    sq_ref,
    got_ref,
    out_ref,
    copy_ref,
    send_ref,
    piece_ref,
    rows_held,
    held,
    row_sems,
    sems,
):
    ny, nx, _, width = first_ref.shape
    apart = pltpu.make_async_copy(got_ref.at[:, second_ref.shape[2] :], piece_ref, row_sems.at[nx])
    apart.start()
    wide = ny * width
    copies = [
        (
            pltpu.make_async_copy(
                data_ref.at[:, x * wide : (x + 1) * wide], held.at[:, x * wide : (x + 1) * wide], sems.at[x]
            ),
            pltpu.make_async_copy(first_ref.at[:, x], rows_held.at[:, x], row_sems.at[x]),
        )
        for x in range(nx)
    ]
    for pair in copies:
        for copy in pair:
            copy.start()
    total = None
    for x in range(nx):
        for copy in copies[x]:
            copy.wait()
        for y in range(ny):
            left = jnp.concatenate([rows_held[y, x], second_ref[x, y]], axis=0)
            at = x * wide + y * width
            one = lax.dot_general(
                left, held[:, at : at + width], (((1,), (1,)), ((), ())), preferred_element_type=F32
            )
            total = one if total is None else total + one
    out_ref[...] = total * scale
    out = pltpu.make_async_copy(out_ref, copy_ref, sems.at[nx])
    out.start()
    local = local_rows(out_ref, pot_ref[...])
    chunks = local.shape[1] // LANES
    members = send_ref.shape[0]
    for k in range(chunks):
        send_ref[:, k, :] = jnp.broadcast_to(local[:, lanes(k)], (members, LANES))
        send_ref[:, chunks + k, :] = jnp.broadcast_to(sq_ref[k : k + 1], (members, LANES))
    out.wait()
    apart.wait()


def row_top(block_ref, pot):
    top = None
    for k in range(pot.shape[0]):
        scores = block_ref[:, lanes(k)] + pot[k : k + 1]
        top = scores if top is None else jnp.maximum(top, scores)
    return jnp.max(top, axis=1, keepdims=True)


def local_rows(block_ref, pot):
    top = row_top(block_ref, pot)
    total = None
    for k in range(pot.shape[0]):
        part = jnp.exp(block_ref[:, lanes(k)] + pot[k : k + 1] - top)
        total = part if total is None else total + part
    return as_rows(top + jnp.log(jnp.sum(total, axis=1, keepdims=True)))[:1]


def rows_kernel(log_cols, got_ref, block_ref, out_ref):
    local = local_rows(block_ref, -(log_cols + joined(got_ref[...])))
    for k in range(out_ref.shape[1]):
        out_ref[:, k, :] = jnp.broadcast_to(local[:, lanes(k)], (out_ref.shape[0], LANES))


def half_rows(got, block, members, log_cols):
    out = shape((members, block.shape[0] // LANES, LANES))
    return call(functools.partial(rows_kernel, log_cols), "half_rows", out, [VMEM, VMEM], VMEM, got, block)


def column_pot(got_ref, chunks, log_rows):
    pot = -(log_rows + joined(got_ref[:, :chunks, :]))
    return jnp.concatenate([as_column(pot[k : k + 1]) for k in range(chunks)], axis=0)


def send_cols(block_ref, pot, out_ref, places):
    for k in places:
        scores = block_ref[:, lanes(k)] + pot
        top = jnp.max(scores, axis=0, keepdims=True)
        local = top + jnp.log(jnp.sum(jnp.exp(scores - top), axis=0, keepdims=True))
        out_ref[:, k, :] = jnp.broadcast_to(local, (out_ref.shape[0], LANES))


def cols_kernel(log_rows, got_ref, block_ref, out_ref):
    pot = column_pot(got_ref, block_ref.shape[0] // LANES, log_rows)
    send_cols(block_ref, pot, out_ref, range(out_ref.shape[1]))


def half_cols(got, block, members, log_rows):
    out = shape((members, block.shape[1] // LANES, LANES))
    return call(functools.partial(cols_kernel, log_rows), "half_cols", out, [VMEM, VMEM], VMEM, got, block)


def first_wide_kernel(log_rows, got_ref, block_ref, out_ref, held_ref, sems):
    parts = sems.shape[0]
    places = out_ref.shape[1] // parts
    width = places * LANES
    copies = [
        pltpu.make_async_copy(
            block_ref.at[:, k * width : (k + 1) * width], held_ref.at[:, k * width : (k + 1) * width], sems.at[k]
        )
        for k in range(parts)
    ]
    for copy in copies:
        copy.start()
    pot = column_pot(got_ref, block_ref.shape[0] // LANES, log_rows)
    for k in range(parts):
        copies[k].wait()
        send_cols(held_ref, pot, out_ref, range(k * places, (k + 1) * places))


def first_wide(got, block, members, log_rows):
    return call(
        functools.partial(first_wide_kernel, log_rows),
        "first_wide",
        (shape((members, block.shape[1] // LANES, LANES)), shape(block.shape)),
        [VMEM, HBM],
        (VMEM, VMEM),
        got,
        block,
        scratch_shapes=[pltpu.SemaphoreType.DMA((4,))],
        vmem=51,
    )


def rounded(values):
    return values.astype(BF16).astype(F32)


def final_kernel(log_cols, got_ref, wide_ref, data_ref, out_ref, pot_ref, weights, held, terms, sems):
    ny, nx, cols, width = data_ref.shape
    rows = wide_ref.shape[0]
    copies = [pltpu.make_async_copy(data_ref.at[y], held.at[y], sems.at[y]) for y in range(ny)]
    for copy in copies:
        copy.start()
    pot = -(log_cols + joined(got_ref[...]))
    pot_ref[...] = pot
    top = row_top(wide_ref, pot)
    total = None
    for k in range(pot.shape[0]):
        part = jnp.exp(wide_ref[:, lanes(k)] + pot[k : k + 1] - top)
        weights[:, lanes(k)] = part.astype(BF16)
        total = part if total is None else total + part
    total = jnp.sum(total, axis=1, keepdims=True)
    inverse = 1.0 / total
    local = as_rows(top + jnp.log(total))[:16]
    first = rounded(local)
    second = rounded(local - first)
    third = local - first - second
    place = lax.broadcasted_iota(jnp.int32, local.shape, 0)
    extra = jnp.where(place == 0, first, jnp.where(place == 1, second, third))
    extra = jnp.where(place < 3, extra, 0.0).astype(BF16)
    half = ny // 2
    for copy in copies[:half]:
        copy.wait()
    for x in range(nx):
        right = jnp.concatenate([held[y, x] for y in range(half)], axis=0)
        terms[x] = jnp.dot(weights[:, : half * cols], right, preferred_element_type=F32)
    for copy in copies[half:]:
        copy.wait()
    for x in range(nx):
        right = jnp.concatenate([held[y, x] for y in range(half, ny)], axis=0)
        term = terms[x] + jnp.dot(weights[:, half * cols :], right, preferred_element_type=F32)
        out_ref[x, :rows, :] = (term * inverse).astype(BF16)
        out_ref[x, rows:, :] = extra


def final_terms(got, wide, data, log_cols):
    ny, nx, cols, width = data.shape
    rows = wide.shape[0]
    return call(
        functools.partial(final_kernel, log_cols),
        "final_terms",
        (shape((nx, rows + 16, width), BF16), shape(got.shape[1:])),
        [VMEM, VMEM, HBM],
        (VMEM, VMEM),
        got,
        wide,
        data,
        scratch_shapes=[
            pltpu.VMEM(wide.shape, BF16),
            pltpu.VMEM(data.shape, BF16),
            pltpu.VMEM((nx, rows, width), F32),
            pltpu.SemaphoreType.DMA((ny,)),
        ],
        vmem=50,
    )


def combine_kernel(log_rows, features, got_ref, began_ref, begin_ref, col_ref, out_ref, pot_ref, col_pot_ref):
    nx, rows = got_ref.shape[0], out_ref.shape[0]
    chunks = rows // LANES
    locals_ = [jnp.sum(got_ref[x, rows:, :].astype(F32), axis=0, keepdims=True) for x in range(nx)]
    top = functools.reduce(jnp.maximum, locals_)
    whole = top + jnp.log(functools.reduce(jnp.add, [jnp.exp(v - top) for v in locals_]))
    parts = col_pot_ref.shape[0]
    mine = lax.axis_index("y")
    own = jnp.zeros(col_pot_ref.shape, F32)
    for y in range(col_ref.shape[0] // parts):
        own = jnp.where(mine == y, col_ref[y * parts : (y + 1) * parts, :], own)
    col_pot_ref[...] = EPSILON * (own - begin_ref[...])
    noise_sq = jnp.sum(began_ref[:, chunks:, :], axis=0)
    for k in range(chunks):
        pot_ref[k : k + 1, :] = noise_sq[k : k + 1] * (1.0 / features) - EPSILON * (log_rows + whole[:, lanes(k)])
    scales = [as_column(jnp.exp(v - whole)) for v in locals_]
    for k in range(out_ref.shape[1] // LANES):
        parts = [scales[x] * got_ref[x, :rows, lanes(k)].astype(F32) for x in range(nx)]
        out_ref[:, lanes(k)] = functools.reduce(jnp.add, parts).astype(BF16)


def shards(noise, data):
    rows, width = noise.shape
    cols, features = data.shape
    nx, ny, nrow, ncol = (lax.axis_size(axes) for axes in ("x", "y", ROW, COL))
    log_rows, log_cols = _log(rows * nrow), _log(cols * ncol)
    chunks = rows // LANES

    low = rows - FIRST_ROWS
    share = cols // nrow
    by_x, by_y, noise_sq = call(
        functools.partial(prepare_kernel, FIRST_ROWS),
        "prepare",
        (
            shape((nx, FIRST_ROWS, width), BF16),
            shape((ny, low + nx * share, width), BF16),
            shape((chunks, LANES)),
        ),
        [VMEM, HBM],
        (VMEM, VMEM, VMEM),
        noise,
        data,
        scratch_shapes=[pltpu.VMEM((share, features), BF16), pltpu.SemaphoreType.DMA],
        vmem=52,
    )
    part = lax.all_to_all(by_x, "x", 0, 0)
    first = lax.all_gather(part, "y")
    part, by_y = lax.optimization_barrier((part, by_y))
    got = lax.all_to_all(by_y, "y", 0, 0)
    second = jnp.broadcast_to(got[None, :, :low], (nx, ny, low, width))
    second = lax.all_to_all(second, "x", 0, 0)

    data_sq = jnp.sum(jnp.square(data.astype(F32)), axis=1)
    begin_pot = (data_sq * (-1.0 / (features * EPSILON))).reshape(-1, LANES)
    scale = 2.0 / (features * EPSILON)
    scaled, copied, sent, piece = call(
        functools.partial(inner_kernel, scale),
        "inner",
        (
            shape((rows, cols)),
            shape((rows, cols)),
            shape((ncol, 2 * chunks, LANES)),
            shape((ny, nx * share, width), BF16),
        ),
        [HBM, VMEM, HBM, VMEM, VMEM, HBM],
        (VMEM, HBM, VMEM, HBM),
        first,
        second,
        data,
        begin_pot,
        noise_sq,
        got,
        scratch_shapes=[
            pltpu.VMEM(first.shape, BF16),
            pltpu.VMEM(data.shape, BF16),
            pltpu.SemaphoreType.DMA((nx + 1,)),
            pltpu.SemaphoreType.DMA((nx + 1,)),
        ],
        vmem=50,
    )
    wide = lax.all_gather(copied, "y", axis=1, tiled=True)

    began = None
    for step in range(ITERS):
        got = lax.all_to_all(sent, "x" if step > WIDE_FROM else COL, 0, 0)
        if step == 0:
            began, piece = lax.optimization_barrier((got, piece))
            mine = lax.all_gather(piece.reshape(ny, nx, share, width), ROW, axis=2, tiled=True)
        if step == WIDE_FROM:
            sent, wide = first_wide(got, wide, nrow, log_rows)
        else:
            sent = half_cols(got, wide if step > WIDE_FROM else scaled, nrow, log_rows)
        got = lax.all_to_all(sent, ROW, 0, 0)
        if step < WIDE_FROM:
            sent = half_rows(got, scaled, ncol, log_cols)
        elif step < ITERS - 1:
            sent = half_rows(got, wide, nx, log_cols)
    terms, col_pot = final_terms(got, wide, mine, log_cols)
    got = lax.all_to_all(terms, "x", 0, 0)
    targets, noise_potential, data_potential = call(
        functools.partial(combine_kernel, log_rows, features),
        "combine",
        (shape((rows, width), BF16), shape((chunks, LANES)), shape(begin_pot.shape)),
        [VMEM] * 4,
        (VMEM, VMEM, VMEM),
        got,
        began,
        begin_pot,
        col_pot,
    )
    return (noise_potential.reshape(rows), data_potential.reshape(cols), targets)


def _log(count):
    return float(np.log(np.float32(count)))


def solution(mesh):
    devices = mesh.devices.reshape(8, 2, 4, 8)
    return jax.shard_map(
        shards,
        mesh=Mesh(devices, ("z", "core", "x", "y")),
        in_specs=(P(ROW, COL), P(COL, None)),
        out_specs=(P(ROW), P(COL), P(ROW, COL)),
        check_vma=False,
    )
```

```python
import functools

import jax
import jax.numpy as jnp
import numpy as np
from jax import lax
from jax.experimental import pallas as pl
from jax.experimental.pallas import tpu as pltpu
from jax.sharding import Mesh, PartitionSpec as P

ITERS = 4
EPSILON = 0.01
ROW = ("z", "core")
COL = ("x", "y")
LANES = 128
FIRST_ROWS = 160
WIDE_FROM = 1
VMEM = pl.BlockSpec(memory_space=pltpu.VMEM)
HBM = pl.BlockSpec(memory_space=pltpu.HBM)
MIB = 2**20
F32, BF16 = jnp.float32, jnp.bfloat16


def call(kernel, name, out_shape, in_specs, out_specs, *args, scratch_shapes=(), vmem=40):
    return pl.pallas_call(
        kernel,
        out_shape=out_shape,
        in_specs=in_specs,
        out_specs=out_specs,
        scratch_shapes=scratch_shapes,
        compiler_params=pltpu.CompilerParams(vmem_limit_bytes=vmem * MIB),
        name=name,
    )(*args)


def shape(dims, dtype=F32):
    return jax.ShapeDtypeStruct(dims, dtype)


def lanes(k):
    return slice(k * LANES, (k + 1) * LANES)


def as_column(values):
    return jnp.broadcast_to(values, (LANES, values.shape[1])).T


def as_rows(column):
    return jnp.broadcast_to(column, (column.shape[0], LANES)).T


def joined(got):
    top = jnp.max(got, axis=0)
    return top + jnp.log(jnp.sum(jnp.exp(got - top[None]), axis=0))


def prepare_kernel(high, noise_ref, data_ref, by_x_ref, by_y_ref, sq_ref, held, sem):
    nx = by_x_ref.shape[0]
    ny, sent, width = by_y_ref.shape
    rows = noise_ref.shape[0]
    low = rows - high
    share = (sent - low) // nx
    at = (lax.axis_index(ROW[0]) * lax.axis_size(ROW[1]) + lax.axis_index(ROW[1])) * share
    copy = pltpu.make_async_copy(data_ref.at[pl.ds(pl.multiple_of(at, share), share), :], held, sem)
    copy.start()
    for x in range(nx):
        by_x_ref[x] = noise_ref[:high]
    for y in range(ny):
        by_y_ref[y, :low] = noise_ref[high:]
    squares = jnp.square(noise_ref[...].astype(F32))
    squares = as_rows(jnp.sum(squares, axis=1, keepdims=True))[:1]
    for k in range(rows // LANES):
        sq_ref[k : k + 1, :] = squares[:, lanes(k)]
    copy.wait()
    for y in range(ny):
        for x in range(nx):
            block = held[:, (x * ny + y) * width : (x * ny + y + 1) * width]
            by_y_ref[y, low + x * share : low + (x + 1) * share] = block


def inner_kernel(
    scale,
    first_ref,
    second_ref,
    data_ref,
    pot_ref,
    sq_ref,
    got_ref,
    out_ref,
    copy_ref,
    send_ref,
    piece_ref,
    rows_held,
    held,
    row_sems,
    sems,
):
    ny, nx, _, width = first_ref.shape
    apart = pltpu.make_async_copy(got_ref.at[:, second_ref.shape[2] :], piece_ref, row_sems.at[nx])
    apart.start()
    wide = ny * width
    copies = [
        (
            pltpu.make_async_copy(
                data_ref.at[:, x * wide : (x + 1) * wide], held.at[:, x * wide : (x + 1) * wide], sems.at[x]
            ),
            pltpu.make_async_copy(first_ref.at[:, x], rows_held.at[:, x], row_sems.at[x]),
        )
        for x in range(nx)
    ]
    for pair in copies:
        for copy in pair:
            copy.start()
    total = None
    for x in range(nx):
        for copy in copies[x]:
            copy.wait()
        for y in range(ny):
            left = jnp.concatenate([rows_held[y, x], second_ref[x, y]], axis=0)
            at = x * wide + y * width
            one = lax.dot_general(
                left, held[:, at : at + width], (((1,), (1,)), ((), ())), preferred_element_type=F32
            )
            total = one if total is None else total + one
    out_ref[...] = total * scale
    out = pltpu.make_async_copy(out_ref, copy_ref, sems.at[nx])
    out.start()
    local = local_rows(out_ref, pot_ref[...])
    chunks = local.shape[1] // LANES
    members = send_ref.shape[0]
    for k in range(chunks):
        send_ref[:, k, :] = jnp.broadcast_to(local[:, lanes(k)], (members, LANES))
        send_ref[:, chunks + k, :] = jnp.broadcast_to(sq_ref[k : k + 1], (members, LANES))
    out.wait()
    apart.wait()


def row_top(block_ref, pot):
    top = None
    for k in range(pot.shape[0]):
        scores = block_ref[:, lanes(k)] + pot[k : k + 1]
        top = scores if top is None else jnp.maximum(top, scores)
    return jnp.max(top, axis=1, keepdims=True)


def local_rows(block_ref, pot):
    top = row_top(block_ref, pot)
    total = None
    for k in range(pot.shape[0]):
        part = jnp.exp(block_ref[:, lanes(k)] + pot[k : k + 1] - top)
        total = part if total is None else total + part
    return as_rows(top + jnp.log(jnp.sum(total, axis=1, keepdims=True)))[:1]


def rows_kernel(log_cols, got_ref, block_ref, out_ref):
    local = local_rows(block_ref, -(log_cols + joined(got_ref[...])))
    for k in range(out_ref.shape[1]):
        out_ref[:, k, :] = jnp.broadcast_to(local[:, lanes(k)], (out_ref.shape[0], LANES))


def half_rows(got, block, members, log_cols):
    out = shape((members, block.shape[0] // LANES, LANES))
    return call(functools.partial(rows_kernel, log_cols), "half_rows", out, [VMEM, VMEM], VMEM, got, block)


def column_pot(got_ref, chunks, log_rows):
    pot = -(log_rows + joined(got_ref[:, :chunks, :]))
    return jnp.concatenate([as_column(pot[k : k + 1]) for k in range(chunks)], axis=0)


def send_cols(block_ref, pot, out_ref, places):
    for k in places:
        scores = block_ref[:, lanes(k)] + pot
        top = jnp.max(scores, axis=0, keepdims=True)
        local = top + jnp.log(jnp.sum(jnp.exp(scores - top), axis=0, keepdims=True))
        out_ref[:, k, :] = jnp.broadcast_to(local, (out_ref.shape[0], LANES))


def cols_kernel(log_rows, got_ref, block_ref, out_ref):
    pot = column_pot(got_ref, block_ref.shape[0] // LANES, log_rows)
    send_cols(block_ref, pot, out_ref, range(out_ref.shape[1]))


def half_cols(got, block, members, log_rows):
    out = shape((members, block.shape[1] // LANES, LANES))
    return call(functools.partial(cols_kernel, log_rows), "half_cols", out, [VMEM, VMEM], VMEM, got, block)


def first_wide_kernel(log_rows, got_ref, block_ref, out_ref, held_ref, sems):
    parts, rows, width = block_ref.shape
    places = width // LANES
    copies = [
        pltpu.make_async_copy(block_ref.at[k], held_ref.at[:, k * width : (k + 1) * width], sems.at[k])
        for k in range(parts)
    ]
    for copy in copies:
        copy.start()
    pot = column_pot(got_ref, rows // LANES, log_rows)
    for k in range(parts):
        copies[k].wait()
        send_cols(held_ref, pot, out_ref, range(k * places, (k + 1) * places))


def first_wide(got, blocks, members, log_rows):
    parts, rows, width = blocks.shape
    return call(
        functools.partial(first_wide_kernel, log_rows),
        "first_wide",
        (shape((members, parts * width // LANES, LANES)), shape((rows, parts * width))),
        [VMEM, HBM],
        (VMEM, VMEM),
        got,
        blocks,
        scratch_shapes=[pltpu.SemaphoreType.DMA((parts,))],
        vmem=51,
    )


def rounded(values):
    return values.astype(BF16).astype(F32)


def final_kernel(log_cols, got_ref, wide_ref, data_ref, out_ref, pot_ref, weights, held, terms, sems):
    nrow, ny, nx, share, _ = data_ref.shape
    cols = nrow * share
    rows = wide_ref.shape[0]
    copies = [pltpu.make_async_copy(data_ref.at[:, y], held.at[y], sems.at[y]) for y in range(ny)]
    for copy in copies:
        copy.start()
    pot = -(log_cols + joined(got_ref[...]))
    pot_ref[...] = pot
    top = row_top(wide_ref, pot)
    total = None
    for k in range(pot.shape[0]):
        part = jnp.exp(wide_ref[:, lanes(k)] + pot[k : k + 1] - top)
        weights[:, lanes(k)] = part.astype(BF16)
        total = part if total is None else total + part
    total = jnp.sum(total, axis=1, keepdims=True)
    inverse = 1.0 / total
    local = as_rows(top + jnp.log(total))[:16]
    first = rounded(local)
    second = rounded(local - first)
    third = local - first - second
    place = lax.broadcasted_iota(jnp.int32, local.shape, 0)
    extra = jnp.where(place == 0, first, jnp.where(place == 1, second, third))
    extra = jnp.where(place < 3, extra, 0.0).astype(BF16)
    half = ny // 2
    for copy in copies[:half]:
        copy.wait()
    for x in range(nx):
        right = jnp.concatenate([held[y, r, x] for y in range(half) for r in range(nrow)], axis=0)
        terms[x] = jnp.dot(weights[:, : half * cols], right, preferred_element_type=F32)
    for copy in copies[half:]:
        copy.wait()
    for x in range(nx):
        right = jnp.concatenate([held[y, r, x] for y in range(half, ny) for r in range(nrow)], axis=0)
        term = terms[x] + jnp.dot(weights[:, half * cols :], right, preferred_element_type=F32)
        out_ref[x, :rows, :] = (term * inverse).astype(BF16)
        out_ref[x, rows:, :] = extra


def final_terms(got, wide, data, log_cols):
    nrow, ny, nx, share, width = data.shape
    rows = wide.shape[0]
    return call(
        functools.partial(final_kernel, log_cols),
        "final_terms",
        (shape((nx, rows + 16, width), BF16), shape(got.shape[1:])),
        [VMEM, VMEM, HBM],
        (VMEM, VMEM),
        got,
        wide,
        data,
        scratch_shapes=[
            pltpu.VMEM(wide.shape, BF16),
            pltpu.VMEM((ny, nrow, nx, share, width), BF16),
            pltpu.VMEM((nx, rows, width), F32),
            pltpu.SemaphoreType.DMA((ny,)),
        ],
        vmem=50,
    )


def combine_kernel(log_rows, features, got_ref, began_ref, begin_ref, col_ref, out_ref, pot_ref, col_pot_ref):
    nx, rows = got_ref.shape[0], out_ref.shape[0]
    chunks = rows // LANES
    locals_ = [jnp.sum(got_ref[x, rows:, :].astype(F32), axis=0, keepdims=True) for x in range(nx)]
    top = functools.reduce(jnp.maximum, locals_)
    whole = top + jnp.log(functools.reduce(jnp.add, [jnp.exp(v - top) for v in locals_]))
    parts = col_pot_ref.shape[0]
    mine = lax.axis_index("y")
    own = jnp.zeros(col_pot_ref.shape, F32)
    for y in range(col_ref.shape[0] // parts):
        own = jnp.where(mine == y, col_ref[y * parts : (y + 1) * parts, :], own)
    col_pot_ref[...] = EPSILON * (own - begin_ref[...])
    noise_sq = jnp.sum(began_ref[:, chunks:, :], axis=0)
    for k in range(chunks):
        pot_ref[k : k + 1, :] = noise_sq[k : k + 1] * (1.0 / features) - EPSILON * (log_rows + whole[:, lanes(k)])
    scales = [as_column(jnp.exp(v - whole)) for v in locals_]
    for k in range(out_ref.shape[1] // LANES):
        parts = [scales[x] * got_ref[x, :rows, lanes(k)].astype(F32) for x in range(nx)]
        out_ref[:, lanes(k)] = functools.reduce(jnp.add, parts).astype(BF16)


def shards(noise, data):
    rows, width = noise.shape
    cols, features = data.shape
    nx, ny, nrow, ncol = (lax.axis_size(axes) for axes in ("x", "y", ROW, COL))
    log_rows, log_cols = _log(rows * nrow), _log(cols * ncol)
    chunks = rows // LANES

    low = rows - FIRST_ROWS
    share = cols // nrow
    by_x, by_y, noise_sq = call(
        functools.partial(prepare_kernel, FIRST_ROWS),
        "prepare",
        (
            shape((nx, FIRST_ROWS, width), BF16),
            shape((ny, low + nx * share, width), BF16),
            shape((chunks, LANES)),
        ),
        [VMEM, HBM],
        (VMEM, VMEM, VMEM),
        noise,
        data,
        scratch_shapes=[pltpu.VMEM((share, features), BF16), pltpu.SemaphoreType.DMA],
        vmem=52,
    )
    part = lax.all_to_all(by_x, "x", 0, 0)
    first = lax.all_gather(part, "y")
    part, by_y = lax.optimization_barrier((part, by_y))
    got = lax.all_to_all(by_y, "y", 0, 0)
    second = jnp.broadcast_to(got[None, :, :low], (nx, ny, low, width))
    second = lax.all_to_all(second, "x", 0, 0)

    data_sq = jnp.sum(jnp.square(data.astype(F32)), axis=1)
    begin_pot = (data_sq * (-1.0 / (features * EPSILON))).reshape(-1, LANES)
    scale = 2.0 / (features * EPSILON)
    scaled, copied, sent, piece = call(
        functools.partial(inner_kernel, scale),
        "inner",
        (
            shape((rows, cols)),
            shape((rows, cols)),
            shape((ncol, 2 * chunks, LANES)),
            shape((ny, nx * share, width), BF16),
        ),
        [HBM, VMEM, HBM, VMEM, VMEM, HBM],
        (VMEM, HBM, VMEM, HBM),
        first,
        second,
        data,
        begin_pot,
        noise_sq,
        got,
        scratch_shapes=[
            pltpu.VMEM(first.shape, BF16),
            pltpu.VMEM(data.shape, BF16),
            pltpu.SemaphoreType.DMA((nx + 1,)),
            pltpu.SemaphoreType.DMA((nx + 1,)),
        ],
        vmem=50,
    )
    wide = lax.all_gather(copied, "y")

    began = None
    for step in range(ITERS):
        got = lax.all_to_all(sent, "x" if step > WIDE_FROM else COL, 0, 0)
        if step == 0:
            began, piece = lax.optimization_barrier((got, piece))
            mine = lax.all_gather(piece.reshape(ny, nx, share, width), ROW)
        if step == WIDE_FROM:
            sent, wide = first_wide(got, wide, nrow, log_rows)
        else:
            sent = half_cols(got, wide if step > WIDE_FROM else scaled, nrow, log_rows)
        got = lax.all_to_all(sent, ROW, 0, 0)
        if step < WIDE_FROM:
            sent = half_rows(got, scaled, ncol, log_cols)
        elif step < ITERS - 1:
            sent = half_rows(got, wide, nx, log_cols)
    terms, col_pot = final_terms(got, wide, mine, log_cols)
    got = lax.all_to_all(terms, "x", 0, 0)
    targets, noise_potential, data_potential = call(
        functools.partial(combine_kernel, log_rows, features),
        "combine",
        (shape((rows, width), BF16), shape((chunks, LANES)), shape(begin_pot.shape)),
        [VMEM] * 4,
        (VMEM, VMEM, VMEM),
        got,
        began,
        begin_pot,
        col_pot,
    )
    return (noise_potential.reshape(rows), data_potential.reshape(cols), targets)


def _log(count):
    return float(np.log(np.float32(count)))


def solution(mesh):
    devices = mesh.devices.reshape(8, 2, 4, 8)
    return jax.shard_map(
        shards,
        mesh=Mesh(devices, ("z", "core", "x", "y")),
        in_specs=(P(ROW, COL), P(COL, None)),
        out_specs=(P(ROW), P(COL), P(ROW, COL)),
        check_vma=False,
    )
```

```python
import functools

import jax
import jax.numpy as jnp
import numpy as np
from jax import lax
from jax.experimental import pallas as pl
from jax.experimental.pallas import tpu as pltpu
from jax.sharding import Mesh, PartitionSpec as P

ITERS = 4
EPSILON = 0.01
ROW = ("z", "core")
COL = ("x", "y")
LANES = 128
FIRST_ROWS = 176
WIDE_FROM = 1
VMEM = pl.BlockSpec(memory_space=pltpu.VMEM)
HBM = pl.BlockSpec(memory_space=pltpu.HBM)
MIB = 2**20
F32, BF16 = jnp.float32, jnp.bfloat16


def call(kernel, name, out_shape, in_specs, out_specs, *args, scratch_shapes=(), vmem=40):
    return pl.pallas_call(
        kernel,
        out_shape=out_shape,
        in_specs=in_specs,
        out_specs=out_specs,
        scratch_shapes=scratch_shapes,
        compiler_params=pltpu.CompilerParams(vmem_limit_bytes=vmem * MIB),
        name=name,
    )(*args)


def shape(dims, dtype=F32):
    return jax.ShapeDtypeStruct(dims, dtype)


def lanes(k):
    return slice(k * LANES, (k + 1) * LANES)


def as_column(values):
    return jnp.broadcast_to(values, (LANES, values.shape[1])).T


def as_rows(column):
    return jnp.broadcast_to(column, (column.shape[0], LANES)).T


def joined(got):
    top = jnp.max(got, axis=0)
    return top + jnp.log(jnp.sum(jnp.exp(got - top[None]), axis=0))


def prepare_kernel(high, noise_ref, data_ref, by_x_ref, by_y_ref, sq_ref, held, sem):
    nx = by_x_ref.shape[0]
    ny, sent, width = by_y_ref.shape
    rows = noise_ref.shape[0]
    low = rows - high
    share = (sent - low) // nx
    at = (lax.axis_index(ROW[0]) * lax.axis_size(ROW[1]) + lax.axis_index(ROW[1])) * share
    copy = pltpu.make_async_copy(data_ref.at[pl.ds(pl.multiple_of(at, share), share), :], held, sem)
    copy.start()
    for x in range(nx):
        by_x_ref[x] = noise_ref[:high]
    for y in range(ny):
        by_y_ref[y, :low] = noise_ref[high:]
    squares = jnp.square(noise_ref[...].astype(F32))
    squares = as_rows(jnp.sum(squares, axis=1, keepdims=True))[:1]
    for k in range(rows // LANES):
        sq_ref[k : k + 1, :] = squares[:, lanes(k)]
    copy.wait()
    for y in range(ny):
        for x in range(nx):
            block = held[:, (x * ny + y) * width : (x * ny + y + 1) * width]
            by_y_ref[y, low + x * share : low + (x + 1) * share] = block


def inner_kernel(
    scale,
    first_ref,
    second_ref,
    data_ref,
    pot_ref,
    sq_ref,
    got_ref,
    out_ref,
    copy_ref,
    send_ref,
    piece_ref,
    rows_held,
    held,
    row_sems,
    sems,
):
    ny, nx, _, width = first_ref.shape
    apart = pltpu.make_async_copy(got_ref.at[:, second_ref.shape[2] :], piece_ref, row_sems.at[nx])
    apart.start()
    wide = ny * width
    copies = [
        (
            pltpu.make_async_copy(
                data_ref.at[:, x * wide : (x + 1) * wide], held.at[:, x * wide : (x + 1) * wide], sems.at[x]
            ),
            pltpu.make_async_copy(first_ref.at[:, x], rows_held.at[:, x], row_sems.at[x]),
        )
        for x in range(nx)
    ]
    for pair in copies:
        for copy in pair:
            copy.start()
    total = None
    for x in range(nx):
        for copy in copies[x]:
            copy.wait()
        for y in range(ny):
            left = jnp.concatenate([rows_held[y, x], second_ref[x, y]], axis=0)
            at = x * wide + y * width
            one = lax.dot_general(
                left, held[:, at : at + width], (((1,), (1,)), ((), ())), preferred_element_type=F32
            )
            total = one if total is None else total + one
    out_ref[...] = total * scale
    out = pltpu.make_async_copy(out_ref, copy_ref, sems.at[nx])
    out.start()
    local = local_rows(out_ref, pot_ref[...])
    chunks = local.shape[1] // LANES
    members = send_ref.shape[0]
    for k in range(chunks):
        send_ref[:, k, :] = jnp.broadcast_to(local[:, lanes(k)], (members, LANES))
        send_ref[:, chunks + k, :] = jnp.broadcast_to(sq_ref[k : k + 1], (members, LANES))
    out.wait()
    apart.wait()


def row_top(block_ref, pot):
    top = None
    for k in range(pot.shape[0]):
        scores = block_ref[:, lanes(k)] + pot[k : k + 1]
        top = scores if top is None else jnp.maximum(top, scores)
    return jnp.max(top, axis=1, keepdims=True)


def local_rows(block_ref, pot):
    top = row_top(block_ref, pot)
    total = None
    for k in range(pot.shape[0]):
        part = jnp.exp(block_ref[:, lanes(k)] + pot[k : k + 1] - top)
        total = part if total is None else total + part
    return as_rows(top + jnp.log(jnp.sum(total, axis=1, keepdims=True)))[:1]


def rows_kernel(log_cols, got_ref, block_ref, out_ref):
    local = local_rows(block_ref, -(log_cols + joined(got_ref[...])))
    for k in range(out_ref.shape[1]):
        out_ref[:, k, :] = jnp.broadcast_to(local[:, lanes(k)], (out_ref.shape[0], LANES))


def half_rows(got, block, members, log_cols):
    out = shape((members, block.shape[0] // LANES, LANES))
    return call(functools.partial(rows_kernel, log_cols), "half_rows", out, [VMEM, VMEM], VMEM, got, block)


def column_pot(got_ref, chunks, log_rows):
    pot = -(log_rows + joined(got_ref[:, :chunks, :]))
    return jnp.concatenate([as_column(pot[k : k + 1]) for k in range(chunks)], axis=0)


def send_cols(block_ref, pot, out_ref, places):
    for k in places:
        scores = block_ref[:, lanes(k)] + pot
        top = jnp.max(scores, axis=0, keepdims=True)
        local = top + jnp.log(jnp.sum(jnp.exp(scores - top), axis=0, keepdims=True))
        out_ref[:, k, :] = jnp.broadcast_to(local, (out_ref.shape[0], LANES))


def cols_kernel(log_rows, got_ref, block_ref, out_ref):
    pot = column_pot(got_ref, block_ref.shape[0] // LANES, log_rows)
    send_cols(block_ref, pot, out_ref, range(out_ref.shape[1]))


def half_cols(got, block, members, log_rows):
    out = shape((members, block.shape[1] // LANES, LANES))
    return call(functools.partial(cols_kernel, log_rows), "half_cols", out, [VMEM, VMEM], VMEM, got, block)


def first_wide_kernel(log_rows, got_ref, block_ref, out_ref, held_ref, sems):
    parts, rows, width = block_ref.shape
    places = width // LANES
    copies = [
        pltpu.make_async_copy(block_ref.at[k], held_ref.at[:, k * width : (k + 1) * width], sems.at[k])
        for k in range(parts)
    ]
    for copy in copies:
        copy.start()
    pot = column_pot(got_ref, rows // LANES, log_rows)
    for k in range(parts):
        copies[k].wait()
        send_cols(held_ref, pot, out_ref, range(k * places, (k + 1) * places))


def first_wide(got, blocks, members, log_rows):
    parts, rows, width = blocks.shape
    return call(
        functools.partial(first_wide_kernel, log_rows),
        "first_wide",
        (shape((members, parts * width // LANES, LANES)), shape((rows, parts * width))),
        [VMEM, HBM],
        (VMEM, VMEM),
        got,
        blocks,
        scratch_shapes=[pltpu.SemaphoreType.DMA((parts,))],
        vmem=51,
    )


def rounded(values):
    return values.astype(BF16).astype(F32)


def final_kernel(log_cols, got_ref, wide_ref, data_ref, out_ref, pot_ref, weights, held, terms, sems):
    nrow, ny, nx, share, _ = data_ref.shape
    cols = nrow * share
    rows = wide_ref.shape[0]
    copies = [pltpu.make_async_copy(data_ref.at[:, y], held.at[y], sems.at[y]) for y in range(ny)]
    for copy in copies:
        copy.start()
    pot = -(log_cols + joined(got_ref[...]))
    pot_ref[...] = pot
    top = row_top(wide_ref, pot)
    total = None
    for k in range(pot.shape[0]):
        part = jnp.exp(wide_ref[:, lanes(k)] + pot[k : k + 1] - top)
        weights[:, lanes(k)] = part.astype(BF16)
        total = part if total is None else total + part
    total = jnp.sum(total, axis=1, keepdims=True)
    inverse = 1.0 / total
    local = as_rows(top + jnp.log(total))[:16]
    first = rounded(local)
    second = rounded(local - first)
    third = local - first - second
    place = lax.broadcasted_iota(jnp.int32, local.shape, 0)
    extra = jnp.where(place == 0, first, jnp.where(place == 1, second, third))
    extra = jnp.where(place < 3, extra, 0.0).astype(BF16)
    half = ny // 2
    for copy in copies[:half]:
        copy.wait()
    for x in range(nx):
        right = jnp.concatenate([held[y, r, x] for y in range(half) for r in range(nrow)], axis=0)
        terms[x] = jnp.dot(weights[:, : half * cols], right, preferred_element_type=F32)
    for copy in copies[half:]:
        copy.wait()
    for x in range(nx):
        right = jnp.concatenate([held[y, r, x] for y in range(half, ny) for r in range(nrow)], axis=0)
        term = terms[x] + jnp.dot(weights[:, half * cols :], right, preferred_element_type=F32)
        out_ref[x, :rows, :] = (term * inverse).astype(BF16)
        out_ref[x, rows:, :] = extra


def final_terms(got, wide, data, log_cols):
    nrow, ny, nx, share, width = data.shape
    rows = wide.shape[0]
    return call(
        functools.partial(final_kernel, log_cols),
        "final_terms",
        (shape((nx, rows + 16, width), BF16), shape(got.shape[1:])),
        [VMEM, VMEM, HBM],
        (VMEM, VMEM),
        got,
        wide,
        data,
        scratch_shapes=[
            pltpu.VMEM(wide.shape, BF16),
            pltpu.VMEM((ny, nrow, nx, share, width), BF16),
            pltpu.VMEM((nx, rows, width), F32),
            pltpu.SemaphoreType.DMA((ny,)),
        ],
        vmem=50,
    )


def combine_kernel(log_rows, features, got_ref, began_ref, begin_ref, col_ref, out_ref, pot_ref, col_pot_ref):
    nx, rows = got_ref.shape[0], out_ref.shape[0]
    chunks = rows // LANES
    locals_ = [jnp.sum(got_ref[x, rows:, :].astype(F32), axis=0, keepdims=True) for x in range(nx)]
    top = functools.reduce(jnp.maximum, locals_)
    whole = top + jnp.log(functools.reduce(jnp.add, [jnp.exp(v - top) for v in locals_]))
    parts = col_pot_ref.shape[0]
    mine = lax.axis_index("y")
    own = jnp.zeros(col_pot_ref.shape, F32)
    for y in range(col_ref.shape[0] // parts):
        own = jnp.where(mine == y, col_ref[y * parts : (y + 1) * parts, :], own)
    col_pot_ref[...] = EPSILON * (own - begin_ref[...])
    noise_sq = jnp.sum(began_ref[:, chunks:, :], axis=0)
    for k in range(chunks):
        pot_ref[k : k + 1, :] = noise_sq[k : k + 1] * (1.0 / features) - EPSILON * (log_rows + whole[:, lanes(k)])
    scales = [as_column(jnp.exp(v - whole)) for v in locals_]
    for k in range(out_ref.shape[1] // LANES):
        parts = [scales[x] * got_ref[x, :rows, lanes(k)].astype(F32) for x in range(nx)]
        out_ref[:, lanes(k)] = functools.reduce(jnp.add, parts).astype(BF16)


def shards(noise, data):
    rows, width = noise.shape
    cols, features = data.shape
    nx, ny, nrow, ncol = (lax.axis_size(axes) for axes in ("x", "y", ROW, COL))
    log_rows, log_cols = _log(rows * nrow), _log(cols * ncol)
    chunks = rows // LANES

    low = rows - FIRST_ROWS
    share = cols // nrow
    by_x, by_y, noise_sq = call(
        functools.partial(prepare_kernel, FIRST_ROWS),
        "prepare",
        (
            shape((nx, FIRST_ROWS, width), BF16),
            shape((ny, low + nx * share, width), BF16),
            shape((chunks, LANES)),
        ),
        [VMEM, HBM],
        (VMEM, VMEM, VMEM),
        noise,
        data,
        scratch_shapes=[pltpu.VMEM((share, features), BF16), pltpu.SemaphoreType.DMA],
        vmem=52,
    )
    part = lax.all_to_all(by_x, "x", 0, 0)
    first = lax.all_gather(part, "y")
    part, by_y = lax.optimization_barrier((part, by_y))
    got = lax.all_to_all(by_y, "y", 0, 0)
    second = jnp.broadcast_to(got[None, :, :low], (nx, ny, low, width))
    second = lax.all_to_all(second, "x", 0, 0)

    data_sq = jnp.sum(jnp.square(data.astype(F32)), axis=1)
    begin_pot = (data_sq * (-1.0 / (features * EPSILON))).reshape(-1, LANES)
    scale = 2.0 / (features * EPSILON)
    scaled, copied, sent, piece = call(
        functools.partial(inner_kernel, scale),
        "inner",
        (
            shape((rows, cols)),
            shape((rows, cols)),
            shape((ncol, 2 * chunks, LANES)),
            shape((ny, nx * share, width), BF16),
        ),
        [HBM, VMEM, HBM, VMEM, VMEM, HBM],
        (VMEM, HBM, VMEM, HBM),
        first,
        second,
        data,
        begin_pot,
        noise_sq,
        got,
        scratch_shapes=[
            pltpu.VMEM(first.shape, BF16),
            pltpu.VMEM(data.shape, BF16),
            pltpu.SemaphoreType.DMA((nx + 1,)),
            pltpu.SemaphoreType.DMA((nx + 1,)),
        ],
        vmem=50,
    )
    wide = lax.all_gather(copied, "y")

    began = None
    for step in range(ITERS):
        got = lax.all_to_all(sent, "x" if step > WIDE_FROM else COL, 0, 0)
        if step == 0:
            began, piece = lax.optimization_barrier((got, piece))
            mine = lax.all_gather(piece.reshape(ny, nx, share, width), ROW)
        if step == WIDE_FROM:
            sent, wide = first_wide(got, wide, nrow, log_rows)
        else:
            sent = half_cols(got, wide if step > WIDE_FROM else scaled, nrow, log_rows)
        got = lax.all_to_all(sent, ROW, 0, 0)
        if step < WIDE_FROM:
            sent = half_rows(got, scaled, ncol, log_cols)
        elif step < ITERS - 1:
            sent = half_rows(got, wide, nx, log_cols)
    terms, col_pot = final_terms(got, wide, mine, log_cols)
    got = lax.all_to_all(terms, "x", 0, 0)
    targets, noise_potential, data_potential = call(
        functools.partial(combine_kernel, log_rows, features),
        "combine",
        (shape((rows, width), BF16), shape((chunks, LANES)), shape(begin_pot.shape)),
        [VMEM] * 4,
        (VMEM, VMEM, VMEM),
        got,
        began,
        begin_pot,
        col_pot,
    )
    return (noise_potential.reshape(rows), data_potential.reshape(cols), targets)


def _log(count):
    return float(np.log(np.float32(count)))


def solution(mesh):
    devices = mesh.devices.reshape(8, 2, 4, 8)
    return jax.shard_map(
        shards,
        mesh=Mesh(devices, ("z", "core", "x", "y")),
        in_specs=(P(ROW, COL), P(COL, None)),
        out_specs=(P(ROW), P(COL), P(ROW, COL)),
        check_vma=False,
    )
```

```python
import functools

import jax
import jax.numpy as jnp
import numpy as np
from jax import lax
from jax.experimental import pallas as pl
from jax.experimental.pallas import tpu as pltpu
from jax.sharding import Mesh, PartitionSpec as P

ITERS = 4
EPSILON = 0.01
ROW = ("z", "core")
COL = ("x", "y")
LANES = 128
FIRST_ROWS = 176
WIDE_FROM = 1
VMEM = pl.BlockSpec(memory_space=pltpu.VMEM)
HBM = pl.BlockSpec(memory_space=pltpu.HBM)
MIB = 2**20
F32, BF16 = jnp.float32, jnp.bfloat16


def call(kernel, name, out_shape, in_specs, out_specs, *args, scratch_shapes=(), vmem=40):
    return pl.pallas_call(
        kernel,
        out_shape=out_shape,
        in_specs=in_specs,
        out_specs=out_specs,
        scratch_shapes=scratch_shapes,
        compiler_params=pltpu.CompilerParams(vmem_limit_bytes=vmem * MIB),
        name=name,
    )(*args)


def shape(dims, dtype=F32):
    return jax.ShapeDtypeStruct(dims, dtype)


def lanes(k):
    return slice(k * LANES, (k + 1) * LANES)


def as_column(values):
    return jnp.broadcast_to(values, (LANES, values.shape[1])).T


def as_rows(column):
    return jnp.broadcast_to(column, (column.shape[0], LANES)).T


def joined(got):
    top = jnp.max(got, axis=0)
    return top + jnp.log(jnp.sum(jnp.exp(got - top[None]), axis=0))


def prepare_kernel(high, noise_ref, data_ref, by_x_ref, by_y_ref, sq_ref, held, sem):
    nx = by_x_ref.shape[0]
    ny, sent, width = by_y_ref.shape
    rows = noise_ref.shape[0]
    low = rows - high
    share = (sent - low) // nx
    at = (lax.axis_index(ROW[0]) * lax.axis_size(ROW[1]) + lax.axis_index(ROW[1])) * share
    copy = pltpu.make_async_copy(data_ref.at[pl.ds(pl.multiple_of(at, share), share), :], held, sem)
    copy.start()
    for x in range(nx):
        by_x_ref[x] = noise_ref[:high]
    for y in range(ny):
        by_y_ref[y, :low] = noise_ref[high:]
    squares = jnp.square(noise_ref[...].astype(F32))
    squares = as_rows(jnp.sum(squares, axis=1, keepdims=True))[:1]
    for k in range(rows // LANES):
        sq_ref[k : k + 1, :] = squares[:, lanes(k)]
    copy.wait()
    for y in range(ny):
        for x in range(nx):
            block = held[:, (x * ny + y) * width : (x * ny + y + 1) * width]
            by_y_ref[y, low + x * share : low + (x + 1) * share] = block


def load_kernel(scale, after_ref, data_ref, out_ref, pot_ref, sems):
    parts = pot_ref.shape[0]
    copies = [pltpu.make_async_copy(data_ref.at[lanes(k)], out_ref.at[lanes(k)], sems.at[k]) for k in range(parts)]
    for copy in copies:
        copy.start()
    for k in range(parts):
        copies[k].wait()
        total = None
        for f in range(out_ref.shape[1] // LANES):
            block = out_ref[lanes(k), lanes(f)].astype(F32)
            total = block * block if total is None else total + block * block
        pot_ref[k : k + 1, :] = as_rows(jnp.sum(total, axis=1, keepdims=True))[:1] * scale


def inner_kernel(
    scale,
    first_ref,
    second_ref,
    data_ref,
    pot_ref,
    sq_ref,
    got_ref,
    out_ref,
    copy_ref,
    send_ref,
    piece_ref,
    sems,
):
    ny, nx, _, width = first_ref.shape
    apart = pltpu.make_async_copy(got_ref.at[:, second_ref.shape[2] :], piece_ref, sems.at[0])
    apart.start()
    wide = ny * width
    total = None
    for x in range(nx):
        for y in range(ny):
            left = jnp.concatenate([first_ref[y, x], second_ref[x, y]], axis=0)
            at = x * wide + y * width
            one = lax.dot_general(
                left, data_ref[:, at : at + width], (((1,), (1,)), ((), ())), preferred_element_type=F32
            )
            total = one if total is None else total + one
    out_ref[...] = total * scale
    out = pltpu.make_async_copy(out_ref, copy_ref, sems.at[1])
    out.start()
    local = local_rows(out_ref, pot_ref[...])
    chunks = local.shape[1] // LANES
    members = send_ref.shape[0]
    for k in range(chunks):
        send_ref[:, k, :] = jnp.broadcast_to(local[:, lanes(k)], (members, LANES))
        send_ref[:, chunks + k, :] = jnp.broadcast_to(sq_ref[k : k + 1], (members, LANES))
    out.wait()
    apart.wait()


def row_top(block_ref, pot):
    top = None
    for k in range(pot.shape[0]):
        scores = block_ref[:, lanes(k)] + pot[k : k + 1]
        top = scores if top is None else jnp.maximum(top, scores)
    return jnp.max(top, axis=1, keepdims=True)


def local_rows(block_ref, pot):
    top = row_top(block_ref, pot)
    total = None
    for k in range(pot.shape[0]):
        part = jnp.exp(block_ref[:, lanes(k)] + pot[k : k + 1] - top)
        total = part if total is None else total + part
    return as_rows(top + jnp.log(jnp.sum(total, axis=1, keepdims=True)))[:1]


def rows_kernel(log_cols, got_ref, block_ref, out_ref):
    local = local_rows(block_ref, -(log_cols + joined(got_ref[...])))
    for k in range(out_ref.shape[1]):
        out_ref[:, k, :] = jnp.broadcast_to(local[:, lanes(k)], (out_ref.shape[0], LANES))


def half_rows(got, block, members, log_cols):
    out = shape((members, block.shape[0] // LANES, LANES))
    return call(functools.partial(rows_kernel, log_cols), "half_rows", out, [VMEM, VMEM], VMEM, got, block)


def column_pot(got_ref, chunks, log_rows):
    pot = -(log_rows + joined(got_ref[:, :chunks, :]))
    return jnp.concatenate([as_column(pot[k : k + 1]) for k in range(chunks)], axis=0)


def send_cols(block_ref, pot, out_ref, places):
    for k in places:
        scores = block_ref[:, lanes(k)] + pot
        top = jnp.max(scores, axis=0, keepdims=True)
        local = top + jnp.log(jnp.sum(jnp.exp(scores - top), axis=0, keepdims=True))
        out_ref[:, k, :] = jnp.broadcast_to(local, (out_ref.shape[0], LANES))


def cols_kernel(log_rows, got_ref, block_ref, out_ref):
    pot = column_pot(got_ref, block_ref.shape[0] // LANES, log_rows)
    send_cols(block_ref, pot, out_ref, range(out_ref.shape[1]))


def half_cols(got, block, members, log_rows):
    out = shape((members, block.shape[1] // LANES, LANES))
    return call(functools.partial(cols_kernel, log_rows), "half_cols", out, [VMEM, VMEM], VMEM, got, block)


def first_wide_kernel(log_rows, got_ref, block_ref, out_ref, held_ref, sems):
    parts, rows, width = block_ref.shape
    places = width // LANES
    copies = [
        pltpu.make_async_copy(block_ref.at[k], held_ref.at[:, k * width : (k + 1) * width], sems.at[k])
        for k in range(parts)
    ]
    for copy in copies:
        copy.start()
    pot = column_pot(got_ref, rows // LANES, log_rows)
    for k in range(parts):
        copies[k].wait()
        send_cols(held_ref, pot, out_ref, range(k * places, (k + 1) * places))


def first_wide(got, blocks, members, log_rows):
    parts, rows, width = blocks.shape
    return call(
        functools.partial(first_wide_kernel, log_rows),
        "first_wide",
        (shape((members, parts * width // LANES, LANES)), shape((rows, parts * width))),
        [VMEM, HBM],
        (VMEM, VMEM),
        got,
        blocks,
        scratch_shapes=[pltpu.SemaphoreType.DMA((parts,))],
        vmem=51,
    )


def rounded(values):
    return values.astype(BF16).astype(F32)


def final_kernel(log_cols, got_ref, wide_ref, data_ref, out_ref, pot_ref, weights, held, terms, sems):
    nrow, ny, nx, share, _ = data_ref.shape
    cols = nrow * share
    rows = wide_ref.shape[0]
    copies = [pltpu.make_async_copy(data_ref.at[:, y], held.at[y], sems.at[y]) for y in range(ny)]
    for copy in copies:
        copy.start()
    pot = -(log_cols + joined(got_ref[...]))
    pot_ref[...] = pot
    top = row_top(wide_ref, pot)
    total = None
    for k in range(pot.shape[0]):
        part = jnp.exp(wide_ref[:, lanes(k)] + pot[k : k + 1] - top)
        weights[:, lanes(k)] = part.astype(BF16)
        total = part if total is None else total + part
    total = jnp.sum(total, axis=1, keepdims=True)
    inverse = 1.0 / total
    local = as_rows(top + jnp.log(total))[:16]
    first = rounded(local)
    second = rounded(local - first)
    third = local - first - second
    place = lax.broadcasted_iota(jnp.int32, local.shape, 0)
    extra = jnp.where(place == 0, first, jnp.where(place == 1, second, third))
    extra = jnp.where(place < 3, extra, 0.0).astype(BF16)
    half = ny // 2
    for copy in copies[:half]:
        copy.wait()
    for x in range(nx):
        right = jnp.concatenate([held[y, r, x] for y in range(half) for r in range(nrow)], axis=0)
        terms[x] = jnp.dot(weights[:, : half * cols], right, preferred_element_type=F32)
    for copy in copies[half:]:
        copy.wait()
    for x in range(nx):
        right = jnp.concatenate([held[y, r, x] for y in range(half, ny) for r in range(nrow)], axis=0)
        term = terms[x] + jnp.dot(weights[:, half * cols :], right, preferred_element_type=F32)
        out_ref[x, :rows, :] = (term * inverse).astype(BF16)
        out_ref[x, rows:, :] = extra


def final_terms(got, wide, data, log_cols):
    nrow, ny, nx, share, width = data.shape
    rows = wide.shape[0]
    return call(
        functools.partial(final_kernel, log_cols),
        "final_terms",
        (shape((nx, rows + 16, width), BF16), shape(got.shape[1:])),
        [VMEM, VMEM, HBM],
        (VMEM, VMEM),
        got,
        wide,
        data,
        scratch_shapes=[
            pltpu.VMEM(wide.shape, BF16),
            pltpu.VMEM((ny, nrow, nx, share, width), BF16),
            pltpu.VMEM((nx, rows, width), F32),
            pltpu.SemaphoreType.DMA((ny,)),
        ],
        vmem=50,
    )


def combine_kernel(log_rows, features, got_ref, began_ref, begin_ref, col_ref, out_ref, pot_ref, col_pot_ref):
    nx, rows = got_ref.shape[0], out_ref.shape[0]
    chunks = rows // LANES
    locals_ = [jnp.sum(got_ref[x, rows:, :].astype(F32), axis=0, keepdims=True) for x in range(nx)]
    top = functools.reduce(jnp.maximum, locals_)
    whole = top + jnp.log(functools.reduce(jnp.add, [jnp.exp(v - top) for v in locals_]))
    parts = col_pot_ref.shape[0]
    mine = lax.axis_index("y")
    own = jnp.zeros(col_pot_ref.shape, F32)
    for y in range(col_ref.shape[0] // parts):
        own = jnp.where(mine == y, col_ref[y * parts : (y + 1) * parts, :], own)
    col_pot_ref[...] = EPSILON * (own - begin_ref[...])
    noise_sq = jnp.sum(began_ref[:, chunks:, :], axis=0)
    for k in range(chunks):
        pot_ref[k : k + 1, :] = noise_sq[k : k + 1] * (1.0 / features) - EPSILON * (log_rows + whole[:, lanes(k)])
    scales = [as_column(jnp.exp(v - whole)) for v in locals_]
    for k in range(out_ref.shape[1] // LANES):
        parts = [scales[x] * got_ref[x, :rows, lanes(k)].astype(F32) for x in range(nx)]
        out_ref[:, lanes(k)] = functools.reduce(jnp.add, parts).astype(BF16)


def shards(noise, data):
    rows, width = noise.shape
    cols, features = data.shape
    nx, ny, nrow, ncol = (lax.axis_size(axes) for axes in ("x", "y", ROW, COL))
    log_rows, log_cols = _log(rows * nrow), _log(cols * ncol)
    chunks = rows // LANES

    low = rows - FIRST_ROWS
    share = cols // nrow
    by_x, by_y, noise_sq = call(
        functools.partial(prepare_kernel, FIRST_ROWS),
        "prepare",
        (
            shape((nx, FIRST_ROWS, width), BF16),
            shape((ny, low + nx * share, width), BF16),
            shape((chunks, LANES)),
        ),
        [VMEM, HBM],
        (VMEM, VMEM, VMEM),
        noise,
        data,
        scratch_shapes=[pltpu.VMEM((share, features), BF16), pltpu.SemaphoreType.DMA],
        vmem=52,
    )
    part = lax.all_to_all(by_x, "x", 0, 0)
    first = lax.all_gather(part, "y")
    part, by_y = lax.optimization_barrier((part, by_y))
    got = lax.all_to_all(by_y, "y", 0, 0)
    second = jnp.broadcast_to(got[None, :, :low], (nx, ny, low, width))
    second = lax.all_to_all(second, "x", 0, 0)

    held, col_pot = call(
        functools.partial(load_kernel, -1.0 / (features * EPSILON)),
        "load",
        (shape(data.shape, BF16), shape((cols // LANES, LANES))),
        [HBM, HBM],
        (VMEM, VMEM),
        second,
        data,
        scratch_shapes=[pltpu.SemaphoreType.DMA((cols // LANES,))],
        vmem=46,
    )
    begin_pot = col_pot
    scale = 2.0 / (features * EPSILON)
    scaled, copied, sent, piece = call(
        functools.partial(inner_kernel, scale),
        "inner",
        (
            shape((rows, cols)),
            shape((rows, cols)),
            shape((ncol, 2 * chunks, LANES)),
            shape((ny, nx * share, width), BF16),
        ),
        [VMEM, VMEM, VMEM, VMEM, VMEM, HBM],
        (VMEM, HBM, VMEM, HBM),
        first,
        second,
        held,
        begin_pot,
        noise_sq,
        got,
        scratch_shapes=[pltpu.SemaphoreType.DMA((2,))],
    )
    wide = lax.all_gather(copied, "y")

    began = None
    for step in range(ITERS):
        got = lax.all_to_all(sent, "x" if step > WIDE_FROM else COL, 0, 0)
        if step == 0:
            began, piece = lax.optimization_barrier((got, piece))
            mine = lax.all_gather(piece.reshape(ny, nx, share, width), ROW)
        if step == WIDE_FROM:
            sent, wide = first_wide(got, wide, nrow, log_rows)
        else:
            sent = half_cols(got, wide if step > WIDE_FROM else scaled, nrow, log_rows)
        got = lax.all_to_all(sent, ROW, 0, 0)
        if step < WIDE_FROM:
            sent = half_rows(got, scaled, ncol, log_cols)
        elif step < ITERS - 1:
            sent = half_rows(got, wide, nx, log_cols)
    terms, col_pot = final_terms(got, wide, mine, log_cols)
    got = lax.all_to_all(terms, "x", 0, 0)
    targets, noise_potential, data_potential = call(
        functools.partial(combine_kernel, log_rows, features),
        "combine",
        (shape((rows, width), BF16), shape((chunks, LANES)), shape(begin_pot.shape)),
        [VMEM] * 4,
        (VMEM, VMEM, VMEM),
        got,
        began,
        begin_pot,
        col_pot,
    )
    return (noise_potential.reshape(rows), data_potential.reshape(cols), targets)


def _log(count):
    return float(np.log(np.float32(count)))


def solution(mesh):
    devices = mesh.devices.reshape(8, 2, 4, 8)
    return jax.shard_map(
        shards,
        mesh=Mesh(devices, ("z", "core", "x", "y")),
        in_specs=(P(ROW, COL), P(COL, None)),
        out_specs=(P(ROW), P(COL), P(ROW, COL)),
        check_vma=False,
    )
```

```python
import functools

import jax
import jax.numpy as jnp
import numpy as np
from jax import lax
from jax.experimental import pallas as pl
from jax.experimental.pallas import tpu as pltpu
from jax.sharding import Mesh, PartitionSpec as P

ITERS = 4
EPSILON = 0.01
ROW = ("z", "core")
COL = ("x", "y")
LANES = 128
FIRST_ROWS = 176
WIDE_FROM = 1
VMEM = pl.BlockSpec(memory_space=pltpu.VMEM)
HBM = pl.BlockSpec(memory_space=pltpu.HBM)
MIB = 2**20
F32, BF16 = jnp.float32, jnp.bfloat16


def call(kernel, name, out_shape, in_specs, out_specs, *args, scratch_shapes=(), vmem=40):
    return pl.pallas_call(
        kernel,
        out_shape=out_shape,
        in_specs=in_specs,
        out_specs=out_specs,
        scratch_shapes=scratch_shapes,
        compiler_params=pltpu.CompilerParams(vmem_limit_bytes=vmem * MIB),
        name=name,
    )(*args)


def shape(dims, dtype=F32):
    return jax.ShapeDtypeStruct(dims, dtype)


def lanes(k):
    return slice(k * LANES, (k + 1) * LANES)


def as_column(values):
    return jnp.broadcast_to(values, (LANES, values.shape[1])).T


def as_rows(column):
    return jnp.broadcast_to(column, (column.shape[0], LANES)).T


def joined(got):
    top = jnp.max(got, axis=0)
    return top + jnp.log(jnp.sum(jnp.exp(got - top[None]), axis=0))


def prepare_kernel(high, noise_ref, data_ref, by_x_ref, by_y_ref, sq_ref, held, sem):
    nx = by_x_ref.shape[0]
    ny, sent, width = by_y_ref.shape
    rows = noise_ref.shape[0]
    low = rows - high
    share = (sent - low) // nx
    at = (lax.axis_index(ROW[0]) * lax.axis_size(ROW[1]) + lax.axis_index(ROW[1])) * share
    copy = pltpu.make_async_copy(data_ref.at[pl.ds(pl.multiple_of(at, share), share), :], held, sem)
    copy.start()
    for x in range(nx):
        by_x_ref[x] = noise_ref[:high]
    for y in range(ny):
        by_y_ref[y, :low] = noise_ref[high:]
    squares = jnp.square(noise_ref[...].astype(F32))
    squares = as_rows(jnp.sum(squares, axis=1, keepdims=True))[:1]
    for k in range(rows // LANES):
        sq_ref[k : k + 1, :] = squares[:, lanes(k)]
    copy.wait()
    for y in range(ny):
        for x in range(nx):
            block = held[:, (x * ny + y) * width : (x * ny + y + 1) * width]
            by_y_ref[y, low + x * share : low + (x + 1) * share] = block


def load_kernel(scale, after_ref, data_ref, upper_ref, lower_ref, pot_ref, sems):
    parts = pot_ref.shape[0]
    outs = (upper_ref, lower_ref)
    copies = [pltpu.make_async_copy(data_ref.at[lanes(k)], outs[k], sems.at[k]) for k in range(parts)]
    for copy in copies:
        copy.start()
    for k in range(parts):
        copies[k].wait()
        total = None
        for f in range(upper_ref.shape[1] // LANES):
            block = outs[k][:, lanes(f)].astype(F32)
            total = block * block if total is None else total + block * block
        pot_ref[k : k + 1, :] = as_rows(jnp.sum(total, axis=1, keepdims=True))[:1] * scale


def inner_kernel(
    scale,
    first_ref,
    second_ref,
    upper_ref,
    lower_ref,
    pot_ref,
    sq_ref,
    got_ref,
    out_ref,
    copy_ref,
    send_ref,
    piece_ref,
    sems,
):
    ny, nx, _, width = first_ref.shape
    apart = pltpu.make_async_copy(got_ref.at[:, second_ref.shape[2] :], piece_ref, sems.at[0])
    apart.start()
    wide = ny * width
    total = None
    for x in range(nx):
        for y in range(ny):
            left = jnp.concatenate([first_ref[y, x], second_ref[x, y]], axis=0)
            at = x * wide + y * width
            one = lax.dot_general(
                left, jnp.concatenate([upper_ref[:, at : at + width], lower_ref[:, at : at + width]], axis=0), (((1,), (1,)), ((), ())), preferred_element_type=F32
            )
            total = one if total is None else total + one
    out_ref[...] = total * scale
    out = pltpu.make_async_copy(out_ref, copy_ref, sems.at[1])
    out.start()
    local = local_rows(out_ref, pot_ref[...])
    chunks = local.shape[1] // LANES
    members = send_ref.shape[0]
    for k in range(chunks):
        send_ref[:, k, :] = jnp.broadcast_to(local[:, lanes(k)], (members, LANES))
        send_ref[:, chunks + k, :] = jnp.broadcast_to(sq_ref[k : k + 1], (members, LANES))
    out.wait()
    apart.wait()


def row_top(block_ref, pot):
    top = None
    for k in range(pot.shape[0]):
        scores = block_ref[:, lanes(k)] + pot[k : k + 1]
        top = scores if top is None else jnp.maximum(top, scores)
    return jnp.max(top, axis=1, keepdims=True)


def local_rows(block_ref, pot):
    top = row_top(block_ref, pot)
    total = None
    for k in range(pot.shape[0]):
        part = jnp.exp(block_ref[:, lanes(k)] + pot[k : k + 1] - top)
        total = part if total is None else total + part
    return as_rows(top + jnp.log(jnp.sum(total, axis=1, keepdims=True)))[:1]


def rows_kernel(log_cols, got_ref, block_ref, out_ref):
    local = local_rows(block_ref, -(log_cols + joined(got_ref[...])))
    for k in range(out_ref.shape[1]):
        out_ref[:, k, :] = jnp.broadcast_to(local[:, lanes(k)], (out_ref.shape[0], LANES))


def half_rows(got, block, members, log_cols):
    out = shape((members, block.shape[0] // LANES, LANES))
    return call(functools.partial(rows_kernel, log_cols), "half_rows", out, [VMEM, VMEM], VMEM, got, block)


def column_pot(got_ref, chunks, log_rows):
    pot = -(log_rows + joined(got_ref[:, :chunks, :]))
    return jnp.concatenate([as_column(pot[k : k + 1]) for k in range(chunks)], axis=0)


def send_cols(block_ref, pot, out_ref, places):
    for k in places:
        scores = block_ref[:, lanes(k)] + pot
        top = jnp.max(scores, axis=0, keepdims=True)
        local = top + jnp.log(jnp.sum(jnp.exp(scores - top), axis=0, keepdims=True))
        out_ref[:, k, :] = jnp.broadcast_to(local, (out_ref.shape[0], LANES))


def cols_kernel(log_rows, got_ref, block_ref, out_ref):
    pot = column_pot(got_ref, block_ref.shape[0] // LANES, log_rows)
    send_cols(block_ref, pot, out_ref, range(out_ref.shape[1]))


def half_cols(got, block, members, log_rows):
    out = shape((members, block.shape[1] // LANES, LANES))
    return call(functools.partial(cols_kernel, log_rows), "half_cols", out, [VMEM, VMEM], VMEM, got, block)


def first_wide_kernel(log_rows, got_ref, block_ref, out_ref, held_ref, sems):
    parts, rows, width = block_ref.shape
    places = width // LANES
    copies = [
        pltpu.make_async_copy(block_ref.at[k], held_ref.at[:, k * width : (k + 1) * width], sems.at[k])
        for k in range(parts)
    ]
    for copy in copies:
        copy.start()
    pot = column_pot(got_ref, rows // LANES, log_rows)
    for k in range(parts):
        copies[k].wait()
        send_cols(held_ref, pot, out_ref, range(k * places, (k + 1) * places))


def first_wide(got, blocks, members, log_rows):
    parts, rows, width = blocks.shape
    return call(
        functools.partial(first_wide_kernel, log_rows),
        "first_wide",
        (shape((members, parts * width // LANES, LANES)), shape((rows, parts * width))),
        [VMEM, HBM],
        (VMEM, VMEM),
        got,
        blocks,
        scratch_shapes=[pltpu.SemaphoreType.DMA((parts,))],
        vmem=51,
    )


def rounded(values):
    return values.astype(BF16).astype(F32)


def final_kernel(log_cols, got_ref, wide_ref, data_ref, out_ref, pot_ref, weights, held, terms, sems):
    nrow, ny, nx, share, _ = data_ref.shape
    cols = nrow * share
    rows = wide_ref.shape[0]
    copies = [pltpu.make_async_copy(data_ref.at[:, y], held.at[y], sems.at[y]) for y in range(ny)]
    for copy in copies:
        copy.start()
    pot = -(log_cols + joined(got_ref[...]))
    pot_ref[...] = pot
    top = row_top(wide_ref, pot)
    total = None
    for k in range(pot.shape[0]):
        part = jnp.exp(wide_ref[:, lanes(k)] + pot[k : k + 1] - top)
        weights[:, lanes(k)] = part.astype(BF16)
        total = part if total is None else total + part
    total = jnp.sum(total, axis=1, keepdims=True)
    inverse = 1.0 / total
    local = as_rows(top + jnp.log(total))[:16]
    first = rounded(local)
    second = rounded(local - first)
    third = local - first - second
    place = lax.broadcasted_iota(jnp.int32, local.shape, 0)
    extra = jnp.where(place == 0, first, jnp.where(place == 1, second, third))
    extra = jnp.where(place < 3, extra, 0.0).astype(BF16)
    half = ny // 2
    for copy in copies[:half]:
        copy.wait()
    for x in range(nx):
        right = jnp.concatenate([held[y, r, x] for y in range(half) for r in range(nrow)], axis=0)
        terms[x] = jnp.dot(weights[:, : half * cols], right, preferred_element_type=F32)
    for copy in copies[half:]:
        copy.wait()
    for x in range(nx):
        right = jnp.concatenate([held[y, r, x] for y in range(half, ny) for r in range(nrow)], axis=0)
        term = terms[x] + jnp.dot(weights[:, half * cols :], right, preferred_element_type=F32)
        out_ref[x, :rows, :] = (term * inverse).astype(BF16)
        out_ref[x, rows:, :] = extra


def final_terms(got, wide, data, log_cols):
    nrow, ny, nx, share, width = data.shape
    rows = wide.shape[0]
    return call(
        functools.partial(final_kernel, log_cols),
        "final_terms",
        (shape((nx, rows + 16, width), BF16), shape(got.shape[1:])),
        [VMEM, VMEM, HBM],
        (VMEM, VMEM),
        got,
        wide,
        data,
        scratch_shapes=[
            pltpu.VMEM(wide.shape, BF16),
            pltpu.VMEM((ny, nrow, nx, share, width), BF16),
            pltpu.VMEM((nx, rows, width), F32),
            pltpu.SemaphoreType.DMA((ny,)),
        ],
        vmem=50,
    )


def combine_kernel(log_rows, features, got_ref, began_ref, begin_ref, col_ref, out_ref, pot_ref, col_pot_ref):
    nx, rows = got_ref.shape[0], out_ref.shape[0]
    chunks = rows // LANES
    locals_ = [jnp.sum(got_ref[x, rows:, :].astype(F32), axis=0, keepdims=True) for x in range(nx)]
    top = functools.reduce(jnp.maximum, locals_)
    whole = top + jnp.log(functools.reduce(jnp.add, [jnp.exp(v - top) for v in locals_]))
    parts = col_pot_ref.shape[0]
    mine = lax.axis_index("y")
    own = jnp.zeros(col_pot_ref.shape, F32)
    for y in range(col_ref.shape[0] // parts):
        own = jnp.where(mine == y, col_ref[y * parts : (y + 1) * parts, :], own)
    col_pot_ref[...] = EPSILON * (own - begin_ref[...])
    noise_sq = jnp.sum(began_ref[:, chunks:, :], axis=0)
    for k in range(chunks):
        pot_ref[k : k + 1, :] = noise_sq[k : k + 1] * (1.0 / features) - EPSILON * (log_rows + whole[:, lanes(k)])
    scales = [as_column(jnp.exp(v - whole)) for v in locals_]
    for k in range(out_ref.shape[1] // LANES):
        parts = [scales[x] * got_ref[x, :rows, lanes(k)].astype(F32) for x in range(nx)]
        out_ref[:, lanes(k)] = functools.reduce(jnp.add, parts).astype(BF16)


def shards(noise, data):
    rows, width = noise.shape
    cols, features = data.shape
    nx, ny, nrow, ncol = (lax.axis_size(axes) for axes in ("x", "y", ROW, COL))
    log_rows, log_cols = _log(rows * nrow), _log(cols * ncol)
    chunks = rows // LANES

    low = rows - FIRST_ROWS
    share = cols // nrow
    by_x, by_y, noise_sq = call(
        functools.partial(prepare_kernel, FIRST_ROWS),
        "prepare",
        (
            shape((nx, FIRST_ROWS, width), BF16),
            shape((ny, low + nx * share, width), BF16),
            shape((chunks, LANES)),
        ),
        [VMEM, HBM],
        (VMEM, VMEM, VMEM),
        noise,
        data,
        scratch_shapes=[pltpu.VMEM((share, features), BF16), pltpu.SemaphoreType.DMA],
        vmem=52,
    )
    part = lax.all_to_all(by_x, "x", 0, 0)
    first = lax.all_gather(part, "y")
    part, by_y = lax.optimization_barrier((part, by_y))
    got = lax.all_to_all(by_y, "y", 0, 0)
    second = jnp.broadcast_to(got[None, :, :low], (nx, ny, low, width))
    second = lax.all_to_all(second, "x", 0, 0)

    upper, lower, col_pot = call(
        functools.partial(load_kernel, -1.0 / (features * EPSILON)),
        "load",
        (shape((LANES, features), BF16), shape((LANES, features), BF16), shape((cols // LANES, LANES))),
        [HBM, HBM],
        (VMEM, VMEM, VMEM),
        second,
        data,
        scratch_shapes=[pltpu.SemaphoreType.DMA((cols // LANES,))],
        vmem=46,
    )
    begin_pot = col_pot
    scale = 2.0 / (features * EPSILON)
    scaled, copied, sent, piece = call(
        functools.partial(inner_kernel, scale),
        "inner",
        (
            shape((rows, cols)),
            shape((rows, cols)),
            shape((ncol, 2 * chunks, LANES)),
            shape((ny, nx * share, width), BF16),
        ),
        [VMEM, VMEM, VMEM, VMEM, VMEM, VMEM, HBM],
        (VMEM, HBM, VMEM, HBM),
        first,
        second,
        upper,
        lower,
        begin_pot,
        noise_sq,
        got,
        scratch_shapes=[pltpu.SemaphoreType.DMA((2,))],
    )
    wide = lax.all_gather(copied, "y")

    began = None
    for step in range(ITERS):
        got = lax.all_to_all(sent, "x" if step > WIDE_FROM else COL, 0, 0)
        if step == 0:
            began, piece = lax.optimization_barrier((got, piece))
            mine = lax.all_gather(piece.reshape(ny, nx, share, width), ROW)
        if step == WIDE_FROM:
            sent, wide = first_wide(got, wide, nrow, log_rows)
        else:
            sent = half_cols(got, wide if step > WIDE_FROM else scaled, nrow, log_rows)
        got = lax.all_to_all(sent, ROW, 0, 0)
        if step < WIDE_FROM:
            sent = half_rows(got, scaled, ncol, log_cols)
        elif step < ITERS - 1:
            sent = half_rows(got, wide, nx, log_cols)
    terms, col_pot = final_terms(got, wide, mine, log_cols)
    got = lax.all_to_all(terms, "x", 0, 0)
    targets, noise_potential, data_potential = call(
        functools.partial(combine_kernel, log_rows, features),
        "combine",
        (shape((rows, width), BF16), shape((chunks, LANES)), shape(begin_pot.shape)),
        [VMEM] * 4,
        (VMEM, VMEM, VMEM),
        got,
        began,
        begin_pot,
        col_pot,
    )
    return (noise_potential.reshape(rows), data_potential.reshape(cols), targets)


def _log(count):
    return float(np.log(np.float32(count)))


def solution(mesh):
    devices = mesh.devices.reshape(8, 2, 4, 8)
    return jax.shard_map(
        shards,
        mesh=Mesh(devices, ("z", "core", "x", "y")),
        in_specs=(P(ROW, COL), P(COL, None)),
        out_specs=(P(ROW), P(COL), P(ROW, COL)),
        check_vma=False,
    )
```
